128 devices in a mesh: seq: 32 (over x, y, core), head: 4 (over z).
Axes of the slice: x: 4, y: 4, z: 4, core: 2. Of those that a mesh axis runs over, the one named last changes fastest.
Arguments:
- queries: bfloat16 [1024, 8192], P(('seq', 'head')), may hold values from -24 to 24
- keys: bfloat16 [262144, 1024], P('seq', 'head'), may hold values from -6 to 6
- values: bfloat16 [262144, 1024], P('seq', 'head'), may hold values from -9 to 9
- gates: int32 [4, 8, 12], replicated, may hold values from 0 to 63, as said below
Outputs:
- attended: bfloat16 [1024, 8192], P('seq', 'head')
The draws below stay inside these ranges and needn't reach their ends.
Inputs may be any that keep to these rules, and one draw needn't show every extreme that they name: `gates`: each list names 12 different blocks, and block 63 is always one of them.
All inputs are finite; a program needn't handle non-finite values.
Results may differ from the reference program's by a relative error of at most 0.004.
Values may be sent and summed in bfloat16 or wider, within the bound.
No kernel may reach another device: no remote copies, remote signals or barrier semaphores. Data moves between devices by JAX's collectives and lax.ppermute only.
A program may use at most 576 MiB of HBM per device.

```python
import jax
import jax.numpy as jnp
from jax import lax

QUERY_HEADS = 64
KEY_VALUE_HEADS = 8
HEAD_SIZE = 128
BLOCK = 4096
TOPK = 12
QUERY_BLOCK_SIZE = 256
NEW_QUERY_TOKENS = 1024
CONTEXT_BLOCKS = 64
CONTEXT_TOKENS = 262144
QUERY_BLOCK_COUNT = 4


KEY_AMP = 4.0


FAR_QUERY = 17.5


FAR_AMP = 1.5


def sign_table(key):
    random_flip_bits = jax.random.randint(jax.random.fold_in(key, 99), (NEW_QUERY_TOKENS, KEY_VALUE_HEADS * HEAD_SIZE), 0, 2)
    return (2 * random_flip_bits - 1).astype(jnp.float32)


def target_of(row_ids):
    levels = jnp.array([130.0, 230.0, 300.0], jnp.float32)
    return levels[row_ids // 64 % 3]


def spread_signs(sign_entries):
    query_group_width = QUERY_HEADS // KEY_VALUE_HEADS
    return jnp.repeat(sign_entries.reshape(NEW_QUERY_TOKENS, KEY_VALUE_HEADS, 1, HEAD_SIZE), query_group_width, axis=2).reshape(NEW_QUERY_TOKENS, QUERY_HEADS * HEAD_SIZE)


def plant_queries(background_level, sign_entries):
    row_ids = jnp.arange(NEW_QUERY_TOKENS)
    spread = spread_signs(sign_entries)
    aligned_rows = spread * (target_of(row_ids) / (KEY_AMP * HEAD_SIZE ** 0.5))[:, None]
    planted = jnp.where((row_ids % 64 == 5)[:, None], aligned_rows, background_level)
    return jnp.where((row_ids % 64 == 21)[:, None], spread * FAR_QUERY, planted)


def plant_far_keys(background_level, sign_entries):
    row_ids = jnp.arange(NEW_QUERY_TOKENS)
    row_width = KEY_VALUE_HEADS * HEAD_SIZE
    blocks = background_level.reshape(CONTEXT_BLOCKS, BLOCK, row_width)
    leading = blocks[:, :NEW_QUERY_TOKENS]
    far_mask = (row_ids % 64 == 21)[None, :, None] & (jnp.arange(CONTEXT_BLOCKS) < CONTEXT_BLOCKS - 1)[:, None, None]
    leading = jnp.where(far_mask, (sign_entries * FAR_AMP)[None], leading)
    return jnp.concatenate([leading, blocks[:, NEW_QUERY_TOKENS:]], axis=1).reshape(CONTEXT_TOKENS, row_width)


def plant_keys(background_level, sign_entries):
    background_level = plant_far_keys(background_level, sign_entries)
    row_ids = jnp.arange(NEW_QUERY_TOKENS)
    target = target_of(row_ids)
    next_signs = jnp.roll(sign_entries, -1, axis=0)
    near_copy = next_signs * (KEY_AMP * (1.0 - 2.0 / target))[:, None]
    tail_rows = background_level[CONTEXT_TOKENS - NEW_QUERY_TOKENS:]
    tail_rows = jnp.where((row_ids % 64 == 4)[:, None], near_copy, tail_rows)
    tail_rows = jnp.where((row_ids % 64 == 5)[:, None], sign_entries * KEY_AMP, tail_rows)
    return jnp.concatenate([background_level[:CONTEXT_TOKENS - NEW_QUERY_TOKENS], tail_rows], axis=0)


def draw_queries(key, part):
    sign_entries = sign_table(key)
    key = jax.random.fold_in(key, 1)
    background_level = jnp.clip(jax.random.normal(key, (NEW_QUERY_TOKENS, QUERY_HEADS * HEAD_SIZE), jnp.float32) * 1.5, -9.0, 9.0)
    return plant_queries(background_level, sign_entries).astype(jnp.bfloat16)


def draw_keys(key, part):
    sign_entries = sign_table(key)
    key = jax.random.fold_in(key, 2)
    background_level = jnp.clip(jax.random.normal(key, (CONTEXT_TOKENS, KEY_VALUE_HEADS * HEAD_SIZE), jnp.float32), -6.0, 6.0)
    return plant_keys(background_level, sign_entries).astype(jnp.bfloat16)


def draw_values(key, part):
    key = jax.random.fold_in(key, 3)
    bias_random_key = jax.random.fold_in(key, 7)
    block_bias_table = jnp.clip(jax.random.normal(bias_random_key, (CONTEXT_BLOCKS, KEY_VALUE_HEADS * HEAD_SIZE), jnp.float32), -4.0, 4.0)
    noise_component = jnp.clip(jax.random.normal(key, (CONTEXT_TOKENS, KEY_VALUE_HEADS * HEAD_SIZE), jnp.float32), -5.0, 5.0)
    return (noise_component + jnp.repeat(block_bias_table, BLOCK, axis=0)).astype(jnp.bfloat16)


def draw_gates(key, part):
    key = jax.random.fold_in(key, 4)
    score_random_key = jax.random.fold_in(key, 11)
    hot_key = jax.random.fold_in(key, 12)
    unscaled_scores = jax.random.randint(score_random_key, (QUERY_BLOCK_COUNT, KEY_VALUE_HEADS, CONTEXT_BLOCKS - 1), 0, 65536)
    hot_flags = (jax.random.randint(hot_key, (CONTEXT_BLOCKS - 1,), 0, 4) == 0).astype(jnp.int32)
    preference = (unscaled_scores + hot_flags[None, None, :] * 65536) * CONTEXT_BLOCKS + jnp.arange(CONTEXT_BLOCKS - 1, dtype=jnp.int32)[None, None, :]
    _, block_ids = jax.lax.top_k(preference, TOPK - 1)
    current_value = jnp.full((QUERY_BLOCK_COUNT, KEY_VALUE_HEADS, 1), CONTEXT_BLOCKS - 1, jnp.int32)
    return jnp.concatenate([block_ids.astype(jnp.int32), current_value], axis=2)


def setup_inputs(seed: int = 0) -> dict:
    arg_keys = jax.random.split(jax.random.key(seed), 5)
    return {
        "queries": draw_queries(jax.random.fold_in(arg_keys[4], 71), 0),
        "keys": draw_keys(jax.random.fold_in(arg_keys[4], 71), 0),
        "values": draw_values(jax.random.fold_in(arg_keys[4], 71), 0),
        "gates": draw_gates(jax.random.fold_in(arg_keys[4], 71), 0),
    }


NEG = -1.0e30


def attend_block(state, query_tile, key_tile, value_tile, query_pos, key_start, score_scale, sub_width):
    sub_steps = key_tile.shape[0] // sub_width

    def sub_step(sub_index, carried):
        run_max, run_sum, run_out = carried
        key_part = lax.dynamic_slice_in_dim(key_tile, sub_index * sub_width, sub_width, 0)
        value_part = lax.dynamic_slice_in_dim(value_tile, sub_index * sub_width, sub_width, 0)
        scores = lax.dot_general(query_tile, key_part, (((1,), (1,)), ((), ())), preferred_element_type=jnp.float32) * score_scale
        key_pos = key_start + sub_index * sub_width + jnp.arange(sub_width, dtype=jnp.int32)
        allowed = key_pos[None, :] <= query_pos[:, None]
        row_max = jnp.max(jnp.where(allowed, scores, NEG), axis=1)
        new_max = jnp.maximum(run_max, row_max)
        weights = jnp.where(allowed, jnp.exp(scores - new_max[:, None]), 0.0)
        correction = jnp.exp(run_max - new_max)
        run_sum = run_sum * correction + jnp.sum(weights, axis=1)
        run_out = run_out * correction[:, None] + jnp.dot(weights.astype(jnp.bfloat16), value_part, preferred_element_type=jnp.float32)
        return new_max, run_sum, run_out

    return lax.fori_loop(0, sub_steps, sub_step, state)


def reference(queries, keys, values, gates):
    query_group_width = QUERY_HEADS // KEY_VALUE_HEADS
    tile_rows = QUERY_BLOCK_SIZE * query_group_width
    score_scale = HEAD_SIZE ** -0.5
    sub_width = min(BLOCK, 1024)

    def pairing_tile(pairing_index):
        query_block_index = (pairing_index // KEY_VALUE_HEADS).astype(jnp.int32)
        key_value_head = (pairing_index % KEY_VALUE_HEADS).astype(jnp.int32)
        query_tile = lax.dynamic_slice(queries, (query_block_index * QUERY_BLOCK_SIZE, key_value_head * (query_group_width * HEAD_SIZE)), (QUERY_BLOCK_SIZE, query_group_width * HEAD_SIZE)).reshape(tile_rows, HEAD_SIZE)
        query_pos = (CONTEXT_TOKENS - NEW_QUERY_TOKENS + query_block_index * QUERY_BLOCK_SIZE + jnp.arange(tile_rows, dtype=jnp.int32) // query_group_width).astype(jnp.int32)
        chosen = gates[query_block_index, key_value_head]

        def visit_block(state, block_id):
            start = (block_id * BLOCK).astype(jnp.int32)
            key_tile = lax.dynamic_slice(keys, (start, key_value_head * HEAD_SIZE), (BLOCK, HEAD_SIZE))
            value_tile = lax.dynamic_slice(values, (start, key_value_head * HEAD_SIZE), (BLOCK, HEAD_SIZE))
            return attend_block(state, query_tile, key_tile, value_tile, query_pos, start, score_scale, sub_width), None

        initial = (jnp.full((tile_rows,), NEG, jnp.float32), jnp.zeros((tile_rows,), jnp.float32), jnp.zeros((tile_rows, HEAD_SIZE), jnp.float32))
        (run_max, run_sum, run_out), _ = lax.scan(visit_block, initial, chosen)
        return (run_out / run_sum[:, None]).astype(jnp.bfloat16).reshape(QUERY_BLOCK_SIZE, query_group_width * HEAD_SIZE)

    tile_list = lax.map(pairing_tile, jnp.arange(QUERY_BLOCK_COUNT * KEY_VALUE_HEADS, dtype=jnp.int32))
    return tile_list.reshape(QUERY_BLOCK_COUNT, KEY_VALUE_HEADS, QUERY_BLOCK_SIZE, query_group_width * HEAD_SIZE).transpose(0, 2, 1, 3).reshape(NEW_QUERY_TOKENS, QUERY_HEADS * HEAD_SIZE)
```

```python
import functools

import jax
import jax.numpy as jnp
from jax import lax
from jax.experimental import pallas as pl
from jax.experimental.pallas import tpu as pltpu
from jax.sharding import PartitionSpec as P

HEAD = 128
BLOCK = 4096
GROUP = 8
WIDE = GROUP * HEAD
PACK = WIDE + 128
CHUNK = 32
ROWS = 4 * CHUNK
SCALE = 128**-0.5 * 1.4426950408889634
NEG = -1e30
NT = (((1,), (1,)), ((), ()))
VMEM = 60 * 2**20


def device_id(x, y, core):
    return ((x % 4) * 4 + y % 4) * 2 + core


def shift(array, dx, dy):
    pairs = [
        (device_id(x + dx, y + dy, core), device_id(x, y, core))
        for x in range(4)
        for y in range(4)
        for core in range(2)
    ]
    return lax.ppermute(array, "seq", pairs)


def other_core(array):
    pairs = [(s, s ^ 1) for s in range(32)]
    return lax.ppermute(array, "seq", pairs)


def attention_kernel(
    need, last, place, queries, *refs, items, prior
):
    sources = refs[: items // 2]
    refs = refs[items // 2 :]
    if prior:
        before, refs = refs[0], refs[1:]
    out, stacked, peak, total, key_buffer, value_buffer, units, starts, sems = refs
    task = pl.program_id(0)
    tasks = 8

    def copies(unit, slot):
        item = units[unit]
        result = []
        for index in range(0, len(sources), 2):
            keys, values = sources[index], sources[index + 1]
            first = 2 * index
            local = item - first
            rows = pl.ds(pl.multiple_of((local // 2) * BLOCK, BLOCK), BLOCK)
            cols = pl.ds(pl.multiple_of((local % 2) * HEAD, HEAD), HEAD)
            inside = jnp.logical_and(item >= first, item < first + 4)
            result.append(
                (
                    inside,
                    pltpu.make_async_copy(keys.at[rows, cols], key_buffer.at[slot], sems.at[0, slot]),
                    pltpu.make_async_copy(
                        values.at[rows, cols], value_buffer.at[slot], sems.at[1, slot]
                    ),
                )
            )
        return result

    def start(unit, slot):
        for inside, key_copy, value_copy in copies(unit, slot):

            @pl.when(inside)
            def _():
                key_copy.start()
                value_copy.start()

    def wait(unit, slot):
        for inside, key_copy, value_copy in copies(unit, slot):

            @pl.when(inside)
            def _():
                key_copy.wait()
                value_copy.wait()

    @pl.when(task == 0)
    def _():
        def one_task(t, count):
            starts[t] = count

            def one_item(i, count):
                wanted = need[t * items + i]

                @pl.when(wanted != 0)
                def _():
                    units[count] = i

                return count + wanted

            return lax.fori_loop(0, items, one_item, count)

        starts[tasks] = lax.fori_loop(0, tasks, one_task, 0)

        @pl.when(starts[tasks] > 0)
        def _():
            start(0, 0)

    for head in range(GROUP):
        stacked[head * ROWS : (head + 1) * ROWS, :] = queries[0, :, head * HEAD : (head + 1) * HEAD]
    if prior:
        for head in range(GROUP):
            rows = slice(head * ROWS, (head + 1) * ROWS)
            stats = before[0, :, WIDE + 4 * head : WIDE + 4 * head + 4].astype(jnp.float32)
            level = stats[:, 0:1] + stats[:, 1:2] + stats[:, 2:3]
            peak[rows, :] = jnp.broadcast_to(level, (ROWS, HEAD))
            total[rows, :HEAD] = before[0, :, head * HEAD : (head + 1) * HEAD].astype(jnp.float32)
            total[rows, HEAD:] = jnp.broadcast_to(
                jnp.where(level > 0.5 * NEG, 1.0, 0.0), (ROWS, HEAD)
            )
    else:
        peak[...] = jnp.full(peak.shape, NEG, jnp.float32)
        total[...] = jnp.zeros(total.shape, jnp.float32)

    tile = 2 * ROWS

    def attend(slot, masked):
        keys = key_buffer[slot]
        values = jnp.concatenate(
            [value_buffer[slot], jnp.ones((BLOCK, HEAD), jnp.bfloat16)], axis=1
        )

        def score(r):
            return lax.dot_general(
                stacked[r : r + tile, :], keys, NT, preferred_element_type=jnp.float32
            )

        s = score(0)
        for r in range(0, GROUP * ROWS, tile):
            after = score(r + tile) if r + tile < GROUP * ROWS else None
            if masked:
                row = lax.broadcasted_iota(jnp.int32, (tile, 1024), 0) % ROWS
                step = row // CHUNK
                token = ((place[0] + task % 4) % 4) * 256
                token = token + ((place[1] + step) % 4) * 64 + place[2] * CHUNK + row % CHUNK
                col = lax.broadcasted_iota(jnp.int32, (tile, 1024), 1)
                s = jnp.concatenate(
                    [s[:, :3072], jnp.where(col <= token, s[:, 3072:], NEG)], axis=1
                )
            rows = slice(r, r + tile)
            old = peak[rows, :]
            new = jnp.maximum(old, jnp.max(s, axis=1, keepdims=True) * SCALE)
            factor = jnp.exp2(old - new)
            weights = jnp.exp2(s * SCALE - new[:, :1]).astype(jnp.bfloat16)
            peak[rows, :] = new
            total[rows, :] = total[rows, :] * jnp.concatenate([factor, factor], axis=1) + jnp.dot(
                weights, values, preferred_element_type=jnp.float32
            )
            s = after

    def visit(unit, carry):
        slot = unit % 2
        wait(unit, slot)

        @pl.when(unit + 1 < starts[tasks])
        def _():
            start(unit + 1, 1 - slot)

        final_block = last[units[unit]]

        @pl.when(final_block != 0)
        def _():
            attend(slot, True)

        @pl.when(final_block == 0)
        def _():
            attend(slot, False)

        return carry

    lax.fori_loop(starts[task], starts[task + 1], visit, 0)

    lane = lax.broadcasted_iota(jnp.int32, (ROWS, 128), 1)
    packed = jnp.full((ROWS, 128), NEG, jnp.float32)
    for head in range(GROUP):
        rows = slice(head * ROWS, (head + 1) * ROWS)
        mass = total[rows, HEAD:]
        filled = mass > 0.0
        safe = jnp.where(filled, mass, 1.0)
        out[0, :, head * HEAD : (head + 1) * HEAD] = (total[rows, :HEAD] / safe).astype(jnp.bfloat16)
        level = jnp.where(filled, peak[rows, :] + jnp.log2(safe), NEG)
        packed = jnp.where(lane // 4 == head, level, packed)
    out[0, :, WIDE:] = pack_stats(packed, lane)


def pack_stats(level, lane):
    high = level.astype(jnp.bfloat16)
    rest = level - high.astype(jnp.float32)
    middle = rest.astype(jnp.bfloat16)
    low = (rest - middle.astype(jnp.float32)).astype(jnp.bfloat16)
    part = lane % 4
    terms = jnp.where(
        part == 0,
        high.astype(jnp.float32),
        jnp.where(part == 1, middle.astype(jnp.float32), low.astype(jnp.float32)),
    )
    return terms.astype(jnp.bfloat16)


def attention(need, last, place, queries, sources, before=None):
    items = 2 * len(sources)
    by_task = pl.BlockSpec((1, ROWS, WIDE), lambda t, *_: (t, 0, 0))
    packed_by_task = pl.BlockSpec((1, ROWS, PACK), lambda t, *_: (t, 0, 0))
    prior = before is not None
    return pl.pallas_call(
        functools.partial(attention_kernel, items=items, prior=prior),
        grid_spec=pltpu.PrefetchScalarGridSpec(
            num_scalar_prefetch=3,
            grid=(8,),
            in_specs=[by_task]
            + [pl.BlockSpec(memory_space=pl.ANY)] * len(sources)
            + [packed_by_task] * prior,
            out_specs=packed_by_task,
            scratch_shapes=[
                pltpu.VMEM((GROUP * ROWS, HEAD), jnp.bfloat16),
                pltpu.VMEM((GROUP * ROWS, HEAD), jnp.float32),
                pltpu.VMEM((GROUP * ROWS, 2 * HEAD), jnp.float32),
                pltpu.VMEM((2, BLOCK, HEAD), jnp.bfloat16),
                pltpu.VMEM((2, BLOCK, HEAD), jnp.bfloat16),
                pltpu.SMEM((8 * items + 1,), jnp.int32),
                pltpu.SMEM((9,), jnp.int32),
                pltpu.SemaphoreType.DMA((2, 2)),
            ],
        ),
        out_shape=jax.ShapeDtypeStruct((8, ROWS, PACK), jnp.bfloat16),
        compiler_params=pltpu.CompilerParams(vmem_limit_bytes=VMEM),
        cost_estimate=pl.CostEstimate(flops=30 * 10**9, bytes_accessed=2**25, transcendentals=0),
        name="attention",
    )(need, last, place, queries, *sources, *([before] if prior else []))


def combine(parts, lane, head):
    levels = []
    for part in parts:
        stats = part[:, WIDE + 4 * head : WIDE + 4 * head + 4].astype(jnp.float32)
        levels.append(stats[:, 0:1] + stats[:, 1:2] + stats[:, 2:3])
    top = functools.reduce(jnp.maximum, levels)
    shares = [jnp.exp2(level - top) for level in levels]
    mass = sum(shares)
    joined = sum(
        share * part[:, head * HEAD : (head + 1) * HEAD].astype(jnp.float32)
        for share, part in zip(shares, parts)
    )
    return joined / mass, top + jnp.log2(mass)


def merge_kernel(*refs):
    parts, out = refs[:4], refs[4]
    lane = lax.broadcasted_iota(jnp.int32, (out.shape[0], 128), 1)
    packed = jnp.full((out.shape[0], 128), NEG, jnp.float32)
    for head in range(GROUP):
        joined, level = combine(parts, lane, head)
        out[:, head * HEAD : (head + 1) * HEAD] = joined.astype(jnp.bfloat16)
        packed = jnp.where(lane // 4 == head, level, packed)
    out[:, WIDE:] = pack_stats(packed, lane)


def merge(parts):
    return pl.pallas_call(
        merge_kernel,
        out_shape=jax.ShapeDtypeStruct((ROWS, PACK), jnp.bfloat16),
        compiler_params=pltpu.CompilerParams(vmem_limit_bytes=VMEM),
        name="merge",
    )(*[part.reshape(ROWS, PACK) for part in parts])


def finish_kernel(*refs):
    out = refs[8]
    lane = lax.broadcasted_iota(jnp.int32, (CHUNK, 128), 1)
    for side in range(2):
        for head in range(GROUP):
            joined, _ = combine(refs[4 * side : 4 * side + 4], lane, head)
            first = side * WIDE + head * HEAD
            out[:, first : first + HEAD] = joined.astype(jnp.bfloat16)


def finish(left, right):
    return pl.pallas_call(
        finish_kernel,
        out_shape=jax.ShapeDtypeStruct((CHUNK, 2 * WIDE), jnp.bfloat16),
        compiler_params=pltpu.CompilerParams(vmem_limit_bytes=VMEM),
        name="finish",
    )(*[part.reshape(CHUNK, PACK) for part in left + right])


def shards(queries, keys, values, gates):
    seq = lax.axis_index("seq")
    zed = lax.axis_index("head")
    x, y, core = seq // 8, (seq // 2) % 4, seq % 2

    near_keys, near_values = other_core(keys), other_core(values)

    mine = lax.all_to_all(queries, "head", split_axis=1, concat_axis=0, tiled=True)
    left, right = mine[:, :WIDE], mine[:, WIDE:]
    left = jnp.concatenate([left] + [shift(left, 0, k) for k in (1, 2, 3)], axis=0)
    right = jnp.stack([right] + [shift(right, j, 0) for j in (1, 2, 3)])
    left = jnp.stack([left] + [shift(left, j, 0) for j in (1, 2, 3)])
    right = jnp.stack([right] + [shift(right, 0, k) for k in (1, 2, 3)], axis=1)
    tasks = jnp.concatenate([left, right.reshape(4, ROWS, WIDE)], axis=0)

    chip = x * 4 + y
    block = chip * 4 + jnp.stack([core * 2, core * 2 + 1, 2 - core * 2, 3 - core * 2])
    local = lax.dynamic_slice_in_dim(gates, zed * 2, 2, 1)
    local = lax.dynamic_slice_in_dim(jnp.concatenate([local, local], axis=0), x, 4, 0)
    wanted = jnp.any(local[:, :, :, None] == block, axis=2).astype(jnp.int32)
    wanted = wanted.transpose(1, 0, 2)
    own_head = jnp.eye(2, dtype=jnp.int32)
    need = (wanted[:, :, :, None] * own_head[:, None, None, :]).reshape(64)
    last = jnp.repeat((block == 63).astype(jnp.int32), 2)
    place = jnp.stack([x, y, core]).astype(jnp.int32)

    partial = attention(need, last, place, tasks, [keys, values, near_keys, near_values])

    left = partial[:4]
    right = partial[4:].reshape(4, 4, CHUNK, PACK)
    left = merge([left[0]] + [shift(left[j], -j, 0) for j in (1, 2, 3)])
    right = merge([right[:, 0]] + [shift(right[:, k], 0, -k) for k in (1, 2, 3)])
    left = left.reshape(4, CHUNK, PACK)
    right = right.reshape(4, CHUNK, PACK)
    left = [left[0]] + [shift(left[k], 0, -k) for k in (1, 2, 3)]
    right = [right[0]] + [shift(right[j], -j, 0) for j in (1, 2, 3)]
    return finish(left, right)


def solution(mesh):
    placed = (P(("seq", "head"), None), P("seq", "head"), P("seq", "head"), P())
    return jax.shard_map(
        shards, mesh=mesh, in_specs=placed, out_specs=P("seq", "head"), check_vma=False
    )
```

```python
import functools

import jax
import jax.numpy as jnp
from jax import lax
from jax.experimental import pallas as pl
from jax.experimental.pallas import tpu as pltpu
from jax.sharding import PartitionSpec as P

HEAD = 128
BLOCK = 4096
GROUP = 8
WIDE = GROUP * HEAD
PACK = WIDE + 128
CHUNK = 32
ROWS = 4 * CHUNK
SCALE = 128**-0.5 * 1.4426950408889634
NEG = -1e30
NT = (((1,), (1,)), ((), ()))
VMEM = 60 * 2**20
HALF = BLOCK // 2
DIRECTIONS = ((1, 0), (-1, 0), (0, 1), (0, -1))


def device_id(x, y, core):
    return ((x % 4) * 4 + y % 4) * 2 + core


def shift(array, dx, dy):
    pairs = [
        (device_id(x + dx, y + dy, core), device_id(x, y, core))
        for x in range(4)
        for y in range(4)
        for core in range(2)
    ]
    return lax.ppermute(array, "seq", pairs)


def other_core(array):
    pairs = [(s, s ^ 1) for s in range(32)]
    return lax.ppermute(array, "seq", pairs)


def plan_kernel(gates, place, table):
    lane = lax.broadcasted_iota(jnp.int32, (8, 128), 1)
    item = lax.broadcasted_iota(jnp.int32, (8, 128), 0)
    chip = lane % 16
    y = chip % 4
    block = chip * 4 + item % 4
    first = place[3] * 2
    kept = []
    for q in range(4):
        hit = jnp.zeros((8, 128), jnp.int32)
        for k in range(12):
            chosen = jnp.where(item < 4, gates[q * 96 + first * 12 + k], gates[q * 96 + first * 12 + 12 + k])
            hit = jnp.where(chosen == block, 1, hit)
        kept.append(hit)

    def ahead(value, d):
        if d == 0:
            return pltpu.roll(value, 124, 1)
        if d == 1:
            return pltpu.roll(value, 4, 1)
        if d == 2:
            return jnp.where(y < 3, pltpu.roll(value, 127, 1), pltpu.roll(value, 3, 1))
        return jnp.where(y > 0, pltpu.roll(value, 1, 1), pltpu.roll(value, 125, 1))

    def over_items(value, how):
        for step in (4, 2, 1):
            value = how(value, pltpu.roll(value, step, 0))
        return value

    load = over_items(kept[0] + kept[1] + kept[2] + kept[3], jnp.add)
    for d in range(4):
        want = jnp.maximum(load - ahead(load, d), 0) >> 1
        left = kept[0] + kept[1] + kept[2] + kept[3]
        moved = jnp.minimum(left, want)
        score = moved * 256 - left * 16 + item
        chosen = jnp.logical_and(score == over_items(score, jnp.maximum), moved > 0)
        moved = jnp.where(chosen, moved, 0)
        entry = jnp.where(chosen, item * 16, 0)
        taken = jnp.zeros((8, 128), jnp.int32)
        for q in range(4):
            goes = jnp.where(taken < moved, kept[q], 0)
            taken = taken + goes
            kept[q] = kept[q] - goes
            entry = entry + goes * (1 << q)
        moved = over_items(moved, jnp.add)
        table[32 + 8 * d : 40 + 8 * d, :] = over_items(entry, jnp.add)
        load = load - moved + ahead(moved, d ^ 1)
    for q in range(4):
        table[8 * q : 8 * q + 8, :] = kept[q]


def plan(gates, place):
    return pl.pallas_call(
        plan_kernel,
        in_specs=[pl.BlockSpec(memory_space=pltpu.SMEM)] * 2,
        out_shape=jax.ShapeDtypeStruct((64, 128), jnp.int32),
        name="plan",
    )(gates.reshape(-1), place)


def ship_kernel(table, place, keys, values, near_keys, near_values, *refs):
    outs, sems = refs[:4], refs[4]
    core = place[2]
    chip = place[0] * 4 + place[1]
    for phase in range(2):
        for d in range(4):
            item = table[32 + 8 * d, chip] // 16
            block = item % 4
            rows = pl.ds(pl.multiple_of((block % 2) * BLOCK + core * HALF, HALF), HALF)
            cols = pl.ds(pl.multiple_of((item // 4) * HEAD, HEAD), HEAD)
            own = block // 2 == core
            for near, pair in ((False, (keys, values)), (True, (near_keys, near_values))):

                @pl.when(own != near)
                def _():
                    for part in range(2):
                        copy = pltpu.make_async_copy(
                            pair[part].at[rows, cols], outs[d].at[part], sems.at[d, part]
                        )
                        if phase == 0:
                            copy.start()
                        else:
                            copy.wait()


def ship(table, place, sources):
    hbm = pl.BlockSpec(memory_space=pl.ANY)
    return pl.pallas_call(
        ship_kernel,
        in_specs=[pl.BlockSpec(memory_space=pltpu.SMEM)] * 2 + [hbm] * 4,
        out_specs=[hbm] * 4,
        out_shape=[jax.ShapeDtypeStruct((2, HALF, HEAD), jnp.bfloat16)] * 4,
        scratch_shapes=[pltpu.SemaphoreType.DMA((4, 2))],
        name="ship",
    )(table, place, *sources)


def attention_kernel(table, place, queries, *refs, head, handed):
    if handed:
        sources, before, refs = refs[:8], refs[8], refs[9:]
    else:
        sources, before, refs = refs[:4], None, refs[4:]
    out, stacked, peak, total, key_buffer, value_buffer, units, starts, sems = refs
    task = pl.program_id(0)
    x, y, core = place[0], place[1], place[2]

    def copies(unit, slot):
        code = units[unit] // 2
        result = []
        if handed:
            for d in range(4):
                group = []
                for part, buffer in ((0, key_buffer), (1, value_buffer)):
                    for place_of, source in ((core, sources[2 * d]), (1 - core, sources[2 * d + 1])):
                        rows = pl.ds(pl.multiple_of(place_of * HALF, HALF), HALF)
                        sem = sems.at[len(group), slot]
                        group.append(pltpu.make_async_copy(source.at[part], buffer.at[slot, rows], sem))
                result.append((code == d, group))
        else:
            rows = pl.ds(pl.multiple_of((code % 2) * BLOCK, BLOCK), BLOCK)
            cols = pl.ds(head * HEAD, HEAD)
            for near in range(2):
                keys, values = sources[2 * near], sources[2 * near + 1]
                group = [
                    pltpu.make_async_copy(keys.at[rows, cols], key_buffer.at[slot], sems.at[0, slot]),
                    pltpu.make_async_copy(values.at[rows, cols], value_buffer.at[slot], sems.at[1, slot]),
                ]
                result.append((code // 2 == near, group))
        return result

    def start(unit, slot):
        for inside, group in copies(unit, slot):

            @pl.when(inside)
            def _():
                for copy in group:
                    copy.start()

    def wait(unit, slot):
        for inside, group in copies(unit, slot):

            @pl.when(inside)
            def _():
                for copy in group:
                    copy.wait()

    def list_units(t, count):
        starts[t] = count
        q = (x + t) % 4
        for code in range(4):
            if handed:
                dx, dy = DIRECTIONS[code]
                giver = ((x - dx + 4) % 4) * 4 + (y - dy + 4) % 4
                entry = table[32 + 8 * code, giver]
                item = entry // 16
                wanted = jnp.where(item // 4 == head, (entry >> q) & 1, 0)
                block = giver * 4 + item % 4
            else:
                own = (core if code < 2 else 1 - core) * 2 + code % 2
                wanted = table[8 * q + 4 * head + own, x * 4 + y]
                block = (x * 4 + y) * 4 + own
            at = count

            @pl.when(wanted != 0)
            def _():
                units[at] = 2 * code + (block == 63).astype(jnp.int32)

            count = count + wanted
        return count

    @pl.when(task == 0)
    def _():
        starts[4] = lax.fori_loop(0, 4, list_units, 0)

        @pl.when(starts[4] > 0)
        def _():
            start(0, 0)

    for h in range(GROUP):
        stacked[h * ROWS : (h + 1) * ROWS, :] = queries[0, :, h * HEAD : (h + 1) * HEAD]
    if handed:
        for h in range(GROUP):
            rows = slice(h * ROWS, (h + 1) * ROWS)
            level = before[0, :, WIDE + 4 * h : WIDE + 4 * h + 1]
            peak[rows, :] = jnp.broadcast_to(level, (ROWS, HEAD))
            total[rows, :HEAD] = before[0, :, h * HEAD : (h + 1) * HEAD]
            total[rows, HEAD:] = jnp.broadcast_to(
                jnp.where(level > 0.5 * NEG, 1.0, 0.0), (ROWS, HEAD)
            )
    else:
        peak[...] = jnp.full(peak.shape, NEG, jnp.float32)
        total[...] = jnp.zeros(total.shape, jnp.float32)

    tile = 2 * ROWS

    def attend(slot, masked):
        keys = key_buffer[slot]
        values = jnp.concatenate(
            [value_buffer[slot], jnp.ones((BLOCK, HEAD), jnp.bfloat16)], axis=1
        )

        def score(r):
            return lax.dot_general(
                stacked[r : r + tile, :], keys, NT, preferred_element_type=jnp.float32
            )

        s = score(0)
        for r in range(0, GROUP * ROWS, tile):
            after = score(r + tile) if r + tile < GROUP * ROWS else None
            if masked:
                row = lax.broadcasted_iota(jnp.int32, (tile, 1024), 0) % ROWS
                token = ((x + task) % 4) * 256 + ((y + row // CHUNK) % 4) * 64
                token = token + core * CHUNK + row % CHUNK
                col = lax.broadcasted_iota(jnp.int32, (tile, 1024), 1)
                s = jnp.concatenate(
                    [s[:, :3072], jnp.where(col <= token, s[:, 3072:], NEG)], axis=1
                )
            rows = slice(r, r + tile)
            old = peak[rows, :]
            new = jnp.maximum(old, jnp.max(s, axis=1, keepdims=True) * SCALE)
            factor = jnp.exp2(old - new)
            weights = jnp.exp2(s * SCALE - new[:, :1]).astype(jnp.bfloat16)
            peak[rows, :] = new
            total[rows, :] = total[rows, :] * jnp.concatenate([factor, factor], axis=1) + jnp.dot(
                weights, values, preferred_element_type=jnp.float32
            )
            s = after

    def visit(unit, carry):
        slot = unit % 2
        wait(unit, slot)

        @pl.when(unit + 1 < starts[4])
        def _():
            start(unit + 1, 1 - slot)

        masked = units[unit] % 2

        @pl.when(masked != 0)
        def _():
            attend(slot, True)

        @pl.when(masked == 0)
        def _():
            attend(slot, False)

        return carry

    lax.fori_loop(starts[task], starts[task + 1], visit, 0)

    lane = lax.broadcasted_iota(jnp.int32, (ROWS, 128), 1)
    packed = jnp.full((ROWS, 128), NEG, jnp.float32)
    for h in range(GROUP):
        rows = slice(h * ROWS, (h + 1) * ROWS)
        mass = total[rows, HEAD:]
        filled = mass > 0.0
        safe = jnp.where(filled, mass, 1.0)
        out[0, :, h * HEAD : (h + 1) * HEAD] = (total[rows, :HEAD] / safe).astype(out.dtype)
        level = jnp.where(filled, peak[rows, :] + jnp.log2(safe), NEG)
        packed = jnp.where(lane // 4 == h, level, packed)
    out[0, :, WIDE:] = pack_stats(packed, lane) if handed else packed


def pack_stats(level, lane):
    high = level.astype(jnp.bfloat16)
    rest = level - high.astype(jnp.float32)
    middle = rest.astype(jnp.bfloat16)
    low = (rest - middle.astype(jnp.float32)).astype(jnp.bfloat16)
    part = lane % 4
    terms = jnp.where(
        part == 0,
        high.astype(jnp.float32),
        jnp.where(part == 1, middle.astype(jnp.float32), low.astype(jnp.float32)),
    )
    return terms.astype(jnp.bfloat16)


def attention(table, place, queries, sources, head, before=None):
    handed = before is not None
    by_task = pl.BlockSpec((1, ROWS, WIDE), lambda t, *_: (t, 0, 0))
    packed_by_task = pl.BlockSpec((1, ROWS, PACK), lambda t, *_: (t, 0, 0))
    return pl.pallas_call(
        functools.partial(attention_kernel, head=head, handed=handed),
        grid_spec=pltpu.PrefetchScalarGridSpec(
            num_scalar_prefetch=2,
            grid=(4,),
            in_specs=[by_task]
            + [pl.BlockSpec(memory_space=pl.ANY)] * len(sources)
            + [packed_by_task] * handed,
            out_specs=packed_by_task,
            scratch_shapes=[
                pltpu.VMEM((GROUP * ROWS, HEAD), jnp.bfloat16),
                pltpu.VMEM((GROUP * ROWS, HEAD), jnp.float32),
                pltpu.VMEM((GROUP * ROWS, 2 * HEAD), jnp.float32),
                pltpu.VMEM((2, BLOCK, HEAD), jnp.bfloat16),
                pltpu.VMEM((2, BLOCK, HEAD), jnp.bfloat16),
                pltpu.SMEM((17,), jnp.int32),
                pltpu.SMEM((5,), jnp.int32),
                pltpu.SemaphoreType.DMA((4, 2)),
            ],
        ),
        out_shape=jax.ShapeDtypeStruct((4, ROWS, PACK), jnp.bfloat16 if handed else jnp.float32),
        compiler_params=pltpu.CompilerParams(vmem_limit_bytes=VMEM),
        cost_estimate=pl.CostEstimate(flops=2 * 10**10, bytes_accessed=2**25, transcendentals=0),
        name="handed" if handed else "own",
    )(table, place, queries, *sources, *([before] if handed else []))


def combine(parts, lane, head):
    levels = []
    for part in parts:
        stats = part[:, WIDE + 4 * head : WIDE + 4 * head + 4].astype(jnp.float32)
        levels.append(stats[:, 0:1] + stats[:, 1:2] + stats[:, 2:3])
    top = functools.reduce(jnp.maximum, levels)
    shares = [jnp.exp2(level - top) for level in levels]
    mass = sum(shares)
    joined = sum(
        share * part[:, head * HEAD : (head + 1) * HEAD].astype(jnp.float32)
        for share, part in zip(shares, parts)
    )
    return joined / mass, top + jnp.log2(mass)


def merge_kernel(*refs):
    parts, out = refs[:4], refs[4]
    lane = lax.broadcasted_iota(jnp.int32, (out.shape[0], 128), 1)
    packed = jnp.full((out.shape[0], 128), NEG, jnp.float32)
    for head in range(GROUP):
        joined, level = combine(parts, lane, head)
        out[:, head * HEAD : (head + 1) * HEAD] = joined.astype(jnp.bfloat16)
        packed = jnp.where(lane // 4 == head, level, packed)
    out[:, WIDE:] = pack_stats(packed, lane)


def merge(parts):
    return pl.pallas_call(
        merge_kernel,
        out_shape=jax.ShapeDtypeStruct((ROWS, PACK), jnp.bfloat16),
        compiler_params=pltpu.CompilerParams(vmem_limit_bytes=VMEM),
        name="merge",
    )(*[part.reshape(ROWS, PACK) for part in parts])


def finish_kernel(*refs):
    out = refs[8]
    lane = lax.broadcasted_iota(jnp.int32, (CHUNK, 128), 1)
    for side in range(2):
        for head in range(GROUP):
            joined, _ = combine(refs[4 * side : 4 * side + 4], lane, head)
            first = side * WIDE + head * HEAD
            out[:, first : first + HEAD] = joined.astype(jnp.bfloat16)


def finish(left, right):
    return pl.pallas_call(
        finish_kernel,
        out_shape=jax.ShapeDtypeStruct((CHUNK, 2 * WIDE), jnp.bfloat16),
        compiler_params=pltpu.CompilerParams(vmem_limit_bytes=VMEM),
        name="finish",
    )(*[part.reshape(CHUNK, PACK) for part in left + right])


def shards(queries, keys, values, gates):
    seq = lax.axis_index("seq")
    zed = lax.axis_index("head")
    x, y, core = seq // 8, (seq // 2) % 4, seq % 2

    place = jnp.stack([x, y, core, zed]).astype(jnp.int32)
    table = plan(gates, place)
    sources = [keys, values, other_core(keys), other_core(values)]

    mine = lax.all_to_all(queries, "head", split_axis=1, concat_axis=0, tiled=True)
    left, right = mine[:, :WIDE], mine[:, WIDE:]
    left = jnp.concatenate([left] + [shift(left, 0, k) for k in (1, 2, 3)], axis=0)
    right = jnp.stack([right] + [shift(right, j, 0) for j in (1, 2, 3)])
    left = jnp.stack([left] + [shift(left, j, 0) for j in (1, 2, 3)])
    right = jnp.stack([right] + [shift(right, 0, k) for k in (1, 2, 3)], axis=1)
    right = right.reshape(4, ROWS, WIDE)

    slots = []
    for half, (dx, dy) in zip(ship(table, place, sources), DIRECTIONS):
        got = shift(half, -dx, -dy)
        slots += [got, other_core(got)]

    left_own = attention(table, place, left, sources, 0)
    right_own = attention(table, place, right, sources, 1)
    left = attention(table, place, left, slots, 0, left_own)
    right = attention(table, place, right, slots, 1, right_own)

    right = right.reshape(4, 4, CHUNK, PACK)
    left = merge([left[0]] + [shift(left[j], -j, 0) for j in (1, 2, 3)])
    right = merge([right[:, 0]] + [shift(right[:, k], 0, -k) for k in (1, 2, 3)])
    left = left.reshape(4, CHUNK, PACK)
    right = right.reshape(4, CHUNK, PACK)
    left = [left[0]] + [shift(left[k], 0, -k) for k in (1, 2, 3)]
    right = [right[0]] + [shift(right[j], -j, 0) for j in (1, 2, 3)]
    return finish(left, right)


def solution(mesh):
    placed = (P(("seq", "head"), None), P("seq", "head"), P("seq", "head"), P())
    return jax.shard_map(
        shards, mesh=mesh, in_specs=placed, out_specs=P("seq", "head"), check_vma=False
    )
```

```python
import functools

import jax
import jax.numpy as jnp
from jax import lax
from jax.experimental import pallas as pl
from jax.experimental.pallas import tpu as pltpu
from jax.sharding import PartitionSpec as P

HEAD = 128
BLOCK = 4096
GROUP = 8
WIDE = GROUP * HEAD
PACK = WIDE + 128
CHUNK = 32
ROWS = 4 * CHUNK
SCALE = 128**-0.5 * 1.4426950408889634
NEG = -1e30
NT = (((1,), (1,)), ((), ()))
VMEM = 60 * 2**20
HALF = BLOCK // 2
DIRECTIONS = ((1, 0), (-1, 0), (0, 1), (0, -1))


def other_core(array):
    return lax.ppermute(array, "core", [(0, 1), (1, 0)])


def hand_on(array, direction):
    dx, dy = DIRECTIONS[direction]
    axis, step = ("x", dx) if dx else ("y", dy)
    return lax.ppermute(array, axis, [(i, (i + step) % 4) for i in range(4)])


def plan_kernel(gates, place, table):
    lane = lax.broadcasted_iota(jnp.int32, (8, 128), 1)
    item = lax.broadcasted_iota(jnp.int32, (8, 128), 0)
    chip = lane % 16
    y = chip % 4
    block = chip * 4 + item % 4
    first = place[3] * 2
    kept = []
    for q in range(4):
        hit = jnp.zeros((8, 128), jnp.int32)
        for k in range(12):
            chosen = jnp.where(item < 4, gates[q * 96 + first * 12 + k], gates[q * 96 + first * 12 + 12 + k])
            hit = jnp.where(chosen == block, 1, hit)
        kept.append(hit)

    def ahead(value, d):
        if d == 0:
            return pltpu.roll(value, 124, 1)
        if d == 1:
            return pltpu.roll(value, 4, 1)
        if d == 2:
            return jnp.where(y < 3, pltpu.roll(value, 127, 1), pltpu.roll(value, 3, 1))
        return jnp.where(y > 0, pltpu.roll(value, 1, 1), pltpu.roll(value, 125, 1))

    def over_items(value, how):
        for step in (4, 2, 1):
            value = how(value, pltpu.roll(value, step, 0))
        return value

    load = over_items(kept[0] + kept[1] + kept[2] + kept[3], jnp.add)
    for d in range(4):
        want = jnp.maximum(load - ahead(load, d), 0) >> 1
        left = kept[0] + kept[1] + kept[2] + kept[3]
        moved = jnp.minimum(left, want)
        score = moved * 256 - left * 16 + item
        chosen = jnp.logical_and(score == over_items(score, jnp.maximum), moved > 0)
        moved = jnp.where(chosen, moved, 0)
        entry = jnp.where(chosen, item * 16, 0)
        taken = jnp.zeros((8, 128), jnp.int32)
        for q in range(4):
            goes = jnp.where(taken < moved, kept[q], 0)
            taken = taken + goes
            kept[q] = kept[q] - goes
            entry = entry + goes * (1 << q)
        moved = over_items(moved, jnp.add)
        table[32 + 8 * d : 40 + 8 * d, :] = over_items(entry, jnp.add)
        load = load - moved + ahead(moved, d ^ 1)
    for q in range(4):
        table[8 * q : 8 * q + 8, :] = kept[q]


def plan(gates, place):
    return pl.pallas_call(
        plan_kernel,
        in_specs=[pl.BlockSpec(memory_space=pltpu.SMEM)] * 2,
        out_shape=jax.ShapeDtypeStruct((64, 128), jnp.int32),
        name="plan",
    )(gates.reshape(-1), place)


def ship_kernel(table, place, keys, values, near_keys, near_values, *refs):
    outs, sems = refs[:4], refs[4]
    core = place[2]
    chip = place[0] * 4 + place[1]
    for phase in range(2):
        for d in range(4):
            item = table[32 + 8 * d, chip] // 16
            block = item % 4
            rows = pl.ds(pl.multiple_of((block % 2) * BLOCK + core * HALF, HALF), HALF)
            cols = pl.ds(pl.multiple_of((item // 4) * HEAD, HEAD), HEAD)
            own = block // 2 == core
            for near, pair in ((False, (keys, values)), (True, (near_keys, near_values))):

                @pl.when(own != near)
                def _():
                    for part in range(2):
                        copy = pltpu.make_async_copy(
                            pair[part].at[rows, cols], outs[d].at[part], sems.at[d, part]
                        )
                        if phase == 0:
                            copy.start()
                        else:
                            copy.wait()


def ship(table, place, sources):
    hbm = pl.BlockSpec(memory_space=pl.ANY)
    return pl.pallas_call(
        ship_kernel,
        in_specs=[pl.BlockSpec(memory_space=pltpu.SMEM)] * 2 + [hbm] * 4,
        out_specs=[pl.BlockSpec(memory_space=pltpu.VMEM)] * 4,
        out_shape=[jax.ShapeDtypeStruct((2, HALF, HEAD), jnp.bfloat16)] * 4,
        scratch_shapes=[pltpu.SemaphoreType.DMA((4, 2))],
        compiler_params=pltpu.CompilerParams(vmem_limit_bytes=VMEM // 2),
        name="ship",
    )(table, place, *sources)


def attention_kernel(table, place, queries, *refs, base, tasks, handed):
    if handed:
        sources, before, refs = refs[:8], refs[8], refs[9:]
    else:
        sources, before, refs = refs[:4], None, refs[4 + base :]
    out, stacked, peak, total, key_buffer, value_buffer, units, starts, sems = refs
    task = pl.program_id(0)
    x, y, core = place[0], place[1], place[2]

    def copies(unit, slot):
        code = (units[unit] // 2) % 4
        head = units[unit] // 8
        result = []
        if handed:
            for d in range(4):
                group = []
                for part, buffer in ((0, key_buffer), (1, value_buffer)):
                    for place_of, source in ((core, sources[2 * d]), (1 - core, sources[2 * d + 1])):
                        rows = pl.ds(pl.multiple_of(place_of * HALF, HALF), HALF)
                        sem = sems.at[len(group), slot]
                        group.append(pltpu.make_async_copy(source.at[part], buffer.at[slot, rows], sem))
                result.append((code == d, group))
        else:
            rows = pl.ds(pl.multiple_of((code % 2) * BLOCK, BLOCK), BLOCK)
            cols = pl.ds(pl.multiple_of(head * HEAD, HEAD), HEAD)
            for near in range(2):
                keys, values = sources[2 * near], sources[2 * near + 1]
                group = [
                    pltpu.make_async_copy(keys.at[rows, cols], key_buffer.at[slot], sems.at[0, slot]),
                    pltpu.make_async_copy(values.at[rows, cols], value_buffer.at[slot], sems.at[1, slot]),
                ]
                result.append((code // 2 == near, group))
        return result

    def start(unit, slot):
        for inside, group in copies(unit, slot):

            @pl.when(inside)
            def _():
                for copy in group:
                    copy.start()

    def wait(unit, slot):
        for inside, group in copies(unit, slot):

            @pl.when(inside)
            def _():
                for copy in group:
                    copy.wait()

    def list_units(t, count):
        starts[t] = count
        head, q = base + t // 4, t % 4
        for code in range(4):
            if handed:
                dx, dy = DIRECTIONS[code]
                giver = ((x - dx + 4) % 4) * 4 + (y - dy + 4) % 4
                entry = table[32 + 8 * code, giver]
                item = entry // 16
                wanted = jnp.where(item // 4 == head, (entry >> q) & 1, 0)
                block = giver * 4 + item % 4
            else:
                own = (core if code < 2 else 1 - core) * 2 + code % 2
                wanted = table[8 * q + 4 * head + own, x * 4 + y]
                block = (x * 4 + y) * 4 + own
            at = count

            @pl.when(wanted != 0)
            def _():
                units[at] = 8 * head + 2 * code + (block == 63).astype(jnp.int32)

            count = count + wanted
        return count

    @pl.when(task == 0)
    def _():
        starts[tasks] = lax.fori_loop(0, tasks, list_units, 0)

        @pl.when(starts[tasks] > 0)
        def _():
            start(0, 0)

    tile = 2 * ROWS

    def attend(slot, masked):
        keys = key_buffer[slot]
        values = jnp.concatenate(
            [value_buffer[slot], jnp.ones((BLOCK, HEAD), jnp.bfloat16)], axis=1
        )

        def score(r):
            return lax.dot_general(
                stacked[r : r + tile, :], keys, NT, preferred_element_type=jnp.float32
            )

        s = score(0)
        for r in range(0, GROUP * ROWS, tile):
            after = score(r + tile) if r + tile < GROUP * ROWS else None
            if masked:
                row = lax.broadcasted_iota(jnp.int32, (tile, 1024), 0) % ROWS
                token = (task % 4) * 256 + (row // CHUNK) * 64 + core * CHUNK + row % CHUNK
                col = lax.broadcasted_iota(jnp.int32, (tile, 1024), 1)
                s = jnp.concatenate(
                    [s[:, :3072], jnp.where(col <= token, s[:, 3072:], NEG)], axis=1
                )
            rows = slice(r, r + tile)
            old = peak[rows, :]
            new = jnp.maximum(old, jnp.max(s, axis=1, keepdims=True) * SCALE)
            factor = jnp.exp2(old - new)
            weights = jnp.exp2(s * SCALE - new[:, :1]).astype(jnp.bfloat16)
            peak[rows, :] = new
            total[rows, :] = total[rows, :] * jnp.concatenate([factor, factor], axis=1) + jnp.dot(
                weights, values, preferred_element_type=jnp.float32
            )
            s = after

    def visit(unit, carry):
        slot = unit % 2
        wait(unit, slot)

        @pl.when(unit + 1 < starts[tasks])
        def _():
            start(unit + 1, 1 - slot)

        masked = units[unit] % 2

        @pl.when(masked != 0)
        def _():
            attend(slot, True)

        @pl.when(masked == 0)
        def _():
            attend(slot, False)

        return carry

    def prepare():
        for h in range(GROUP):
            stacked[h * ROWS : (h + 1) * ROWS, :] = queries[:, h * HEAD : (h + 1) * HEAD]
        if handed:
            for h in range(GROUP):
                rows = slice(h * ROWS, (h + 1) * ROWS)
                level = before[0, :, WIDE + 4 * h : WIDE + 4 * h + 1]
                peak[rows, :] = jnp.broadcast_to(level, (ROWS, HEAD))
                total[rows, :HEAD] = before[0, :, h * HEAD : (h + 1) * HEAD]
                total[rows, HEAD:] = jnp.broadcast_to(
                    jnp.where(level > 0.5 * NEG, 1.0, 0.0), (ROWS, HEAD)
                )
        else:
            peak[...] = jnp.full(peak.shape, NEG, jnp.float32)
            total[...] = jnp.zeros(total.shape, jnp.float32)

    lane = lax.broadcasted_iota(jnp.int32, (ROWS, 128), 1)

    @pl.when(starts[task] < starts[task + 1])
    def _():
        prepare()
        lax.fori_loop(starts[task], starts[task + 1], visit, 0)
        packed = jnp.full((ROWS, 128), NEG, jnp.float32)
        for h in range(GROUP):
            rows = slice(h * ROWS, (h + 1) * ROWS)
            mass = total[rows, HEAD:]
            out[0, :, h * HEAD : (h + 1) * HEAD] = (total[rows, :HEAD] / mass).astype(out.dtype)
            packed = jnp.where(lane // 4 == h, peak[rows, :] + jnp.log2(mass), packed)
        out[0, :, WIDE:] = pack_stats(packed, lane) if handed else packed

    @pl.when(starts[task] == starts[task + 1])
    def _():
        if handed:
            out[0, :, :WIDE] = before[0, :, :WIDE].astype(jnp.bfloat16)
            out[0, :, WIDE:] = pack_stats(before[0, :, WIDE:], lane)
        else:
            out[0, :, :WIDE] = jnp.zeros((ROWS, WIDE), out.dtype)
            out[0, :, WIDE:] = jnp.full((ROWS, 128), NEG, out.dtype)


def pack_stats(level, lane):
    high = level.astype(jnp.bfloat16)
    rest = level - high.astype(jnp.float32)
    middle = rest.astype(jnp.bfloat16)
    low = (rest - middle.astype(jnp.float32)).astype(jnp.bfloat16)
    part = lane % 4
    terms = jnp.where(
        part == 0,
        high.astype(jnp.float32),
        jnp.where(part == 1, middle.astype(jnp.float32), low.astype(jnp.float32)),
    )
    return terms.astype(jnp.bfloat16)


def attention(table, place, queries, sources, base, tasks, before=None):
    handed = tasks == 8
    by_task = pl.BlockSpec((ROWS, WIDE), lambda t, *_: (t % 4, base + t // 4))
    packed_by_task = pl.BlockSpec((1, ROWS, PACK), lambda t, *_: (t % 4, 0, base + t // 4))
    hbm = pl.BlockSpec(memory_space=pl.ANY)
    more = [] if before is None else [before]
    return pl.pallas_call(
        functools.partial(attention_kernel, base=base, tasks=tasks, handed=handed),
        grid_spec=pltpu.PrefetchScalarGridSpec(
            num_scalar_prefetch=2,
            grid=(tasks,),
            in_specs=[by_task]
            + [hbm] * len(sources)
            + [packed_by_task if handed else hbm] * len(more),
            out_specs=packed_by_task,
            scratch_shapes=[
                pltpu.VMEM((GROUP * ROWS, HEAD), jnp.bfloat16),
                pltpu.VMEM((GROUP * ROWS, HEAD), jnp.float32),
                pltpu.VMEM((GROUP * ROWS, 2 * HEAD), jnp.float32),
                pltpu.VMEM((2, BLOCK, HEAD), jnp.bfloat16),
                pltpu.VMEM((2, BLOCK, HEAD), jnp.bfloat16),
                pltpu.SMEM((33,), jnp.int32),
                pltpu.SMEM((9,), jnp.int32),
                pltpu.SemaphoreType.DMA((4, 2)),
            ],
        ),
        out_shape=jax.ShapeDtypeStruct(
            (4, ROWS, 2 * PACK), jnp.bfloat16 if handed else jnp.float32
        ),
        input_output_aliases={7: 0} if more and not handed else {},
        compiler_params=pltpu.CompilerParams(vmem_limit_bytes=VMEM),
        cost_estimate=pl.CostEstimate(flops=2 * 10**10, bytes_accessed=2**25, transcendentals=0),
        name="handed" if handed else "own",
    )(table, place, queries, *sources, *more)


def finish_kernel(parts, out):
    for head in range(2):
        for h in range(GROUP):
            first = head * PACK + WIDE + 4 * h
            stats = parts[:, :, first : first + 4].astype(jnp.float32)
            level = stats[:, :, 0:1] + stats[:, :, 1:2] + stats[:, :, 2:3]
            share = jnp.exp2(level - jnp.max(level, axis=0, keepdims=True))
            first = head * PACK + h * HEAD
            part = parts[:, :, first : first + HEAD].astype(jnp.float32)
            joined = jnp.sum(share * part, axis=0) / jnp.sum(share, axis=0)
            first = head * WIDE + h * HEAD
            out[:, first : first + HEAD] = joined.astype(jnp.bfloat16)


def finish(partial):
    parts = lax.all_to_all(
        partial.reshape(16, CHUNK, 2 * PACK), ("x", "y"), split_axis=0, concat_axis=0, tiled=True
    )
    return pl.pallas_call(
        finish_kernel,
        out_shape=jax.ShapeDtypeStruct((CHUNK, 2 * WIDE), jnp.bfloat16),
        compiler_params=pltpu.CompilerParams(vmem_limit_bytes=VMEM),
        name="finish",
    )(parts)


def gather(queries):
    columns = queries.reshape(8, 4, 2 * WIDE).transpose(1, 0, 2)
    sent = jnp.broadcast_to(columns[None], (16, 4, 8, 2 * WIDE)).reshape(64, 8, 2 * WIDE)
    got = lax.all_to_all(sent, ("x", "y", "head"), split_axis=0, concat_axis=0, tiled=True)
    return got.reshape(4 * ROWS, 2 * WIDE)


def shards(queries, keys, values, gates):
    place = jnp.stack([lax.axis_index(name) for name in ("x", "y", "core", "head")]).astype(jnp.int32)
    gathered = gather(queries)
    table = plan(gates, place)
    sources = [keys, values, other_core(keys), other_core(values)]

    slots = []
    for d, half in enumerate(ship(table, place, sources)):
        got = hand_on(half, d)
        slots += [got, other_core(got)]

    partial = attention(table, place, gathered, sources, 0, 4)
    partial = attention(table, place, gathered, sources, 1, 4, partial)
    return finish(attention(table, place, gathered, slots, 0, 8, partial))


def solution(mesh):
    parts = jax.sharding.Mesh(mesh.devices.reshape(4, 4, 2, 4), ("x", "y", "core", "head"))
    seq = ("x", "y", "core")
    placed = (P((*seq, "head"), None), P(seq, "head"), P(seq, "head"), P())
    return jax.shard_map(
        shards, mesh=parts, in_specs=placed, out_specs=P(seq, "head"), check_vma=False
    )
```

```python
import functools

import jax
import jax.numpy as jnp
from jax import lax
from jax.experimental import pallas as pl
from jax.experimental.pallas import tpu as pltpu
from jax.sharding import PartitionSpec as P

HEAD = 128
BLOCK = 4096
GROUP = 8
WIDE = GROUP * HEAD
PACK = WIDE + 128
CHUNK = 32
ROWS = 4 * CHUNK
SCALE = 128**-0.5 * 1.4426950408889634
NEG = -1e30
NT = (((1,), (1,)), ((), ()))
VMEM = 60 * 2**20
HALF = BLOCK // 2
ARRIVAL = 5
DIRECTIONS = ((1, 0), (-1, 0), (0, 1), (0, -1))


def other_core(array):
    return lax.ppermute(array, "core", [(0, 1), (1, 0)])


def hand_on(array, direction):
    dx, dy = DIRECTIONS[direction]
    axis, step = ("x", dx) if dx else ("y", dy)
    return lax.ppermute(array, axis, [(i, (i + step) % 4) for i in range(4)])


def plan_kernel(gates, place, table):
    lane = lax.broadcasted_iota(jnp.int32, (8, 128), 1)
    item = lax.broadcasted_iota(jnp.int32, (8, 128), 0)
    chip = lane % 16
    y = chip % 4
    block = chip * 4 + item % 4
    first = place[3] * 2
    kept = []
    for q in range(4):
        hit = jnp.zeros((8, 128), jnp.int32)
        for k in range(12):
            chosen = jnp.where(item < 4, gates[q * 96 + first * 12 + k], gates[q * 96 + first * 12 + 12 + k])
            hit = jnp.where(chosen == block, 1, hit)
        kept.append(hit)

    def ahead(value, d):
        if d == 0:
            return pltpu.roll(value, 124, 1)
        if d == 1:
            return pltpu.roll(value, 4, 1)
        if d == 2:
            return jnp.where(y < 3, pltpu.roll(value, 127, 1), pltpu.roll(value, 3, 1))
        return jnp.where(y > 0, pltpu.roll(value, 1, 1), pltpu.roll(value, 125, 1))

    def over_items(value, how):
        for step in (4, 2, 1):
            value = how(value, pltpu.roll(value, step, 0))
        return value

    own = over_items(kept[0] + kept[1] + kept[2] + kept[3], jnp.add)
    handed = jnp.zeros((8, 128), jnp.int32)
    given, got = [], []
    for d in range(4):
        ready = jnp.maximum(own, ARRIVAL) + handed
        done = jnp.where(handed > 0, ready, own)
        want = jnp.maximum(done - ahead(ready, d), 0) >> 1
        left = kept[0] + kept[1] + kept[2] + kept[3]
        moved = jnp.minimum(left, want)
        score = moved * 256 - left * 16 + item
        chosen = jnp.logical_and(score == over_items(score, jnp.maximum), moved > 0)
        moved = jnp.where(chosen, moved, 0)
        entry = jnp.where(chosen, item * 16, 0)
        taken = jnp.zeros((8, 128), jnp.int32)
        for q in range(4):
            goes = jnp.where(taken < moved, kept[q], 0)
            taken = taken + goes
            kept[q] = kept[q] - goes
            entry = entry + goes * (1 << q)
        moved = over_items(moved, jnp.add)
        entry = over_items(entry, jnp.add)
        given.append(entry)
        got.append(ahead(entry, d ^ 1))
        own = own - moved
        handed = handed + ahead(moved, d ^ 1)
    keeps = jnp.zeros((8, 128), jnp.int32)
    for q in range(4):
        keeps = keeps + (kept[q] << (8 * q + item))
    row = jnp.zeros((8, 128), jnp.int32)
    here = place[0] * 4 + place[1]
    for i, value in enumerate([over_items(keeps, jnp.add)] + given + got):
        row = jnp.where(lane == i, pltpu.roll(value, (i + 128 - here) % 128, 1), row)
    table[...] = row


def plan(gates, place):
    return pl.pallas_call(
        plan_kernel,
        in_specs=[pl.BlockSpec(memory_space=pltpu.SMEM)] * 2,
        out_shape=jax.ShapeDtypeStruct((8, 128), jnp.int32),
        name="plan",
    )(gates.reshape(-1), place)


def ship_kernel(table, place, keys, values, near_keys, near_values, *refs):
    outs, sems = refs[:4], refs[4]
    core = place[2]
    for phase in range(2):
        for d in range(4):
            item = table[0, 1 + d] // 16
            block = item % 4
            rows = pl.ds(pl.multiple_of((block % 2) * BLOCK + core * HALF, HALF), HALF)
            cols = pl.ds(pl.multiple_of((item // 4) * HEAD, HEAD), HEAD)
            own = block // 2 == core
            for near, pair in ((False, (keys, values)), (True, (near_keys, near_values))):

                @pl.when(own != near)
                def _():
                    for part in range(2):
                        copy = pltpu.make_async_copy(
                            pair[part].at[rows, cols], outs[d].at[part], sems.at[d, part]
                        )
                        if phase == 0:
                            copy.start()
                        else:
                            copy.wait()


def ship(table, place, sources):
    hbm = pl.BlockSpec(memory_space=pltpu.HBM)
    return pl.pallas_call(
        ship_kernel,
        in_specs=[pl.BlockSpec(memory_space=pltpu.SMEM)] * 2 + [hbm] * 4,
        out_specs=[pl.BlockSpec(memory_space=pltpu.VMEM)] * 4,
        out_shape=[jax.ShapeDtypeStruct((2, HALF, HEAD), jnp.bfloat16)] * 4,
        scratch_shapes=[pltpu.SemaphoreType.DMA((4, 2))],
        cost_estimate=pl.CostEstimate(flops=0, bytes_accessed=2**10, transcendentals=0),
        compiler_params=pltpu.CompilerParams(vmem_limit_bytes=VMEM // 2),
        name="ship",
    )(table, place, *sources)


def attention_kernel(table, place, queries, *refs, base, tasks, handed):
    if handed:
        sources, before, refs = refs[:8], refs[8], refs[9:]
    else:
        sources, before, refs = refs[:4], None, refs[4 + base :]
    out, stacked, peak, total, key_buffer, value_buffer, units, starts, sems = refs
    task = pl.program_id(0)
    x, y, core = place[0], place[1], place[2]

    def copies(unit, slot):
        code = (units[unit] // 2) % 4
        head = units[unit] // 8
        result = []
        if handed:
            for d in range(4):
                group = []
                for part, buffer in ((0, key_buffer), (1, value_buffer)):
                    for place_of, source in ((core, sources[2 * d]), (1 - core, sources[2 * d + 1])):
                        rows = pl.ds(pl.multiple_of(place_of * HALF, HALF), HALF)
                        sem = sems.at[len(group), slot]
                        group.append(pltpu.make_async_copy(source.at[part], buffer.at[slot, rows], sem))
                result.append((code == d, group))
        else:
            rows = pl.ds(pl.multiple_of((code % 2) * BLOCK, BLOCK), BLOCK)
            cols = pl.ds(pl.multiple_of(head * HEAD, HEAD), HEAD)
            for near in range(2):
                keys, values = sources[2 * near], sources[2 * near + 1]
                group = [
                    pltpu.make_async_copy(keys.at[rows, cols], key_buffer.at[slot], sems.at[0, slot]),
                    pltpu.make_async_copy(values.at[rows, cols], value_buffer.at[slot], sems.at[1, slot]),
                ]
                result.append((code // 2 == near, group))
        return result

    def start(unit, slot):
        for inside, group in copies(unit, slot):

            @pl.when(inside)
            def _():
                for copy in group:
                    copy.start()

    def wait(unit, slot):
        for inside, group in copies(unit, slot):

            @pl.when(inside)
            def _():
                for copy in group:
                    copy.wait()

    def list_units(t, count):
        starts[t] = count
        head, q = base + t // 4, t % 4
        for code in range(4):
            if handed:
                dx, dy = DIRECTIONS[code]
                giver = ((x - dx + 4) % 4) * 4 + (y - dy + 4) % 4
                entry = table[0, 5 + code]
                item = entry // 16
                wanted = jnp.where(item // 4 == head, (entry >> q) & 1, 0)
                block = giver * 4 + item % 4
            else:
                own = (core if code < 2 else 1 - core) * 2 + code % 2
                wanted = (table[0, 0] >> (8 * q + 4 * head + own)) & 1
                block = (x * 4 + y) * 4 + own
            at = count

            @pl.when(wanted != 0)
            def _():
                units[at] = 8 * head + 2 * code + (block == 63).astype(jnp.int32)

            count = count + wanted
        return count

    @pl.when(task == 0)
    def _():
        starts[tasks] = lax.fori_loop(0, tasks, list_units, 0)

        @pl.when(starts[tasks] > 0)
        def _():
            start(0, 0)

    tile = 2 * ROWS

    def attend(slot, masked):
        keys = key_buffer[slot]
        values = jnp.concatenate(
            [value_buffer[slot], jnp.ones((BLOCK, HEAD), jnp.bfloat16)], axis=1
        )

        def score(r):
            return lax.dot_general(
                stacked[r : r + tile, :], keys, NT, preferred_element_type=jnp.float32
            )

        s = score(0)
        for r in range(0, GROUP * ROWS, tile):
            after = score(r + tile) if r + tile < GROUP * ROWS else None
            if masked:
                row = lax.broadcasted_iota(jnp.int32, (tile, 1024), 0) % ROWS
                token = (task % 4) * 256 + (row // CHUNK) * 64 + core * CHUNK + row % CHUNK
                col = lax.broadcasted_iota(jnp.int32, (tile, 1024), 1)
                s = jnp.concatenate(
                    [s[:, :3072], jnp.where(col <= token, s[:, 3072:], NEG)], axis=1
                )
            rows = slice(r, r + tile)
            old = peak[rows, :]
            new = jnp.maximum(old, jnp.max(s, axis=1, keepdims=True) * SCALE)
            factor = jnp.exp2(old - new)
            weights = jnp.exp2(s * SCALE - new[:, :1]).astype(jnp.bfloat16)
            peak[rows, :] = new
            total[rows, :] = total[rows, :] * jnp.concatenate([factor, factor], axis=1) + jnp.dot(
                weights, values, preferred_element_type=jnp.float32
            )
            s = after

    def visit(unit, carry):
        slot = unit % 2
        wait(unit, slot)

        @pl.when(unit + 1 < starts[tasks])
        def _():
            start(unit + 1, 1 - slot)

        masked = units[unit] % 2

        @pl.when(masked != 0)
        def _():
            attend(slot, True)

        @pl.when(masked == 0)
        def _():
            attend(slot, False)

        return carry

    def prepare():
        for h in range(GROUP):
            stacked[h * ROWS : (h + 1) * ROWS, :] = queries[:, h * HEAD : (h + 1) * HEAD]
        if handed:
            for h in range(GROUP):
                rows = slice(h * ROWS, (h + 1) * ROWS)
                level = before[0, :, WIDE + 4 * h : WIDE + 4 * h + 1]
                peak[rows, :] = jnp.broadcast_to(level, (ROWS, HEAD))
                total[rows, :HEAD] = before[0, :, h * HEAD : (h + 1) * HEAD]
                total[rows, HEAD:] = jnp.broadcast_to(
                    jnp.where(level > 0.5 * NEG, 1.0, 0.0), (ROWS, HEAD)
                )
        else:
            peak[...] = jnp.full(peak.shape, NEG, jnp.float32)
            total[...] = jnp.zeros(total.shape, jnp.float32)

    lane = lax.broadcasted_iota(jnp.int32, (ROWS, 128), 1)

    @pl.when(starts[task] < starts[task + 1])
    def _():
        prepare()
        lax.fori_loop(starts[task], starts[task + 1], visit, 0)
        packed = jnp.full((ROWS, 128), NEG, jnp.float32)
        for h in range(GROUP):
            rows = slice(h * ROWS, (h + 1) * ROWS)
            mass = total[rows, HEAD:]
            out[0, :, h * HEAD : (h + 1) * HEAD] = (total[rows, :HEAD] / mass).astype(out.dtype)
            packed = jnp.where(lane // 4 == h, peak[rows, :] + jnp.log2(mass), packed)
        out[0, :, WIDE:] = pack_stats(packed, lane) if handed else packed

    @pl.when(starts[task] == starts[task + 1])
    def _():
        if handed:
            out[0, :, :WIDE] = before[0, :, :WIDE].astype(jnp.bfloat16)
            out[0, :, WIDE:] = pack_stats(before[0, :, WIDE:], lane)
        else:
            out[0, :, :WIDE] = jnp.zeros((ROWS, WIDE), out.dtype)
            out[0, :, WIDE:] = jnp.full((ROWS, 128), NEG, out.dtype)


def pack_stats(level, lane):
    high = level.astype(jnp.bfloat16)
    rest = level - high.astype(jnp.float32)
    middle = rest.astype(jnp.bfloat16)
    low = (rest - middle.astype(jnp.float32)).astype(jnp.bfloat16)
    part = lane % 4
    terms = jnp.where(
        part == 0,
        high.astype(jnp.float32),
        jnp.where(part == 1, middle.astype(jnp.float32), low.astype(jnp.float32)),
    )
    return terms.astype(jnp.bfloat16)


def attention(table, place, queries, sources, base, tasks, before=None):
    handed = tasks == 8
    by_task = pl.BlockSpec((ROWS, WIDE), lambda t, *_: (t % 4, base + t // 4))
    packed_by_task = pl.BlockSpec((1, ROWS, PACK), lambda t, *_: (t % 4, 0, base + t // 4))
    hbm = pl.BlockSpec(memory_space=pltpu.HBM)
    more = [] if before is None else [before]
    return pl.pallas_call(
        functools.partial(attention_kernel, base=base, tasks=tasks, handed=handed),
        grid_spec=pltpu.PrefetchScalarGridSpec(
            num_scalar_prefetch=2,
            grid=(tasks,),
            in_specs=[by_task]
            + [hbm] * len(sources)
            + [packed_by_task if handed else hbm] * len(more),
            out_specs=packed_by_task,
            scratch_shapes=[
                pltpu.VMEM((GROUP * ROWS, HEAD), jnp.bfloat16),
                pltpu.VMEM((GROUP * ROWS, HEAD), jnp.float32),
                pltpu.VMEM((GROUP * ROWS, 2 * HEAD), jnp.float32),
                pltpu.VMEM((2, BLOCK, HEAD), jnp.bfloat16),
                pltpu.VMEM((2, BLOCK, HEAD), jnp.bfloat16),
                pltpu.SMEM((33,), jnp.int32),
                pltpu.SMEM((9,), jnp.int32),
                pltpu.SemaphoreType.DMA((4, 2)),
            ],
        ),
        out_shape=jax.ShapeDtypeStruct(
            (4, ROWS, 2 * PACK), jnp.bfloat16 if handed else jnp.float32
        ),
        input_output_aliases={7: 0} if more and not handed else {},
        compiler_params=pltpu.CompilerParams(vmem_limit_bytes=VMEM),
        cost_estimate=pl.CostEstimate(flops=2 * 10**10, bytes_accessed=2**25, transcendentals=0),
        name="handed" if handed else "own",
    )(table, place, queries, *sources, *more)


def finish_kernel(parts, out):
    for head in range(2):
        first = head * PACK + WIDE
        level = parts[:, :, first : first + 128].astype(jnp.float32)
        level = level + pltpu.roll(level, 127, 2) + pltpu.roll(level, 126, 2)
        share = jnp.exp2(level - jnp.max(level, axis=0, keepdims=True))
        share = share / jnp.sum(share, axis=0, keepdims=True)
        for h in range(GROUP):
            first = head * PACK + h * HEAD
            joined = jnp.zeros((CHUNK, HEAD), jnp.float32)
            for i in range(16):
                part = parts[i, :, first : first + HEAD].astype(jnp.float32)
                joined = joined + share[i, :, 4 * h : 4 * h + 1] * part
            first = head * WIDE + h * HEAD
            out[:, first : first + HEAD] = joined.astype(jnp.bfloat16)


def finish(partial):
    parts = lax.all_to_all(
        partial.reshape(16, CHUNK, 2 * PACK), ("x", "y"), split_axis=0, concat_axis=0, tiled=True
    )
    return pl.pallas_call(
        finish_kernel,
        out_shape=jax.ShapeDtypeStruct((CHUNK, 2 * WIDE), jnp.bfloat16),
        compiler_params=pltpu.CompilerParams(vmem_limit_bytes=VMEM),
        name="finish",
    )(parts)


def gather(queries):
    columns = queries.reshape(8, 4, 2 * WIDE).transpose(1, 0, 2)
    sent = jnp.broadcast_to(columns[None], (16, 4, 8, 2 * WIDE)).reshape(64, 8, 2 * WIDE)
    got = lax.all_to_all(sent, ("x", "y", "head"), split_axis=0, concat_axis=0, tiled=True)
    return got.reshape(4 * ROWS, 2 * WIDE)


def shards(queries, keys, values, gates):
    place = jnp.stack([lax.axis_index(name) for name in ("x", "y", "core", "head")]).astype(jnp.int32)
    gathered = gather(queries)
    table = plan(gates, place)
    sources = [keys, values, other_core(keys), other_core(values)]

    slots = []
    for d, half in enumerate(ship(table, place, sources)):
        got = hand_on(half, d)
        slots += [got, other_core(got)]

    partial = attention(table, place, gathered, sources, 0, 4)
    partial = attention(table, place, gathered, sources, 1, 4, partial)
    return finish(attention(table, place, gathered, slots, 0, 8, partial))


def solution(mesh):
    parts = jax.sharding.Mesh(mesh.devices.reshape(4, 4, 2, 4), ("x", "y", "core", "head"))
    seq = ("x", "y", "core")
    placed = (P((*seq, "head"), None), P(seq, "head"), P(seq, "head"), P())
    return jax.shard_map(
        shards, mesh=parts, in_specs=placed, out_specs=P(seq, "head"), check_vma=False
    )
```

```python
import functools

import jax
import jax.numpy as jnp
from jax import lax
from jax.experimental import pallas as pl
from jax.experimental.pallas import tpu as pltpu
from jax.sharding import PartitionSpec as P

HEAD = 128
BLOCK = 4096
GROUP = 8
WIDE = GROUP * HEAD
PACK = WIDE + 128
BOTH = 2 * WIDE + 128
CHUNK = 32
ROWS = 4 * CHUNK
SCALE = 128**-0.5 * 1.4426950408889634
NEG = -1e30
NT = (((1,), (1,)), ((), ()))
VMEM = 36 * 2**20
HALF = BLOCK // 2
ARRIVAL = 5
DIRECTIONS = ((1, 0), (-1, 0), (0, 1), (0, -1))


def other_core(array):
    return lax.ppermute(array, "core", [(0, 1), (1, 0)])


def hand_on(array, direction):
    dx, dy = DIRECTIONS[direction]
    axis, step = ("x", dx) if dx else ("y", dy)
    return lax.ppermute(array, axis, [(i, (i + step) % 4) for i in range(4)])


def plan_kernel(gates, place, table):
    lane = lax.broadcasted_iota(jnp.int32, (8, 128), 1)
    item = lax.broadcasted_iota(jnp.int32, (8, 128), 0)
    chip = lane % 16
    y = chip % 4
    block = chip * 4 + item % 4
    first = place[3] * 2
    kept = []
    for q in range(4):
        hit = jnp.zeros((8, 128), jnp.int32)
        for k in range(12):
            chosen = jnp.where(item < 4, gates[q * 96 + first * 12 + k], gates[q * 96 + first * 12 + 12 + k])
            hit = jnp.where(chosen == block, 1, hit)
        kept.append(hit)

    def ahead(value, d):
        if d == 0:
            return pltpu.roll(value, 124, 1)
        if d == 1:
            return pltpu.roll(value, 4, 1)
        if d == 2:
            return jnp.where(y < 3, pltpu.roll(value, 127, 1), pltpu.roll(value, 3, 1))
        return jnp.where(y > 0, pltpu.roll(value, 1, 1), pltpu.roll(value, 125, 1))

    def over_items(value, how):
        for step in (4, 2, 1):
            value = how(value, pltpu.roll(value, step, 0))
        return value

    own = over_items(kept[0] + kept[1] + kept[2] + kept[3], jnp.add)
    handed = jnp.zeros((8, 128), jnp.int32)
    given, got = [], []
    for d in range(4):
        ready = jnp.maximum(own, ARRIVAL) + handed
        done = jnp.where(handed > 0, ready, own)
        want = jnp.maximum(done - ahead(ready, d), 0) >> 1
        left = kept[0] + kept[1] + kept[2] + kept[3]
        moved = jnp.minimum(left, want)
        score = moved * 256 - left * 16 + item
        chosen = jnp.logical_and(score == over_items(score, jnp.maximum), moved > 0)
        moved = jnp.where(chosen, moved, 0)
        entry = jnp.where(chosen, item * 16, 0)
        taken = jnp.zeros((8, 128), jnp.int32)
        for q in range(4):
            goes = jnp.where(taken < moved, kept[q], 0)
            taken = taken + goes
            kept[q] = kept[q] - goes
            entry = entry + goes * (1 << q)
        moved = over_items(moved, jnp.add)
        entry = over_items(entry, jnp.add)
        given.append(entry)
        got.append(ahead(entry, d ^ 1))
        own = own - moved
        handed = handed + ahead(moved, d ^ 1)
    keeps = jnp.zeros((8, 128), jnp.int32)
    for q in range(4):
        keeps = keeps + (kept[q] << (8 * q + item))
    row = jnp.zeros((8, 128), jnp.int32)
    here = place[0] * 4 + place[1]
    for i, value in enumerate([over_items(keeps, jnp.add)] + given + got):
        row = jnp.where(lane == i, pltpu.roll(value, (i + 128 - here) % 128, 1), row)
    table[...] = row


def plan(gates, place):
    return pl.pallas_call(
        plan_kernel,
        in_specs=[pl.BlockSpec(memory_space=pltpu.SMEM)] * 2,
        out_shape=jax.ShapeDtypeStruct((8, 128), jnp.int32),
        name="plan",
    )(gates.reshape(-1), place)


def ship_kernel(table, place, keys, values, near_keys, near_values, *refs):
    outs, sems = refs[:4], refs[4]
    core = place[2]
    for phase in range(2):
        for d in range(4):
            item = table[0, 1 + d] // 16
            block = item % 4
            rows = pl.ds(pl.multiple_of((block % 2) * BLOCK + core * HALF, HALF), HALF)
            cols = pl.ds(pl.multiple_of((item // 4) * HEAD, HEAD), HEAD)
            own = block // 2 == core
            for near, pair in ((False, (keys, values)), (True, (near_keys, near_values))):

                @pl.when(own != near)
                def _():
                    for part in range(2):
                        copy = pltpu.make_async_copy(
                            pair[part].at[rows, cols], outs[d].at[part], sems.at[d, part]
                        )
                        if phase == 0:
                            copy.start()
                        else:
                            copy.wait()


def ship(table, place, sources):
    hbm = pl.BlockSpec(memory_space=pl.ANY)
    return pl.pallas_call(
        ship_kernel,
        in_specs=[pl.BlockSpec(memory_space=pltpu.SMEM)] * 2 + [hbm] * 4,
        out_specs=[pl.BlockSpec(memory_space=pltpu.VMEM)] * 4,
        out_shape=[jax.ShapeDtypeStruct((2, HALF, HEAD), jnp.bfloat16)] * 4,
        scratch_shapes=[pltpu.SemaphoreType.DMA((4, 2))],
        cost_estimate=pl.CostEstimate(flops=0, bytes_accessed=2**10, transcendentals=0),
        compiler_params=pltpu.CompilerParams(vmem_limit_bytes=VMEM // 2),
        name="ship",
    )(table, place, *sources)


def attention_kernel(table, place, queries, *refs, base, tasks):
    handed = tasks == 8
    if handed:
        sources, before, refs = refs[:8], refs[8:10], refs[10:]
    else:
        sources, refs = refs[:4], refs[4:]
    out, stacked, peak, total, key_buffer, value_buffer, units, starts, sems = refs
    x, y, core = place[0], place[1], place[2]
    lane = lax.broadcasted_iota(jnp.int32, (ROWS, 128), 1)

    def copies(unit, slot):
        code = (units[unit] // 2) % 4
        head = units[unit] // 8
        result = []
        if handed:
            for d in range(4):
                group = []
                for part, buffer in ((0, key_buffer), (1, value_buffer)):
                    for place_of, source in ((core, sources[2 * d]), (1 - core, sources[2 * d + 1])):
                        rows = pl.ds(pl.multiple_of(place_of * HALF, HALF), HALF)
                        sem = sems.at[len(group), slot]
                        group.append(pltpu.make_async_copy(source.at[part], buffer.at[slot, rows], sem))
                result.append((code == d, group))
        else:
            rows = pl.ds(pl.multiple_of((code % 2) * BLOCK, BLOCK), BLOCK)
            cols = pl.ds(pl.multiple_of(head * HEAD, HEAD), HEAD)
            for near in range(2):
                keys, values = sources[2 * near], sources[2 * near + 1]
                group = [
                    pltpu.make_async_copy(keys.at[rows, cols], key_buffer.at[slot], sems.at[0, slot]),
                    pltpu.make_async_copy(values.at[rows, cols], value_buffer.at[slot], sems.at[1, slot]),
                ]
                result.append((code // 2 == near, group))
        return result

    def start(unit, slot):
        for inside, group in copies(unit, slot):

            @pl.when(inside)
            def _():
                for copy in group:
                    copy.start()

    def wait(unit, slot):
        for inside, group in copies(unit, slot):

            @pl.when(inside)
            def _():
                for copy in group:
                    copy.wait()

    def list_units(t, count):
        starts[t] = count
        head, q = base + t // 4, t % 4
        for code in range(4):
            if handed:
                dx, dy = DIRECTIONS[code]
                giver = ((x - dx + 4) % 4) * 4 + (y - dy + 4) % 4
                entry = table[0, 5 + code]
                item = entry // 16
                wanted = jnp.where(item // 4 == head, (entry >> q) & 1, 0)
                block = giver * 4 + item % 4
            else:
                own = (core if code < 2 else 1 - core) * 2 + code % 2
                wanted = (table[0, 0] >> (8 * q + 4 * head + own)) & 1
                block = (x * 4 + y) * 4 + own
            at = count

            @pl.when(wanted != 0)
            def _():
                units[at] = 8 * head + 2 * code + (block == 63).astype(jnp.int32)

            count = count + wanted
        return count

    starts[tasks] = lax.fori_loop(0, tasks, list_units, 0)

    @pl.when(starts[tasks] > 0)
    def _():
        start(0, 0)

    def columns(task, h):
        first = (base + task // 4) * WIDE + h * HEAD
        return pl.ds(pl.multiple_of(first, HEAD), HEAD)

    def for_head(task, action):
        for head in range(2):
            pl.when(task // 4 == head)(functools.partial(action, before[head].at[task % 4]))

    def load(task, earlier=None):
        tokens = pl.ds(pl.multiple_of((task % 4) * ROWS, ROWS), ROWS)
        for h in range(GROUP):
            rows = slice(h * ROWS, (h + 1) * ROWS)
            stacked[rows, :] = queries[tokens, columns(task, h)]
            if earlier is not None:
                level = earlier[:, WIDE + 4 * h : WIDE + 4 * h + 1]
                peak[rows, :] = jnp.broadcast_to(level, (ROWS, HEAD))
                total[rows, :HEAD] = earlier[:, h * HEAD : (h + 1) * HEAD]
                total[rows, HEAD:] = jnp.broadcast_to(
                    jnp.where(level > 0.5 * NEG, 1.0, 0.0), (ROWS, HEAD)
                )
        if earlier is None:
            peak[...] = jnp.full(peak.shape, NEG, jnp.float32)
            total[...] = jnp.zeros(total.shape, jnp.float32)

    tile = 2 * ROWS

    def attend(task, slot, masked):
        keys = key_buffer[slot]
        values = jnp.concatenate(
            [value_buffer[slot], jnp.ones((BLOCK, HEAD), jnp.bfloat16)], axis=1
        )

        def score(r):
            return lax.dot_general(
                stacked[r : r + tile, :], keys, NT, preferred_element_type=jnp.float32
            )

        s = score(0)
        for r in range(0, GROUP * ROWS, tile):
            after = score(r + tile) if r + tile < GROUP * ROWS else None
            if masked:
                row = lax.broadcasted_iota(jnp.int32, (tile, 1024), 0) % ROWS
                token = (task % 4) * 256 + (row // CHUNK) * 64 + core * CHUNK + row % CHUNK
                col = lax.broadcasted_iota(jnp.int32, (tile, 1024), 1)
                s = jnp.concatenate(
                    [s[:, :3072], jnp.where(col <= token, s[:, 3072:], NEG)], axis=1
                )
            rows = slice(r, r + tile)
            old = peak[rows, :]
            new = jnp.maximum(old, jnp.max(s, axis=1, keepdims=True) * SCALE)
            factor = jnp.exp2(old - new)
            weights = jnp.exp2(s * SCALE - new[:, :1]).astype(jnp.bfloat16)
            peak[rows, :] = new
            total[rows, :] = total[rows, :] * jnp.concatenate([factor, factor], axis=1) + jnp.dot(
                weights, values, preferred_element_type=jnp.float32
            )
            s = after

    def visit(unit, task):
        slot = unit % 2
        wait(unit, slot)

        @pl.when(unit + 1 < starts[tasks])
        def _():
            start(unit + 1, 1 - slot)

        masked = units[unit] % 2

        @pl.when(masked != 0)
        def _():
            attend(task, slot, True)

        @pl.when(masked == 0)
        def _():
            attend(task, slot, False)

        return task

    def prepare():
        for h in range(GROUP):
            stacked[h * ROWS : (h + 1) * ROWS, :] = queries[:, h * HEAD : (h + 1) * HEAD]
        if handed:
            for h in range(GROUP):
                rows = slice(h * ROWS, (h + 1) * ROWS)
                level = before[0, :, WIDE + 4 * h : WIDE + 4 * h + 1]
                peak[rows, :] = jnp.broadcast_to(level, (ROWS, HEAD))
                total[rows, :HEAD] = before[0, :, h * HEAD : (h + 1) * HEAD]
                total[rows, HEAD:] = jnp.broadcast_to(
                    jnp.where(level > 0.5 * NEG, 1.0, 0.0), (ROWS, HEAD)
                )
        else:
            peak[...] = jnp.full(peak.shape, NEG, jnp.float32)
            total[...] = jnp.zeros(total.shape, jnp.float32)

    def write(task, h, value):
        if handed:
            out[task % 4, :, columns(task, h)] = value.astype(jnp.bfloat16)
        else:
            out[task % 4, :, h * HEAD : (h + 1) * HEAD] = value

    def write_levels(task, levels):
        q = task % 4
        if not handed:
            out[q, :, WIDE:] = levels
            return
        packed = pack_stats(levels, lane)
        kept = out[q, :, 2 * WIDE :].astype(jnp.float32)
        kept = jnp.where(jnp.logical_and(task >= 4, lane < 32), kept, packed.astype(jnp.float32))
        out[q, :, 2 * WIDE :] = kept.astype(jnp.bfloat16)

    def one_task(task, carry):
        @pl.when(starts[task] < starts[task + 1])
        def _():
            if handed:
                for_head(task, functools.partial(load, task))
            else:
                load(task)
            lax.fori_loop(starts[task], starts[task + 1], visit, task)
            levels = jnp.full((ROWS, 128), NEG, jnp.float32)
            for h in range(GROUP):
                rows = slice(h * ROWS, (h + 1) * ROWS)
                mass = total[rows, HEAD:]
                write(task, h, total[rows, :HEAD] / mass)
                levels = jnp.where((lane % 32) // 4 == h, peak[rows, :] + jnp.log2(mass), levels)
            write_levels(task, levels)

        @pl.when(starts[task] == starts[task + 1])
        def _():
            def same(earlier):
                for h in range(GROUP):
                    write(task, h, earlier[:, h * HEAD : (h + 1) * HEAD])
                write_levels(task, earlier[:, WIDE:])

            if handed:
                for_head(task, same)
            else:
                out[task % 4, :, :WIDE] = jnp.zeros((ROWS, WIDE), jnp.float32)
                write_levels(task, jnp.full((ROWS, 128), NEG, jnp.float32))

        return carry

    lax.fori_loop(0, tasks, one_task, 0)


def pack_stats(level, lane):
    high = level.astype(jnp.bfloat16)
    rest = level - high.astype(jnp.float32)
    middle = rest.astype(jnp.bfloat16)
    low = (rest - middle.astype(jnp.float32)).astype(jnp.bfloat16)
    part = lane % 4
    terms = jnp.where(
        part == 0,
        high.astype(jnp.float32),
        jnp.where(part == 1, middle.astype(jnp.float32), low.astype(jnp.float32)),
    )
    return terms.astype(jnp.bfloat16)


def attention(table, place, queries, sources, base, tasks, before=()):
    smem = pl.BlockSpec(memory_space=pltpu.SMEM)
    vmem = pl.BlockSpec(memory_space=pltpu.VMEM)
    hbm = pl.BlockSpec(memory_space=pl.ANY)
    if tasks == 8:
        shape = jax.ShapeDtypeStruct((4, ROWS, BOTH), jnp.bfloat16)
    else:
        shape = jax.ShapeDtypeStruct((4, ROWS, PACK), jnp.float32)
    return pl.pallas_call(
        functools.partial(attention_kernel, base=base, tasks=tasks),
        in_specs=[smem] * 2 + [vmem] + [hbm] * len(sources) + [vmem] * len(before),
        out_specs=vmem,
        out_shape=shape,
        scratch_shapes=[
            pltpu.VMEM((GROUP * ROWS, HEAD), jnp.bfloat16),
            pltpu.VMEM((GROUP * ROWS, HEAD), jnp.float32),
            pltpu.VMEM((GROUP * ROWS, 2 * HEAD), jnp.float32),
            pltpu.VMEM((2, BLOCK, HEAD), jnp.bfloat16),
            pltpu.VMEM((2, BLOCK, HEAD), jnp.bfloat16),
            pltpu.SMEM((33,), jnp.int32),
            pltpu.SMEM((9,), jnp.int32),
            pltpu.SemaphoreType.DMA((4, 2)),
        ],
        compiler_params=pltpu.CompilerParams(vmem_limit_bytes=VMEM),
        cost_estimate=pl.CostEstimate(flops=2 * 10**10, bytes_accessed=2**25, transcendentals=0),
        name="handed" if tasks == 8 else "own",
    )(table, place, queries, *sources, *before)


def finish_kernel(parts, out):
    level = parts[:, :, 2 * WIDE :].astype(jnp.float32)
    level = level + pltpu.roll(level, 127, 2) + pltpu.roll(level, 126, 2)
    share = jnp.exp2(level - jnp.max(level, axis=0, keepdims=True))
    share = share / jnp.sum(share, axis=0, keepdims=True)
    for h in range(2 * GROUP):
        columns = slice(h * HEAD, (h + 1) * HEAD)
        joined = jnp.zeros((CHUNK, HEAD), jnp.float32)
        for i in range(16):
            part = parts[i, :, columns].astype(jnp.float32)
            joined = joined + share[i, :, 4 * h : 4 * h + 1] * part
        out[:, columns] = joined.astype(jnp.bfloat16)


def finish(partial):
    parts = lax.all_to_all(
        partial.reshape(16, CHUNK, BOTH), ("x", "y"), split_axis=0, concat_axis=0, tiled=True
    )
    return pl.pallas_call(
        finish_kernel,
        out_shape=jax.ShapeDtypeStruct((CHUNK, 2 * WIDE), jnp.bfloat16),
        compiler_params=pltpu.CompilerParams(vmem_limit_bytes=VMEM),
        name="finish",
    )(parts)


def gather(queries):
    columns = queries.reshape(8, 4, 2 * WIDE).transpose(1, 0, 2)
    sent = jnp.broadcast_to(columns[None], (16, 4, 8, 2 * WIDE)).reshape(64, 8, 2 * WIDE)
    got = lax.all_to_all(sent, ("x", "y", "head"), split_axis=0, concat_axis=0, tiled=True)
    return got.reshape(4 * ROWS, 2 * WIDE)


def shards(queries, keys, values, gates):
    place = jnp.stack([lax.axis_index(name) for name in ("x", "y", "core", "head")]).astype(jnp.int32)
    gathered = gather(queries)
    table = plan(gates, place)
    sources = [keys, values, other_core(keys), other_core(values)]

    slots = []
    for d, half in enumerate(ship(table, place, sources)):
        got = hand_on(half, d)
        slots += [got, other_core(got)]

    own = [attention(table, place, gathered, sources, head, 4) for head in range(2)]
    return finish(attention(table, place, gathered, slots, 0, 8, own))


def solution(mesh):
    parts = jax.sharding.Mesh(mesh.devices.reshape(4, 4, 2, 4), ("x", "y", "core", "head"))
    seq = ("x", "y", "core")
    placed = (P((*seq, "head"), None), P(seq, "head"), P(seq, "head"), P())
    return jax.shard_map(
        shards, mesh=parts, in_specs=placed, out_specs=P(seq, "head"), check_vma=False
    )
```

```python
import functools

import jax
import jax.numpy as jnp
from jax import lax
from jax.experimental import pallas as pl
from jax.experimental.pallas import tpu as pltpu
from jax.sharding import PartitionSpec as P

HEAD = 128
BLOCK = 4096
GROUP = 8
WIDE = GROUP * HEAD
PACK = WIDE + 128
BOTH = 2 * WIDE + 128
CHUNK = 32
ROWS = 4 * CHUNK
SCALE = 128**-0.5 * 1.4426950408889634
NEG = -1e30
NT = (((1,), (1,)), ((), ()))
VMEM = 127 * 2**19
HALF = BLOCK // 2
ARRIVAL = 5
DIRECTIONS = ((1, 0), (-1, 0), (0, 1), (0, -1))


def other_core(array):
    return lax.ppermute(array, "core", [(0, 1), (1, 0)])


def hand_on(array, direction):
    dx, dy = DIRECTIONS[direction]
    axis, step = ("x", dx) if dx else ("y", dy)
    return lax.ppermute(array, axis, [(i, (i + step) % 4) for i in range(4)])


def plan_kernel(gates, place, table):
    lane = lax.broadcasted_iota(jnp.int32, (8, 128), 1)
    item = lax.broadcasted_iota(jnp.int32, (8, 128), 0)
    chip = lane % 16
    y = chip % 4
    block = chip * 4 + item % 4
    first = place[3] * 2
    kept = []
    for q in range(4):
        hit = jnp.zeros((8, 128), jnp.int32)
        for k in range(12):
            chosen = jnp.where(item < 4, gates[q * 96 + first * 12 + k], gates[q * 96 + first * 12 + 12 + k])
            hit = jnp.where(chosen == block, 1, hit)
        kept.append(hit)

    def ahead(value, d):
        if d == 0:
            return pltpu.roll(value, 124, 1)
        if d == 1:
            return pltpu.roll(value, 4, 1)
        if d == 2:
            return jnp.where(y < 3, pltpu.roll(value, 127, 1), pltpu.roll(value, 3, 1))
        return jnp.where(y > 0, pltpu.roll(value, 1, 1), pltpu.roll(value, 125, 1))

    def over_items(value, how):
        for step in (4, 2, 1):
            value = how(value, pltpu.roll(value, step, 0))
        return value

    own = over_items(kept[0] + kept[1] + kept[2] + kept[3], jnp.add)
    handed = jnp.zeros((8, 128), jnp.int32)
    given, got = [], []
    for d in range(4):
        ready = jnp.maximum(own, ARRIVAL) + handed
        done = jnp.where(handed > 0, ready, own)
        want = jnp.maximum(done - ahead(ready, d), 0) >> 1
        left = kept[0] + kept[1] + kept[2] + kept[3]
        moved = jnp.minimum(left, want)
        score = moved * 256 - left * 16 + item
        chosen = jnp.logical_and(score == over_items(score, jnp.maximum), moved > 0)
        moved = jnp.where(chosen, moved, 0)
        entry = jnp.where(chosen, item * 16, 0)
        taken = jnp.zeros((8, 128), jnp.int32)
        for q in range(4):
            goes = jnp.where(taken < moved, kept[q], 0)
            taken = taken + goes
            kept[q] = kept[q] - goes
            entry = entry + goes * (1 << q)
        moved = over_items(moved, jnp.add)
        entry = over_items(entry, jnp.add)
        given.append(entry)
        got.append(ahead(entry, d ^ 1))
        own = own - moved
        handed = handed + ahead(moved, d ^ 1)
    keeps = jnp.zeros((8, 128), jnp.int32)
    for q in range(4):
        keeps = keeps + (kept[q] << (8 * q + item))
    row = jnp.zeros((8, 128), jnp.int32)
    here = place[0] * 4 + place[1]
    for i, value in enumerate([over_items(keeps, jnp.add)] + given + got):
        row = jnp.where(lane == i, pltpu.roll(value, (i + 128 - here) % 128, 1), row)
    table[...] = row


def plan(gates, place):
    return pl.pallas_call(
        plan_kernel,
        in_specs=[pl.BlockSpec(memory_space=pltpu.SMEM)] * 2,
        out_shape=jax.ShapeDtypeStruct((8, 128), jnp.int32),
        compiler_params=pltpu.CompilerParams(vmem_limit_bytes=VMEM),
        name="plan",
    )(gates.reshape(-1), place)


def ship_kernel(table, place, keys, values, near_keys, near_values, *refs):
    outs, sems = refs[:4], refs[4]
    core = place[2]
    for phase in range(2):
        for d in range(4):
            item = table[0, 1 + d] // 16
            block = item % 4
            rows = pl.ds(pl.multiple_of((block % 2) * BLOCK + core * HALF, HALF), HALF)
            cols = pl.ds(pl.multiple_of((item // 4) * HEAD, HEAD), HEAD)
            own = block // 2 == core
            for near, pair in ((False, (keys, values)), (True, (near_keys, near_values))):

                @pl.when(own != near)
                def _():
                    for part in range(2):
                        copy = pltpu.make_async_copy(
                            pair[part].at[rows, cols], outs[d].at[part], sems.at[d, part]
                        )
                        if phase == 0:
                            copy.start()
                        else:
                            copy.wait()


def ship(table, place, sources):
    hbm = pl.BlockSpec(memory_space=pl.ANY)
    return pl.pallas_call(
        ship_kernel,
        in_specs=[pl.BlockSpec(memory_space=pltpu.SMEM)] * 2 + [hbm] * 4,
        out_specs=[pl.BlockSpec(memory_space=pltpu.VMEM)] * 4,
        out_shape=[jax.ShapeDtypeStruct((2, HALF, HEAD), jnp.bfloat16)] * 4,
        scratch_shapes=[pltpu.SemaphoreType.DMA((4, 2))],
        cost_estimate=pl.CostEstimate(flops=0, bytes_accessed=2**10, transcendentals=0),
        compiler_params=pltpu.CompilerParams(vmem_limit_bytes=VMEM // 2),
        name="ship",
    )(table, place, *sources)


def attention_kernel(table, place, queries, *refs, base, tasks):
    handed = tasks == 8
    if handed:
        sources, before, refs = refs[:8], refs[8:10], refs[10:]
    else:
        sources, refs = refs[:4], refs[4:]
    out, stacked, peak, total, key_buffer, value_buffer, units, starts, sems = refs
    x, y, core = place[0], place[1], place[2]
    lane = lax.broadcasted_iota(jnp.int32, (ROWS, 128), 1)

    def copies(unit, slot):
        code = (units[unit] // 2) % 4
        head = units[unit] // 8
        result = []
        if handed:
            for d in range(4):
                group = []
                for part, buffer in ((0, key_buffer), (1, value_buffer)):
                    for place_of, source in ((core, sources[2 * d]), (1 - core, sources[2 * d + 1])):
                        rows = pl.ds(pl.multiple_of(place_of * HALF, HALF), HALF)
                        sem = sems.at[len(group), slot]
                        group.append(pltpu.make_async_copy(source.at[part], buffer.at[slot, rows], sem))
                result.append((code == d, group))
        else:
            rows = pl.ds(pl.multiple_of((code % 2) * BLOCK, BLOCK), BLOCK)
            cols = pl.ds(pl.multiple_of(head * HEAD, HEAD), HEAD)
            for near in range(2):
                keys, values = sources[2 * near], sources[2 * near + 1]
                group = [
                    pltpu.make_async_copy(keys.at[rows, cols], key_buffer.at[slot], sems.at[0, slot]),
                    pltpu.make_async_copy(values.at[rows, cols], value_buffer.at[slot], sems.at[1, slot]),
                ]
                result.append((code // 2 == near, group))
        return result

    def start(unit, slot):
        for inside, group in copies(unit, slot):

            @pl.when(inside)
            def _():
                for copy in group:
                    copy.start()

    def wait(unit, slot):
        for inside, group in copies(unit, slot):

            @pl.when(inside)
            def _():
                for copy in group:
                    copy.wait()

    def list_units(t, count):
        starts[t] = count
        head, q = base + t // 4, t % 4
        for code in range(4):
            if handed:
                dx, dy = DIRECTIONS[code]
                giver = ((x - dx + 4) % 4) * 4 + (y - dy + 4) % 4
                entry = table[0, 5 + code]
                item = entry // 16
                wanted = jnp.where(item // 4 == head, (entry >> q) & 1, 0)
                block = giver * 4 + item % 4
            else:
                own = (core if code < 2 else 1 - core) * 2 + code % 2
                wanted = (table[0, 0] >> (8 * q + 4 * head + own)) & 1
                block = (x * 4 + y) * 4 + own
            at = count

            @pl.when(wanted != 0)
            def _():
                units[at] = 8 * head + 2 * code + (block == 63).astype(jnp.int32)

            count = count + wanted
        return count

    starts[tasks] = lax.fori_loop(0, tasks, list_units, 0)

    @pl.when(starts[tasks] > 0)
    def _():
        start(0, 0)

    def columns(task, h):
        first = (base + task // 4) * WIDE + h * HEAD
        return pl.ds(pl.multiple_of(first, HEAD), HEAD)

    def for_head(task, action):
        for head in range(2):
            pl.when(task // 4 == head)(functools.partial(action, before[head].at[task % 4]))

    def load(task, earlier=None):
        tokens = pl.ds(pl.multiple_of((task % 4) * ROWS, ROWS), ROWS)
        for h in range(GROUP):
            rows = slice(h * ROWS, (h + 1) * ROWS)
            stacked[rows, :] = queries[tokens, columns(task, h)]
            if earlier is not None:
                level = earlier[:, WIDE + 4 * h : WIDE + 4 * h + 1]
                peak[rows, :] = jnp.broadcast_to(level, (ROWS, HEAD))
                total[rows, :HEAD] = earlier[:, h * HEAD : (h + 1) * HEAD]
                total[rows, HEAD:] = jnp.broadcast_to(
                    jnp.where(level > 0.5 * NEG, 1.0, 0.0), (ROWS, HEAD)
                )
        if earlier is None:
            peak[...] = jnp.full(peak.shape, NEG, jnp.float32)
            total[...] = jnp.zeros(total.shape, jnp.float32)

    tile = 2 * ROWS

    def attend(task, slot, masked):
        keys = key_buffer[slot]
        values = jnp.concatenate(
            [value_buffer[slot], jnp.ones((BLOCK, HEAD), jnp.bfloat16)], axis=1
        )

        def score(r):
            return lax.dot_general(
                stacked[r : r + tile, :], keys, NT, preferred_element_type=jnp.float32
            )

        s = score(0)
        for r in range(0, GROUP * ROWS, tile):
            after = score(r + tile) if r + tile < GROUP * ROWS else None
            if masked:
                row = lax.broadcasted_iota(jnp.int32, (tile, 1024), 0) % ROWS
                token = (task % 4) * 256 + (row // CHUNK) * 64 + core * CHUNK + row % CHUNK
                col = lax.broadcasted_iota(jnp.int32, (tile, 1024), 1)
                s = jnp.concatenate(
                    [s[:, :3072], jnp.where(col <= token, s[:, 3072:], NEG)], axis=1
                )
            rows = slice(r, r + tile)
            old = peak[rows, :]
            new = jnp.maximum(old, jnp.max(s, axis=1, keepdims=True) * SCALE)
            factor = jnp.exp2(old - new)
            weights = jnp.exp2(s * SCALE - new[:, :1]).astype(jnp.bfloat16)
            peak[rows, :] = new
            total[rows, :] = total[rows, :] * jnp.concatenate([factor, factor], axis=1) + jnp.dot(
                weights, values, preferred_element_type=jnp.float32
            )
            s = after

    def visit(unit, task):
        slot = unit % 2
        wait(unit, slot)

        @pl.when(unit + 1 < starts[tasks])
        def _():
            start(unit + 1, 1 - slot)

        masked = units[unit] % 2

        @pl.when(masked != 0)
        def _():
            attend(task, slot, True)

        @pl.when(masked == 0)
        def _():
            attend(task, slot, False)

        return task

    def prepare():
        for h in range(GROUP):
            stacked[h * ROWS : (h + 1) * ROWS, :] = queries[:, h * HEAD : (h + 1) * HEAD]
        if handed:
            for h in range(GROUP):
                rows = slice(h * ROWS, (h + 1) * ROWS)
                level = before[0, :, WIDE + 4 * h : WIDE + 4 * h + 1]
                peak[rows, :] = jnp.broadcast_to(level, (ROWS, HEAD))
                total[rows, :HEAD] = before[0, :, h * HEAD : (h + 1) * HEAD]
                total[rows, HEAD:] = jnp.broadcast_to(
                    jnp.where(level > 0.5 * NEG, 1.0, 0.0), (ROWS, HEAD)
                )
        else:
            peak[...] = jnp.full(peak.shape, NEG, jnp.float32)
            total[...] = jnp.zeros(total.shape, jnp.float32)

    def write(task, h, value):
        if handed:
            out[task % 4, :, columns(task, h)] = value.astype(jnp.bfloat16)
        else:
            out[task % 4, :, h * HEAD : (h + 1) * HEAD] = value

    def write_levels(task, levels):
        q = task % 4
        if not handed:
            out[q, :, WIDE:] = levels
            return
        packed = pack_stats(levels, lane)
        kept = out[q, :, 2 * WIDE :].astype(jnp.float32)
        kept = jnp.where(jnp.logical_and(task >= 4, lane < 32), kept, packed.astype(jnp.float32))
        out[q, :, 2 * WIDE :] = kept.astype(jnp.bfloat16)

    def one_task(task, carry):
        @pl.when(starts[task] < starts[task + 1])
        def _():
            if handed:
                for_head(task, functools.partial(load, task))
            else:
                load(task)
            lax.fori_loop(starts[task], starts[task + 1], visit, task)
            levels = jnp.full((ROWS, 128), NEG, jnp.float32)
            for h in range(GROUP):
                rows = slice(h * ROWS, (h + 1) * ROWS)
                mass = total[rows, HEAD:]
                write(task, h, total[rows, :HEAD] / mass)
                levels = jnp.where((lane % 32) // 4 == h, peak[rows, :] + jnp.log2(mass), levels)
            write_levels(task, levels)

        @pl.when(starts[task] == starts[task + 1])
        def _():
            def same(earlier):
                for h in range(GROUP):
                    write(task, h, earlier[:, h * HEAD : (h + 1) * HEAD])
                write_levels(task, earlier[:, WIDE:])

            if handed:
                for_head(task, same)
            else:
                out[task % 4, :, :WIDE] = jnp.zeros((ROWS, WIDE), jnp.float32)
                write_levels(task, jnp.full((ROWS, 128), NEG, jnp.float32))

        return carry

    lax.fori_loop(0, tasks, one_task, 0)


def pack_stats(level, lane):
    high = level.astype(jnp.bfloat16)
    rest = level - high.astype(jnp.float32)
    middle = rest.astype(jnp.bfloat16)
    low = (rest - middle.astype(jnp.float32)).astype(jnp.bfloat16)
    part = lane % 4
    terms = jnp.where(
        part == 0,
        high.astype(jnp.float32),
        jnp.where(part == 1, middle.astype(jnp.float32), low.astype(jnp.float32)),
    )
    return terms.astype(jnp.bfloat16)


def attention(table, place, queries, sources, base, tasks, before=()):
    smem = pl.BlockSpec(memory_space=pltpu.SMEM)
    vmem = pl.BlockSpec(memory_space=pltpu.VMEM)
    hbm = pl.BlockSpec(memory_space=pl.ANY)
    if tasks == 8:
        shape = jax.ShapeDtypeStruct((4, ROWS, BOTH), jnp.bfloat16)
    else:
        shape = jax.ShapeDtypeStruct((4, ROWS, PACK), jnp.float32)
    return pl.pallas_call(
        functools.partial(attention_kernel, base=base, tasks=tasks),
        in_specs=[smem] * 2 + [vmem] + [hbm] * len(sources) + [vmem] * len(before),
        out_specs=vmem,
        out_shape=shape,
        scratch_shapes=[
            pltpu.VMEM((GROUP * ROWS, HEAD), jnp.bfloat16),
            pltpu.VMEM((GROUP * ROWS, HEAD), jnp.float32),
            pltpu.VMEM((GROUP * ROWS, 2 * HEAD), jnp.float32),
            pltpu.VMEM((2, BLOCK, HEAD), jnp.bfloat16),
            pltpu.VMEM((2, BLOCK, HEAD), jnp.bfloat16),
            pltpu.SMEM((33,), jnp.int32),
            pltpu.SMEM((9,), jnp.int32),
            pltpu.SemaphoreType.DMA((4, 2)),
        ],
        compiler_params=pltpu.CompilerParams(vmem_limit_bytes=VMEM),
        cost_estimate=pl.CostEstimate(flops=2 * 10**10, bytes_accessed=2**25, transcendentals=0),
        name="handed" if tasks == 8 else "own",
    )(table, place, queries, *sources, *before)


def finish_kernel(parts, out):
    level = parts[:, :, 2 * WIDE :].astype(jnp.float32)
    level = level + pltpu.roll(level, 127, 2) + pltpu.roll(level, 126, 2)
    share = jnp.exp2(level - jnp.max(level, axis=0, keepdims=True))
    share = share / jnp.sum(share, axis=0, keepdims=True)
    for h in range(2 * GROUP):
        columns = slice(h * HEAD, (h + 1) * HEAD)
        joined = jnp.zeros((CHUNK, HEAD), jnp.float32)
        for i in range(16):
            part = parts[i, :, columns].astype(jnp.float32)
            joined = joined + share[i, :, 4 * h : 4 * h + 1] * part
        out[:, columns] = joined.astype(jnp.bfloat16)


def finish(partial):
    parts = lax.all_to_all(
        partial.reshape(16, CHUNK, BOTH), ("x", "y"), split_axis=0, concat_axis=0, tiled=True
    )
    return pl.pallas_call(
        finish_kernel,
        out_shape=jax.ShapeDtypeStruct((CHUNK, 2 * WIDE), jnp.bfloat16),
        compiler_params=pltpu.CompilerParams(vmem_limit_bytes=VMEM),
        name="finish",
    )(parts)


def gather(queries):
    columns = queries.reshape(8, 4, 2 * WIDE).transpose(1, 0, 2)
    sent = jnp.broadcast_to(columns[None], (16, 4, 8, 2 * WIDE)).reshape(64, 8, 2 * WIDE)
    got = lax.all_to_all(sent, ("x", "y", "head"), split_axis=0, concat_axis=0, tiled=True)
    return got.reshape(4 * ROWS, 2 * WIDE)


def shards(queries, keys, values, gates):
    place = jnp.stack([lax.axis_index(name) for name in ("x", "y", "core", "head")]).astype(jnp.int32)
    gathered = gather(queries)
    table = plan(gates, place)
    sources = [keys, values, other_core(keys), other_core(values)]
    sources = [pltpu.with_memory_space_constraint(source, pltpu.HBM) for source in sources]

    slots = []
    for d, half in enumerate(ship(table, place, sources)):
        got = hand_on(half, d)
        slots += [got, other_core(got)]

    own = [attention(table, place, gathered, sources, head, 4) for head in range(2)]
    return finish(attention(table, place, gathered, slots, 0, 8, own))


def solution(mesh):
    parts = jax.sharding.Mesh(mesh.devices.reshape(4, 4, 2, 4), ("x", "y", "core", "head"))
    seq = ("x", "y", "core")
    placed = (P((*seq, "head"), None), P(seq, "head"), P(seq, "head"), P())
    return jax.shard_map(
        shards, mesh=parts, in_specs=placed, out_specs=P(seq, "head"), check_vma=False
    )
```

```python
import functools

import jax
import jax.numpy as jnp
from jax import lax
from jax.experimental import pallas as pl
from jax.experimental.pallas import tpu as pltpu
from jax.sharding import PartitionSpec as P

HEAD = 128
BLOCK = 4096
GROUP = 8
WIDE = GROUP * HEAD
PACK = WIDE + 128
BOTH = 2 * WIDE + 128
CHUNK = 32
ROWS = 4 * CHUNK
SCALE = 128**-0.5 * 1.4426950408889634
NEG = -1e30
NT = (((1,), (1,)), ((), ()))
VMEM = 127 * 2**19
ROOM = 36 * 2**20
EARLY, LATER = 4, 6
HALF = BLOCK // 2
ARRIVAL = 5
DIRECTIONS = ((1, 0), (-1, 0), (0, 1), (0, -1))


def other_core(array):
    return lax.ppermute(array, "core", [(0, 1), (1, 0)])


def in_hbm(array):
    return pltpu.with_memory_space_constraint(array, pltpu.HBM)


def hand_on(array, direction):
    dx, dy = DIRECTIONS[direction]
    axis, step = ("x", dx) if dx else ("y", dy)
    return lax.ppermute(array, axis, [(i, (i + step) % 4) for i in range(4)])


def plan_kernel(gates, place, table):
    lane = lax.broadcasted_iota(jnp.int32, (8, 128), 1)
    item = lax.broadcasted_iota(jnp.int32, (8, 128), 0)
    chip = lane % 16
    y = chip % 4
    block = chip * 4 + item % 4
    first = place[3] * 2
    kept = []
    for q in range(4):
        hit = jnp.zeros((8, 128), jnp.int32)
        for k in range(12):
            chosen = jnp.where(item < 4, gates[q * 96 + first * 12 + k], gates[q * 96 + first * 12 + 12 + k])
            hit = jnp.where(chosen == block, 1, hit)
        kept.append(hit)

    def ahead(value, d):
        if d == 0:
            return pltpu.roll(value, 124, 1)
        if d == 1:
            return pltpu.roll(value, 4, 1)
        if d == 2:
            return jnp.where(y < 3, pltpu.roll(value, 127, 1), pltpu.roll(value, 3, 1))
        return jnp.where(y > 0, pltpu.roll(value, 1, 1), pltpu.roll(value, 125, 1))

    def over_items(value, how):
        for step in (4, 2, 1):
            value = how(value, pltpu.roll(value, step, 0))
        return value

    own = over_items(kept[0] + kept[1] + kept[2] + kept[3], jnp.add)
    handed = jnp.zeros((8, 128), jnp.int32)
    given, got = [], []
    for d in range(4):
        ready = jnp.maximum(own, ARRIVAL) + handed
        done = jnp.where(handed > 0, ready, own)
        want = jnp.maximum(done - ahead(ready, d), 0) >> 1
        left = kept[0] + kept[1] + kept[2] + kept[3]
        moved = jnp.minimum(left, want)
        score = moved * 256 - left * 16 + item
        chosen = jnp.logical_and(score == over_items(score, jnp.maximum), moved > 0)
        moved = jnp.where(chosen, moved, 0)
        entry = jnp.where(chosen, item * 16, 0)
        taken = jnp.zeros((8, 128), jnp.int32)
        for q in range(4):
            goes = jnp.where(taken < moved, kept[q], 0)
            taken = taken + goes
            kept[q] = kept[q] - goes
            entry = entry + goes * (1 << q)
        moved = over_items(moved, jnp.add)
        entry = over_items(entry, jnp.add)
        given.append(entry)
        got.append(ahead(entry, d ^ 1))
        own = own - moved
        handed = handed + ahead(moved, d ^ 1)
    keeps = jnp.zeros((8, 128), jnp.int32)
    for q in range(4):
        keeps = keeps + (kept[q] << (8 * q + item))
    row = jnp.zeros((8, 128), jnp.int32)
    here = place[0] * 4 + place[1]
    for i, value in enumerate([over_items(keeps, jnp.add)] + given + got):
        row = jnp.where(lane == i, pltpu.roll(value, (i + 128 - here) % 128, 1), row)
    table[...] = row


def plan(gates, place):
    return pl.pallas_call(
        plan_kernel,
        in_specs=[pl.BlockSpec(memory_space=pltpu.SMEM)] * 2,
        out_shape=jax.ShapeDtypeStruct((8, 128), jnp.int32),
        compiler_params=pltpu.CompilerParams(vmem_limit_bytes=VMEM),
        name="plan",
    )(gates.reshape(-1), place)


def ship_kernel(table, place, keys, values, near_keys, near_values, *refs):
    outs, sems = refs[:4], refs[4]
    core = place[2]
    for phase in range(2):
        for d in range(4):
            item = table[0, 1 + d] // 16
            block = item % 4
            rows = pl.ds(pl.multiple_of((block % 2) * BLOCK + core * HALF, HALF), HALF)
            cols = pl.ds(pl.multiple_of((item // 4) * HEAD, HEAD), HEAD)
            own = block // 2 == core
            for near, pair in ((False, (keys, values)), (True, (near_keys, near_values))):

                @pl.when(own != near)
                def _():
                    for part in range(2):
                        copy = pltpu.make_async_copy(
                            pair[part].at[rows, cols], outs[d].at[part], sems.at[d, part]
                        )
                        if phase == 0:
                            copy.start()
                        else:
                            copy.wait()


def ship(table, place, sources):
    hbm = pl.BlockSpec(memory_space=pl.ANY)
    return pl.pallas_call(
        ship_kernel,
        in_specs=[pl.BlockSpec(memory_space=pltpu.SMEM)] * 2 + [hbm] * 4,
        out_specs=[pl.BlockSpec(memory_space=pltpu.VMEM)] * 4,
        out_shape=[jax.ShapeDtypeStruct((2, HALF, HEAD), jnp.bfloat16)] * 4,
        scratch_shapes=[pltpu.SemaphoreType.DMA((4, 2))],
        cost_estimate=pl.CostEstimate(flops=0, bytes_accessed=2**10, transcendentals=0),
        compiler_params=pltpu.CompilerParams(vmem_limit_bytes=VMEM // 2),
        name="ship",
    )(table, place, *sources)


def attention_kernel(table, place, queries, *refs, first, limit):
    final = limit is None
    sources, refs = refs[: 12 if final else 4], refs[12 if final else 4 :]
    if first:
        before, refs = refs[0], refs[1:]
    out, stacked, peak, total, key_buffer, value_buffer, units, starts, touched, sems = refs
    x, y, core = place[0], place[1], place[2]
    lane = lax.broadcasted_iota(jnp.int32, (ROWS, 128), 1)

    def copies(unit, slot):
        code = (units[unit] // 2) % 8
        head = units[unit] // 16
        result = []
        rows = pl.ds(pl.multiple_of((code % 2) * BLOCK, BLOCK), BLOCK)
        cols = pl.ds(pl.multiple_of(head * HEAD, HEAD), HEAD)
        for near in range(2):
            keys, values = sources[2 * near], sources[2 * near + 1]
            group = [
                pltpu.make_async_copy(keys.at[rows, cols], key_buffer.at[slot], sems.at[0, slot]),
                pltpu.make_async_copy(values.at[rows, cols], value_buffer.at[slot], sems.at[1, slot]),
            ]
            result.append((code // 2 == near, group))
        for d in range(4 if final else 0):
            group = []
            for part, buffer in ((0, key_buffer), (1, value_buffer)):
                for half, source in ((core, sources[4 + 2 * d]), (1 - core, sources[5 + 2 * d])):
                    rows = pl.ds(pl.multiple_of(half * HALF, HALF), HALF)
                    sem = sems.at[len(group), slot]
                    group.append(pltpu.make_async_copy(source.at[part], buffer.at[slot, rows], sem))
            result.append((code == 4 + d, group))
        return result

    def start(unit, slot):
        for inside, group in copies(unit, slot):

            @pl.when(inside)
            def _():
                for copy in group:
                    copy.start()

    def wait(unit, slot):
        for inside, group in copies(unit, slot):

            @pl.when(inside)
            def _():
                for copy in group:
                    copy.wait()

    def list_units(t, carry):
        count, seen = carry
        starts[t] = count
        head, q = t // 4, t % 4
        seen_before = seen
        for code in range(8 if final else 4):
            if code < 4:
                own = (core if code < 2 else 1 - core) * 2 + code % 2
                wanted = (table[0, 0] >> (8 * q + 4 * head + own)) & 1
                block = (x * 4 + y) * 4 + own
                ours = seen >= first
                if not final:
                    ours = jnp.logical_and(ours, seen < limit)
                seen = seen + wanted
                wanted = jnp.where(ours, wanted, 0)
            else:
                dx, dy = DIRECTIONS[code - 4]
                giver = ((x - dx + 4) % 4) * 4 + (y - dy + 4) % 4
                entry = table[0, 1 + code]
                item = entry // 16
                wanted = jnp.where(item // 4 == head, (entry >> q) & 1, 0)
                block = giver * 4 + item % 4
            at = count

            @pl.when(wanted != 0)
            def _():
                units[at] = 16 * head + 2 * code + (block == 63).astype(jnp.int32)

            count = count + wanted
        touched[t] = (jnp.minimum(seen, first) > seen_before).astype(jnp.int32)
        return count, seen

    starts[8] = lax.fori_loop(0, 8, list_units, (0, 0))[0]

    @pl.when(starts[8] > 0)
    def _():
        start(0, 0)

    def columns(task, h):
        return pl.ds(pl.multiple_of((task // 4) * WIDE + h * HEAD, HEAD), HEAD)

    def load(task):
        tokens = pl.ds(pl.multiple_of((task % 4) * ROWS, ROWS), ROWS)
        for h in range(GROUP):
            stacked[h * ROWS : (h + 1) * ROWS, :] = queries[tokens, columns(task, h)]

        @pl.when(touched[task] == 0)
        def _():
            peak[...] = jnp.full(peak.shape, NEG, jnp.float32)
            total[...] = jnp.zeros(total.shape, jnp.float32)

        if first:

            @pl.when(touched[task] != 0)
            def _():
                total[:, HEAD:] = jnp.ones((GROUP * ROWS, HEAD), jnp.float32)
                for h in range(GROUP):
                    rows = slice(h * ROWS, (h + 1) * ROWS)
                    level = before[task, :, WIDE + 4 * h : WIDE + 4 * h + 1]
                    peak[rows, :] = jnp.broadcast_to(level, (ROWS, HEAD))
                    total[rows, :HEAD] = before[task, :, h * HEAD : (h + 1) * HEAD]

    tile = 2 * ROWS

    def attend(task, slot, masked):
        keys = key_buffer[slot]
        values = jnp.concatenate(
            [value_buffer[slot], jnp.ones((BLOCK, HEAD), jnp.bfloat16)], axis=1
        )

        def score(r):
            return lax.dot_general(
                stacked[r : r + tile, :], keys, NT, preferred_element_type=jnp.float32
            )

        s = score(0)
        for r in range(0, GROUP * ROWS, tile):
            after = score(r + tile) if r + tile < GROUP * ROWS else None
            if masked:
                row = lax.broadcasted_iota(jnp.int32, (tile, 1024), 0) % ROWS
                token = (task % 4) * 256 + (row // CHUNK) * 64 + core * CHUNK + row % CHUNK
                col = lax.broadcasted_iota(jnp.int32, (tile, 1024), 1)
                s = jnp.concatenate(
                    [s[:, :3072], jnp.where(col <= token, s[:, 3072:], NEG)], axis=1
                )
            rows = slice(r, r + tile)
            old = peak[rows, :]
            new = jnp.maximum(old, jnp.max(s, axis=1, keepdims=True) * SCALE)
            factor = jnp.exp2(old - new)
            weights = jnp.exp2(s * SCALE - new[:, :1]).astype(jnp.bfloat16)
            peak[rows, :] = new
            total[rows, :] = total[rows, :] * jnp.concatenate([factor, factor], axis=1) + jnp.dot(
                weights, values, preferred_element_type=jnp.float32
            )
            s = after

    def visit(unit, task):
        slot = unit % 2
        wait(unit, slot)

        @pl.when(unit + 1 < starts[8])
        def _():
            start(unit + 1, 1 - slot)

        masked = units[unit] % 2

        @pl.when(masked != 0)
        def _():
            attend(task, slot, True)

        @pl.when(masked == 0)
        def _():
            attend(task, slot, False)

        return task

    def prepare():
        for h in range(GROUP):
            stacked[h * ROWS : (h + 1) * ROWS, :] = queries[:, h * HEAD : (h + 1) * HEAD]
        if handed:
            for h in range(GROUP):
                rows = slice(h * ROWS, (h + 1) * ROWS)
                level = before[0, :, WIDE + 4 * h : WIDE + 4 * h + 1]
                peak[rows, :] = jnp.broadcast_to(level, (ROWS, HEAD))
                total[rows, :HEAD] = before[0, :, h * HEAD : (h + 1) * HEAD]
                total[rows, HEAD:] = jnp.broadcast_to(
                    jnp.where(level > 0.5 * NEG, 1.0, 0.0), (ROWS, HEAD)
                )
        else:
            peak[...] = jnp.full(peak.shape, NEG, jnp.float32)
            total[...] = jnp.zeros(total.shape, jnp.float32)

    def write(task, h, value):
        if final:
            out[task % 4, :, columns(task, h)] = value.astype(jnp.bfloat16)
        else:
            out[task, :, h * HEAD : (h + 1) * HEAD] = value

    def write_levels(task, levels):
        if not final:
            out[task, :, WIDE:] = levels
            return
        q = task % 4
        packed = pack_stats(levels, lane)
        kept = out[q, :, 2 * WIDE :].astype(jnp.float32)
        kept = jnp.where(jnp.logical_and(task >= 4, lane < 32), kept, packed.astype(jnp.float32))
        out[q, :, 2 * WIDE :] = kept.astype(jnp.bfloat16)

    def one_task(task, carry):
        some = starts[task] < starts[task + 1]

        @pl.when(some)
        def _():
            load(task)
            lax.fori_loop(starts[task], starts[task + 1], visit, task)
            levels = jnp.full((ROWS, 128), NEG, jnp.float32)
            for h in range(GROUP):
                rows = slice(h * ROWS, (h + 1) * ROWS)
                mass = total[rows, HEAD:]
                write(task, h, total[rows, :HEAD] / mass)
                levels = jnp.where((lane % 32) // 4 == h, peak[rows, :] + jnp.log2(mass), levels)
            write_levels(task, levels)

        if first:

            @pl.when(jnp.logical_and(jnp.logical_not(some), touched[task] != 0))
            def _():
                for h in range(GROUP):
                    write(task, h, before[task, :, h * HEAD : (h + 1) * HEAD])
                write_levels(task, before[task, :, WIDE:])

        if final:

            @pl.when(jnp.logical_and(jnp.logical_not(some), touched[task] == 0))
            def _():
                for h in range(GROUP):
                    write(task, h, jnp.zeros((ROWS, HEAD), jnp.float32))
                write_levels(task, jnp.full((ROWS, 128), NEG, jnp.float32))

        return carry

    lax.fori_loop(0, 8, one_task, 0)


def pack_stats(level, lane):
    high = level.astype(jnp.bfloat16)
    rest = level - high.astype(jnp.float32)
    middle = rest.astype(jnp.bfloat16)
    low = (rest - middle.astype(jnp.float32)).astype(jnp.bfloat16)
    part = lane % 4
    terms = jnp.where(
        part == 0,
        high.astype(jnp.float32),
        jnp.where(part == 1, middle.astype(jnp.float32), low.astype(jnp.float32)),
    )
    return terms.astype(jnp.bfloat16)


def attention(table, place, queries, sources, first, limit, before=()):
    smem = pl.BlockSpec(memory_space=pltpu.SMEM)
    vmem = pl.BlockSpec(memory_space=pltpu.VMEM)
    hbm = pl.BlockSpec(memory_space=pl.ANY)
    if limit is None:
        shape = jax.ShapeDtypeStruct((4, ROWS, BOTH), jnp.bfloat16)
    else:
        shape = jax.ShapeDtypeStruct((8, ROWS, PACK), jnp.float32)
    return pl.pallas_call(
        functools.partial(attention_kernel, first=first, limit=limit),
        in_specs=[smem] * 2 + [vmem] + [hbm] * len(sources) + [vmem] * len(before),
        out_specs=vmem,
        out_shape=shape,
        scratch_shapes=[
            pltpu.VMEM((GROUP * ROWS, HEAD), jnp.bfloat16),
            pltpu.VMEM((GROUP * ROWS, HEAD), jnp.float32),
            pltpu.VMEM((GROUP * ROWS, 2 * HEAD), jnp.float32),
            pltpu.VMEM((2, BLOCK, HEAD), jnp.bfloat16),
            pltpu.VMEM((2, BLOCK, HEAD), jnp.bfloat16),
            pltpu.SMEM((65,), jnp.int32),
            pltpu.SMEM((9,), jnp.int32),
            pltpu.SMEM((8,), jnp.int32),
            pltpu.SemaphoreType.DMA((4, 2)),
        ],
        compiler_params=pltpu.CompilerParams(vmem_limit_bytes=ROOM),
        cost_estimate=pl.CostEstimate(flops=2 * 10**10, bytes_accessed=2**25, transcendentals=0),
        name="handed" if limit is None else "own",
    )(table, place, queries, *sources, *before)


def finish_kernel(parts, out):
    level = parts[:, :, 2 * WIDE :].astype(jnp.float32)
    level = level + pltpu.roll(level, 127, 2) + pltpu.roll(level, 126, 2)
    share = jnp.exp2(level - jnp.max(level, axis=0, keepdims=True))
    share = share / jnp.sum(share, axis=0, keepdims=True)
    for h in range(2 * GROUP):
        columns = slice(h * HEAD, (h + 1) * HEAD)
        joined = jnp.zeros((CHUNK, HEAD), jnp.float32)
        for i in range(16):
            part = parts[i, :, columns].astype(jnp.float32)
            joined = joined + share[i, :, 4 * h : 4 * h + 1] * part
        out[:, columns] = joined.astype(jnp.bfloat16)


def finish(partial):
    parts = lax.all_to_all(
        partial.reshape(16, CHUNK, BOTH), ("x", "y"), split_axis=0, concat_axis=0, tiled=True
    )
    return pl.pallas_call(
        finish_kernel,
        out_shape=jax.ShapeDtypeStruct((CHUNK, 2 * WIDE), jnp.bfloat16),
        compiler_params=pltpu.CompilerParams(vmem_limit_bytes=VMEM),
        name="finish",
    )(parts)


def gather(queries):
    columns = queries.reshape(8, 4, 2 * WIDE).transpose(1, 0, 2)
    sent = jnp.broadcast_to(columns[None], (16, 4, 8, 2 * WIDE)).reshape(64, 8, 2 * WIDE)
    got = lax.all_to_all(sent, ("x", "y", "head"), split_axis=0, concat_axis=0, tiled=True)
    return got.reshape(4 * ROWS, 2 * WIDE)


def shards(queries, keys, values, gates):
    place = jnp.stack([lax.axis_index(name) for name in ("x", "y", "core", "head")]).astype(jnp.int32)
    gathered = gather(queries)
    table = plan(gates, place)
    sources = [in_hbm(a) for a in (keys, values, other_core(keys), other_core(values))]

    slots = []
    for d, half in enumerate(ship(table, place, sources)):
        got = hand_on(half, d)
        slots += [got, other_core(got)]

    partial = attention(table, place, gathered, sources, 0, EARLY)
    partial = attention(table, place, gathered, sources, EARLY, LATER, [partial])
    return finish(attention(table, place, gathered, sources + slots, LATER, None, [partial]))


def solution(mesh):
    parts = jax.sharding.Mesh(mesh.devices.reshape(4, 4, 2, 4), ("x", "y", "core", "head"))
    seq = ("x", "y", "core")
    placed = (P((*seq, "head"), None), P(seq, "head"), P(seq, "head"), P())
    return jax.shard_map(
        shards, mesh=parts, in_specs=placed, out_specs=P(seq, "head"), check_vma=False
    )
```

```python
import functools

import jax
import jax.numpy as jnp
from jax import lax
from jax.experimental import pallas as pl
from jax.experimental.pallas import tpu as pltpu
from jax.sharding import PartitionSpec as P

HEAD = 128
BLOCK = 4096
GROUP = 8
WIDE = GROUP * HEAD
PACK = WIDE + 128
BOTH = 2 * WIDE + 128
CHUNK = 32
ROWS = 4 * CHUNK
SCALE = 128**-0.5 * 1.4426950408889634
NEG = -1e30
NT = (((1,), (1,)), ((), ()))
VMEM = 127 * 2**19
ROOM = 36 * 2**20
EARLY, LATER = 3, 5
HALF = BLOCK // 2
ARRIVAL = 5
DIRECTIONS = ((1, 0), (-1, 0), (0, 1), (0, -1))


def other_core(array):
    return lax.ppermute(array, "core", [(0, 1), (1, 0)])


def in_hbm(array):
    return pltpu.with_memory_space_constraint(array, pltpu.HBM)


def hand_on(array, direction):
    dx, dy = DIRECTIONS[direction]
    axis, step = ("x", dx) if dx else ("y", dy)
    return lax.ppermute(array, axis, [(i, (i + step) % 4) for i in range(4)])


def plan_kernel(gates, table):
    lane = lax.broadcasted_iota(jnp.int32, (8, 128), 1)
    item = lax.broadcasted_iota(jnp.int32, (8, 128), 0)
    variant = lane // 16
    chip = lane % 16
    x, y = chip // 4, chip % 4
    block = chip * 4 + item % 4
    here_x, here_y, core = (lax.axis_index(name) for name in ("x", "y", "core"))
    first = lax.axis_index("head") * 2
    kept = []
    for q in range(4):
        hit = jnp.zeros((8, 128), jnp.int32)
        for k in range(12):
            chosen = jnp.where(item < 4, gates[q, first, k], gates[q, first + 1, k])
            hit = jnp.where(chosen == block, 1, hit)
        kept.append(hit)

    def ahead(value, direction):
        forward = jnp.where(x < 3, pltpu.roll(value, 124, 1), pltpu.roll(value, 12, 1))
        back = jnp.where(x > 0, pltpu.roll(value, 4, 1), pltpu.roll(value, 116, 1))
        up = jnp.where(y < 3, pltpu.roll(value, 127, 1), pltpu.roll(value, 3, 1))
        down = jnp.where(y > 0, pltpu.roll(value, 1, 1), pltpu.roll(value, 125, 1))
        along_x = jnp.where(direction == 0, forward, back)
        return jnp.where(direction < 2, along_x, jnp.where(direction == 2, up, down))

    def over_items(value, how):
        for step in (4, 2, 1):
            value = how(value, pltpu.roll(value, step, 0))
        return value

    own = over_items(kept[0] + kept[1] + kept[2] + kept[3], jnp.add)
    handed = jnp.zeros((8, 128), jnp.int32)
    given = [jnp.zeros((8, 128), jnp.int32)] * 4
    got = [jnp.zeros((8, 128), jnp.int32)] * 4
    for orders in zip((0, 1, 2, 3), (2, 3, 0, 1), (0, 2, 1, 3), (3, 1, 2, 0)):
        direction = jnp.zeros((8, 128), jnp.int32)
        for i, d in enumerate(orders):
            direction = jnp.where(variant // 2 == i, d, direction)
        ready = jnp.maximum(own, ARRIVAL) + handed
        done = jnp.where(handed > 0, ready, own)
        want = jnp.maximum(done - ahead(ready, direction) + variant % 2, 0) >> 1
        left = kept[0] + kept[1] + kept[2] + kept[3]
        moved = jnp.minimum(left, want)
        score = moved * 256 - left * 16 + item
        chosen = jnp.logical_and(score == over_items(score, jnp.maximum), moved > 0)
        moved = jnp.where(chosen, moved, 0)
        entry = jnp.where(chosen, item * 16, 0)
        taken = jnp.zeros((8, 128), jnp.int32)
        for q in range(4):
            goes = jnp.where(taken < moved, kept[q], 0)
            taken = taken + goes
            kept[q] = kept[q] - goes
            entry = entry + goes * (1 << q)
        moved = over_items(moved, jnp.add)
        entry = over_items(entry, jnp.add)
        gets = ahead(entry, direction ^ 1)
        for d in range(4):
            given[d] = jnp.where(direction == d, entry, given[d])
            got[d] = jnp.where(direction == d, gets, got[d])
        own = own - moved
        handed = handed + ahead(moved, direction ^ 1)
    worst = jnp.where(handed > 0, jnp.maximum(own, ARRIVAL) + handed, own)
    for step in (8, 4, 2, 1):
        around = jnp.where(chip + step < 16, pltpu.roll(worst, 128 - step, 1), pltpu.roll(worst, 16 - step, 1))
        worst = jnp.maximum(worst, around)
    best = jnp.min((worst * 8 + variant).astype(jnp.float32)).astype(jnp.int32) % 8
    here = best * 16 + here_x * 4 + here_y
    keeps = jnp.zeros((8, 128), jnp.int32)
    for q in range(4):
        keeps = keeps + (kept[q] << (8 * q + item))
    row = jnp.zeros((8, 128), jnp.int32)
    for i, value in enumerate([over_items(keeps, jnp.add)] + given + got):
        row = jnp.where(lane == i, pltpu.roll(value, (i + 128 - here) % 128, 1), row)
    for i, value in enumerate((here_x, here_y, core)):
        row = jnp.where(lane == 9 + i, value, row)
    table[...] = row


def plan(gates):
    return pl.pallas_call(
        plan_kernel,
        in_specs=[pl.BlockSpec(memory_space=pltpu.SMEM)],
        out_shape=jax.ShapeDtypeStruct((8, 128), jnp.int32),
        compiler_params=pltpu.CompilerParams(vmem_limit_bytes=VMEM),
        name="plan",
    )(gates)


def ship_kernel(table, keys, values, near_keys, near_values, *refs):
    outs, sems = refs[:4], refs[4]
    core = table[0, 11]
    for phase in range(2):
        for d in range(4):
            item = table[0, 1 + d] // 16
            block = item % 4
            rows = pl.ds(pl.multiple_of((block % 2) * BLOCK + core * HALF, HALF), HALF)
            cols = pl.ds(pl.multiple_of((item // 4) * HEAD, HEAD), HEAD)
            own = block // 2 == core
            for near, pair in ((False, (keys, values)), (True, (near_keys, near_values))):

                @pl.when(own != near)
                def _():
                    for part in range(2):
                        copy = pltpu.make_async_copy(
                            pair[part].at[rows, cols], outs[d].at[part], sems.at[d, part]
                        )
                        if phase == 0:
                            copy.start()
                        else:
                            copy.wait()


def ship(table, sources):
    hbm = pl.BlockSpec(memory_space=pl.ANY)
    return pl.pallas_call(
        ship_kernel,
        in_specs=[pl.BlockSpec(memory_space=pltpu.SMEM)] + [hbm] * 4,
        out_specs=[pl.BlockSpec(memory_space=pltpu.VMEM)] * 4,
        out_shape=[jax.ShapeDtypeStruct((2, HALF, HEAD), jnp.bfloat16)] * 4,
        scratch_shapes=[pltpu.SemaphoreType.DMA((4, 2))],
        cost_estimate=pl.CostEstimate(flops=0, bytes_accessed=2**10, transcendentals=0),
        compiler_params=pltpu.CompilerParams(vmem_limit_bytes=VMEM // 2),
        name="ship",
    )(table, *sources)


def attention_kernel(table, queries, *refs, first, limit):
    final = limit is None
    sources, refs = refs[: 12 if final else 4], refs[12 if final else 4 :]
    if first:
        before, refs = refs[0], refs[1:]
    out, stacked, peak, total, key_buffer, value_buffer, units, starts, touched, sems = refs
    x, y, core = table[0, 9], table[0, 10], table[0, 11]
    lane = lax.broadcasted_iota(jnp.int32, (ROWS, 128), 1)

    def copies(unit, slot):
        code = (units[unit] // 2) % 8
        head = units[unit] // 16
        result = []
        rows = pl.ds(pl.multiple_of((code % 2) * BLOCK, BLOCK), BLOCK)
        cols = pl.ds(pl.multiple_of(head * HEAD, HEAD), HEAD)
        for near in range(2):
            keys, values = sources[2 * near], sources[2 * near + 1]
            group = [
                pltpu.make_async_copy(keys.at[rows, cols], key_buffer.at[slot], sems.at[0, slot]),
                pltpu.make_async_copy(values.at[rows, cols], value_buffer.at[slot], sems.at[1, slot]),
            ]
            result.append((code // 2 == near, group))
        for d in range(4 if final else 0):
            group = []
            for part, buffer in ((0, key_buffer), (1, value_buffer)):
                for half, source in ((core, sources[4 + 2 * d]), (1 - core, sources[5 + 2 * d])):
                    rows = pl.ds(pl.multiple_of(half * HALF, HALF), HALF)
                    sem = sems.at[len(group), slot]
                    group.append(pltpu.make_async_copy(source.at[part], buffer.at[slot, rows], sem))
            result.append((code == 4 + d, group))
        return result

    def start(unit, slot):
        for inside, group in copies(unit, slot):

            @pl.when(inside)
            def _():
                for copy in group:
                    copy.start()

    def wait(unit, slot):
        for inside, group in copies(unit, slot):

            @pl.when(inside)
            def _():
                for copy in group:
                    copy.wait()

    def list_units(t, carry):
        count, seen = carry
        starts[t] = count
        head, q = t // 4, t % 4
        seen_before = seen
        for code in range(8 if final else 4):
            if code < 4:
                own = (core if code < 2 else 1 - core) * 2 + code % 2
                wanted = (table[0, 0] >> (8 * q + 4 * head + own)) & 1
                block = (x * 4 + y) * 4 + own
                ours = seen >= first
                if not final:
                    ours = jnp.logical_and(ours, seen < limit)
                seen = seen + wanted
                wanted = jnp.where(ours, wanted, 0)
            else:
                dx, dy = DIRECTIONS[code - 4]
                giver = ((x - dx + 4) % 4) * 4 + (y - dy + 4) % 4
                entry = table[0, 1 + code]
                item = entry // 16
                wanted = jnp.where(item // 4 == head, (entry >> q) & 1, 0)
                block = giver * 4 + item % 4
            at = count

            @pl.when(wanted != 0)
            def _():
                units[at] = 16 * head + 2 * code + (block == 63).astype(jnp.int32)

            count = count + wanted
        touched[t] = (jnp.minimum(seen, first) > seen_before).astype(jnp.int32)
        return count, seen

    starts[8] = lax.fori_loop(0, 8, list_units, (0, 0))[0]

    @pl.when(starts[8] > 0)
    def _():
        start(0, 0)

    def columns(task, h):
        return pl.ds(pl.multiple_of((task // 4) * WIDE + h * HEAD, HEAD), HEAD)

    def load(task):
        tokens = pl.ds(pl.multiple_of((task % 4) * ROWS, ROWS), ROWS)
        for h in range(GROUP):
            stacked[h * ROWS : (h + 1) * ROWS, :] = queries[tokens, columns(task, h)]

        @pl.when(touched[task] == 0)
        def _():
            peak[...] = jnp.full(peak.shape, NEG, jnp.float32)
            total[...] = jnp.zeros(total.shape, jnp.float32)

        if first:

            @pl.when(touched[task] != 0)
            def _():
                total[:, HEAD:] = jnp.ones((GROUP * ROWS, HEAD), jnp.float32)
                for h in range(GROUP):
                    rows = slice(h * ROWS, (h + 1) * ROWS)
                    level = before[task, :, WIDE + 4 * h : WIDE + 4 * h + 1]
                    peak[rows, :] = jnp.broadcast_to(level, (ROWS, HEAD))
                    total[rows, :HEAD] = before[task, :, h * HEAD : (h + 1) * HEAD]

    tile = 2 * ROWS

    def attend(task, slot, masked):
        keys = key_buffer[slot]
        values = jnp.concatenate(
            [value_buffer[slot], jnp.ones((BLOCK, HEAD), jnp.bfloat16)], axis=1
        )

        def score(r):
            return lax.dot_general(
                stacked[r : r + tile, :], keys, NT, preferred_element_type=jnp.float32
            )

        s = score(0)
        for r in range(0, GROUP * ROWS, tile):
            after = score(r + tile) if r + tile < GROUP * ROWS else None
            if masked:
                row = lax.broadcasted_iota(jnp.int32, (tile, 1024), 0) % ROWS
                token = (task % 4) * 256 + (row // CHUNK) * 64 + core * CHUNK + row % CHUNK
                col = lax.broadcasted_iota(jnp.int32, (tile, 1024), 1)
                s = jnp.concatenate(
                    [s[:, :3072], jnp.where(col <= token, s[:, 3072:], NEG)], axis=1
                )
            rows = slice(r, r + tile)
            old = peak[rows, :]
            new = jnp.maximum(old, jnp.max(s, axis=1, keepdims=True) * SCALE)
            factor = jnp.exp2(old - new)
            weights = jnp.exp2(s * SCALE - new[:, :1]).astype(jnp.bfloat16)
            peak[rows, :] = new
            total[rows, :] = total[rows, :] * jnp.concatenate([factor, factor], axis=1) + jnp.dot(
                weights, values, preferred_element_type=jnp.float32
            )
            s = after

    def visit(unit, task):
        slot = unit % 2
        wait(unit, slot)

        @pl.when(unit + 1 < starts[8])
        def _():
            start(unit + 1, 1 - slot)

        masked = units[unit] % 2

        @pl.when(masked != 0)
        def _():
            attend(task, slot, True)

        @pl.when(masked == 0)
        def _():
            attend(task, slot, False)

        return task

    def prepare():
        for h in range(GROUP):
            stacked[h * ROWS : (h + 1) * ROWS, :] = queries[:, h * HEAD : (h + 1) * HEAD]
        if handed:
            for h in range(GROUP):
                rows = slice(h * ROWS, (h + 1) * ROWS)
                level = before[0, :, WIDE + 4 * h : WIDE + 4 * h + 1]
                peak[rows, :] = jnp.broadcast_to(level, (ROWS, HEAD))
                total[rows, :HEAD] = before[0, :, h * HEAD : (h + 1) * HEAD]
                total[rows, HEAD:] = jnp.broadcast_to(
                    jnp.where(level > 0.5 * NEG, 1.0, 0.0), (ROWS, HEAD)
                )
        else:
            peak[...] = jnp.full(peak.shape, NEG, jnp.float32)
            total[...] = jnp.zeros(total.shape, jnp.float32)

    def write(task, h, value):
        if final:
            out[task % 4, :, columns(task, h)] = value.astype(jnp.bfloat16)
        else:
            out[task, :, h * HEAD : (h + 1) * HEAD] = value

    def write_levels(task, levels):
        if not final:
            out[task, :, WIDE:] = levels
            return
        q = task % 4
        packed = pack_stats(levels, lane)
        kept = out[q, :, 2 * WIDE :].astype(jnp.float32)
        kept = jnp.where(jnp.logical_and(task >= 4, lane < 32), kept, packed.astype(jnp.float32))
        out[q, :, 2 * WIDE :] = kept.astype(jnp.bfloat16)

    def one_task(task, carry):
        some = starts[task] < starts[task + 1]

        @pl.when(some)
        def _():
            load(task)
            lax.fori_loop(starts[task], starts[task + 1], visit, task)
            levels = jnp.full((ROWS, 128), NEG, jnp.float32)
            for h in range(GROUP):
                rows = slice(h * ROWS, (h + 1) * ROWS)
                mass = total[rows, HEAD:]
                write(task, h, total[rows, :HEAD] / mass)
                levels = jnp.where((lane % 32) // 4 == h, peak[rows, :] + jnp.log2(mass), levels)
            write_levels(task, levels)

        if first:

            @pl.when(jnp.logical_and(jnp.logical_not(some), touched[task] != 0))
            def _():
                for h in range(GROUP):
                    write(task, h, before[task, :, h * HEAD : (h + 1) * HEAD])
                write_levels(task, before[task, :, WIDE:])

        if final:

            @pl.when(jnp.logical_and(jnp.logical_not(some), touched[task] == 0))
            def _():
                for h in range(GROUP):
                    write(task, h, jnp.zeros((ROWS, HEAD), jnp.float32))
                write_levels(task, jnp.full((ROWS, 128), NEG, jnp.float32))

        return carry

    lax.fori_loop(0, 8, one_task, 0)


def pack_stats(level, lane):
    high = level.astype(jnp.bfloat16)
    rest = level - high.astype(jnp.float32)
    middle = rest.astype(jnp.bfloat16)
    low = (rest - middle.astype(jnp.float32)).astype(jnp.bfloat16)
    part = lane % 4
    terms = jnp.where(
        part == 0,
        high.astype(jnp.float32),
        jnp.where(part == 1, middle.astype(jnp.float32), low.astype(jnp.float32)),
    )
    return terms.astype(jnp.bfloat16)


def attention(table, queries, sources, first, limit, before=()):
    smem = pl.BlockSpec(memory_space=pltpu.SMEM)
    vmem = pl.BlockSpec(memory_space=pltpu.VMEM)
    hbm = pl.BlockSpec(memory_space=pl.ANY)
    if limit is None:
        shape = jax.ShapeDtypeStruct((4, ROWS, BOTH), jnp.bfloat16)
    else:
        shape = jax.ShapeDtypeStruct((8, ROWS, PACK), jnp.float32)
    return pl.pallas_call(
        functools.partial(attention_kernel, first=first, limit=limit),
        in_specs=[smem, vmem] + [hbm] * len(sources) + [vmem] * len(before),
        out_specs=vmem,
        out_shape=shape,
        scratch_shapes=[
            pltpu.VMEM((GROUP * ROWS, HEAD), jnp.bfloat16),
            pltpu.VMEM((GROUP * ROWS, HEAD), jnp.float32),
            pltpu.VMEM((GROUP * ROWS, 2 * HEAD), jnp.float32),
            pltpu.VMEM((2, BLOCK, HEAD), jnp.bfloat16),
            pltpu.VMEM((2, BLOCK, HEAD), jnp.bfloat16),
            pltpu.SMEM((65,), jnp.int32),
            pltpu.SMEM((9,), jnp.int32),
            pltpu.SMEM((8,), jnp.int32),
            pltpu.SemaphoreType.DMA((4, 2)),
        ],
        compiler_params=pltpu.CompilerParams(vmem_limit_bytes=ROOM),
        cost_estimate=pl.CostEstimate(flops=2 * 10**10, bytes_accessed=2**25, transcendentals=0),
        name="handed" if limit is None else "own",
    )(table, queries, *sources, *before)


def finish_kernel(parts, out):
    level = parts[:, :, 2 * WIDE :].astype(jnp.float32)
    level = level + pltpu.roll(level, 127, 2) + pltpu.roll(level, 126, 2)
    share = jnp.exp2(level - jnp.max(level, axis=0, keepdims=True))
    share = share / jnp.sum(share, axis=0, keepdims=True)
    for h in range(2 * GROUP):
        columns = slice(h * HEAD, (h + 1) * HEAD)
        joined = jnp.zeros((CHUNK, HEAD), jnp.float32)
        for i in range(16):
            part = parts[i, :, columns].astype(jnp.float32)
            joined = joined + share[i, :, 4 * h : 4 * h + 1] * part
        out[:, columns] = joined.astype(jnp.bfloat16)


def finish(partial):
    parts = lax.all_to_all(
        partial.reshape(16, CHUNK, BOTH), ("x", "y"), split_axis=0, concat_axis=0, tiled=True
    )
    return pl.pallas_call(
        finish_kernel,
        out_shape=jax.ShapeDtypeStruct((CHUNK, 2 * WIDE), jnp.bfloat16),
        compiler_params=pltpu.CompilerParams(vmem_limit_bytes=VMEM),
        name="finish",
    )(parts)


def gather(queries):
    columns = queries.reshape(8, 4, 2 * WIDE).transpose(1, 0, 2)
    sent = jnp.broadcast_to(columns[None], (16, 4, 8, 2 * WIDE)).reshape(64, 8, 2 * WIDE)
    got = lax.all_to_all(sent, ("x", "y", "head"), split_axis=0, concat_axis=0, tiled=True)
    return got.reshape(4 * ROWS, 2 * WIDE)


def shards(queries, keys, values, gates):
    gathered = gather(queries)
    table = plan(gates)
    sources = [in_hbm(a) for a in (keys, values, other_core(keys), other_core(values))]

    slots = []
    for d, half in enumerate(ship(table, sources)):
        got = hand_on(half, d)
        slots += [got, other_core(got)]

    partial = attention(table, gathered, sources, 0, EARLY)
    partial = attention(table, gathered, sources, EARLY, LATER, [partial])
    return finish(attention(table, gathered, sources + slots, LATER, None, [partial]))


def solution(mesh):
    parts = jax.sharding.Mesh(mesh.devices.reshape(4, 4, 2, 4), ("x", "y", "core", "head"))
    seq = ("x", "y", "core")
    placed = (P((*seq, "head"), None), P(seq, "head"), P(seq, "head"), P())
    return jax.shard_map(
        shards, mesh=parts, in_specs=placed, out_specs=P(seq, "head"), check_vma=False
    )
```

```python
import functools

import jax
import jax.numpy as jnp
from jax import lax
from jax.experimental import pallas as pl
from jax.experimental.pallas import tpu as pltpu
from jax.sharding import PartitionSpec as P

HEAD = 128
BLOCK = 4096
GROUP = 8
WIDE = GROUP * HEAD
PACK = WIDE + 128
BOTH = 2 * WIDE + 128
CHUNK = 32
ROWS = 4 * CHUNK
SCALE = 128**-0.5 * 1.4426950408889634
NEG = -1e30
NT = (((1,), (1,)), ((), ()))
VMEM = 127 * 2**19
ROOM = 36 * 2**20
EARLY, LATER = 3, 5
HALF = BLOCK // 2
SPAN = 2048
TILE = 512
ARRIVAL = 5
DIRECTIONS = ((1, 0), (-1, 0), (0, 1), (0, -1))


def other_core(array):
    return lax.ppermute(array, "core", [(0, 1), (1, 0)])


def in_hbm(array):
    return pltpu.with_memory_space_constraint(array, pltpu.HBM)


def hand_on(array, direction):
    dx, dy = DIRECTIONS[direction]
    axis, step = ("x", dx) if dx else ("y", dy)
    return lax.ppermute(array, axis, [(i, (i + step) % 4) for i in range(4)])


def plan_kernel(gates, table):
    lane = lax.broadcasted_iota(jnp.int32, (8, 128), 1)
    item = lax.broadcasted_iota(jnp.int32, (8, 128), 0)
    variant = lane // 16
    chip = lane % 16
    x, y = chip // 4, chip % 4
    block = chip * 4 + item % 4
    here_x, here_y, core = (lax.axis_index(name) for name in ("x", "y", "core"))
    first = lax.axis_index("head") * 2
    kept = []
    for q in range(4):
        hit = jnp.zeros((8, 128), jnp.int32)
        for k in range(12):
            chosen = jnp.where(item < 4, gates[q, first, k], gates[q, first + 1, k])
            hit = jnp.where(chosen == block, 1, hit)
        kept.append(hit)

    def ahead(value, direction):
        forward = jnp.where(x < 3, pltpu.roll(value, 124, 1), pltpu.roll(value, 12, 1))
        back = jnp.where(x > 0, pltpu.roll(value, 4, 1), pltpu.roll(value, 116, 1))
        up = jnp.where(y < 3, pltpu.roll(value, 127, 1), pltpu.roll(value, 3, 1))
        down = jnp.where(y > 0, pltpu.roll(value, 1, 1), pltpu.roll(value, 125, 1))
        along_x = jnp.where(direction == 0, forward, back)
        return jnp.where(direction < 2, along_x, jnp.where(direction == 2, up, down))

    def over_items(value, how):
        for step in (4, 2, 1):
            value = how(value, pltpu.roll(value, step, 0))
        return value

    own = over_items(kept[0] + kept[1] + kept[2] + kept[3], jnp.add)
    handed = jnp.zeros((8, 128), jnp.int32)
    given = [jnp.zeros((8, 128), jnp.int32)] * 4
    got = [jnp.zeros((8, 128), jnp.int32)] * 4
    for orders in zip((0, 1, 2, 3), (2, 3, 0, 1), (0, 2, 1, 3), (3, 1, 2, 0)):
        direction = jnp.zeros((8, 128), jnp.int32)
        for i, d in enumerate(orders):
            direction = jnp.where(variant // 2 == i, d, direction)
        ready = jnp.maximum(own, ARRIVAL) + handed
        done = jnp.where(handed > 0, ready, own)
        want = jnp.maximum(done - ahead(ready, direction) + variant % 2, 0) >> 1
        left = kept[0] + kept[1] + kept[2] + kept[3]
        moved = jnp.minimum(left, want)
        score = moved * 256 - left * 16 + item
        chosen = jnp.logical_and(score == over_items(score, jnp.maximum), moved > 0)
        moved = jnp.where(chosen, moved, 0)
        entry = jnp.where(chosen, item * 16, 0)
        taken = jnp.zeros((8, 128), jnp.int32)
        for q in range(4):
            goes = jnp.where(taken < moved, kept[q], 0)
            taken = taken + goes
            kept[q] = kept[q] - goes
            entry = entry + goes * (1 << q)
        moved = over_items(moved, jnp.add)
        entry = over_items(entry, jnp.add)
        gets = ahead(entry, direction ^ 1)
        for d in range(4):
            given[d] = jnp.where(direction == d, entry, given[d])
            got[d] = jnp.where(direction == d, gets, got[d])
        own = own - moved
        handed = handed + ahead(moved, direction ^ 1)
    worst = jnp.where(handed > 0, jnp.maximum(own, ARRIVAL) + handed, own)
    for step in (8, 4, 2, 1):
        around = jnp.where(chip + step < 16, pltpu.roll(worst, 128 - step, 1), pltpu.roll(worst, 16 - step, 1))
        worst = jnp.maximum(worst, around)
    best = jnp.min((worst * 8 + variant).astype(jnp.float32)).astype(jnp.int32) % 8
    here = best * 16 + here_x * 4 + here_y
    keeps = jnp.zeros((8, 128), jnp.int32)
    for q in range(4):
        keeps = keeps + (kept[q] << (8 * q + item))
    row = jnp.zeros((8, 128), jnp.int32)
    for i, value in enumerate([over_items(keeps, jnp.add)] + given + got):
        row = jnp.where(lane == i, pltpu.roll(value, (i + 128 - here) % 128, 1), row)
    for i, value in enumerate((here_x, here_y, core)):
        row = jnp.where(lane == 9 + i, value, row)
    table[...] = row


def plan(gates):
    return pl.pallas_call(
        plan_kernel,
        in_specs=[pl.BlockSpec(memory_space=pltpu.SMEM)],
        out_shape=jax.ShapeDtypeStruct((8, 128), jnp.int32),
        compiler_params=pltpu.CompilerParams(vmem_limit_bytes=VMEM),
        name="plan",
    )(gates)


def ship_kernel(table, keys, values, near_keys, near_values, *refs):
    outs, sems = refs[:4], refs[4]
    core = table[0, 11]
    for phase in range(2):
        for d in range(4):
            item = table[0, 1 + d] // 16
            block = item % 4
            rows = pl.ds(pl.multiple_of((block % 2) * BLOCK + core * HALF, HALF), HALF)
            cols = pl.ds(pl.multiple_of((item // 4) * HEAD, HEAD), HEAD)
            own = block // 2 == core
            for near, pair in ((False, (keys, values)), (True, (near_keys, near_values))):

                @pl.when(own != near)
                def _():
                    for part in range(2):
                        copy = pltpu.make_async_copy(
                            pair[part].at[rows, cols], outs[d].at[part], sems.at[d, part]
                        )
                        if phase == 0:
                            copy.start()
                        else:
                            copy.wait()


def ship(table, sources):
    hbm = pl.BlockSpec(memory_space=pl.ANY)
    return pl.pallas_call(
        ship_kernel,
        in_specs=[pl.BlockSpec(memory_space=pltpu.SMEM)] + [hbm] * 4,
        out_specs=[pl.BlockSpec(memory_space=pltpu.VMEM)] * 4,
        out_shape=[jax.ShapeDtypeStruct((2, HALF, HEAD), jnp.bfloat16)] * 4,
        scratch_shapes=[pltpu.SemaphoreType.DMA((4, 2))],
        cost_estimate=pl.CostEstimate(flops=0, bytes_accessed=2**10, transcendentals=0),
        compiler_params=pltpu.CompilerParams(vmem_limit_bytes=VMEM // 2),
        name="ship",
    )(table, *sources)


def attention_kernel(table, left, right, *refs, first, limit):
    final = limit is None
    sources, refs = refs[: 12 if final else 4], refs[12 if final else 4 :]
    if first:
        before, refs = refs[0], refs[1:]
    out, stacked, peak, total, key_buffer, value_buffer, units, starts, touched, sems = refs
    x, y, core = table[0, 9], table[0, 10], table[0, 11]
    lane = lax.broadcasted_iota(jnp.int32, (ROWS, 128), 1)

    def copies(unit, slot):
        code = (units[unit] // 2) % 8
        head = units[unit] // 16
        result = []
        rows = pl.ds(pl.multiple_of((code % 2) * BLOCK, BLOCK), BLOCK)
        cols = pl.ds(pl.multiple_of(head * HEAD, HEAD), HEAD)
        for near in range(2):
            keys, values = sources[2 * near], sources[2 * near + 1]
            group = [
                pltpu.make_async_copy(keys.at[rows, cols], key_buffer.at[slot], sems.at[0, slot]),
                pltpu.make_async_copy(values.at[rows, cols], value_buffer.at[slot], sems.at[1, slot]),
            ]
            result.append((code // 2 == near, group))
        for d in range(4 if final else 0):
            group = []
            for part, buffer in ((0, key_buffer), (1, value_buffer)):
                for half, source in ((core, sources[4 + 2 * d]), (1 - core, sources[5 + 2 * d])):
                    rows = pl.ds(pl.multiple_of(half * HALF, HALF), HALF)
                    sem = sems.at[len(group), slot]
                    group.append(pltpu.make_async_copy(source.at[part], buffer.at[slot, rows], sem))
            result.append((code == 4 + d, group))
        return result

    def start(unit, slot):
        for inside, group in copies(unit, slot):

            @pl.when(inside)
            def _():
                for copy in group:
                    copy.start()

    def wait(unit, slot):
        for inside, group in copies(unit, slot):

            @pl.when(inside)
            def _():
                for copy in group:
                    copy.wait()

    def list_units(t, carry):
        count, seen = carry
        starts[t] = count
        head, q = t // 4, t % 4
        seen_before = seen
        for code in range(8 if final else 4):
            if code < 4:
                own = (core if code < 2 else 1 - core) * 2 + code % 2
                wanted = (table[0, 0] >> (8 * q + 4 * head + own)) & 1
                block = (x * 4 + y) * 4 + own
                ours = seen >= first
                if not final:
                    ours = jnp.logical_and(ours, seen < limit)
                seen = seen + wanted
                wanted = jnp.where(ours, wanted, 0)
            else:
                dx, dy = DIRECTIONS[code - 4]
                giver = ((x - dx + 4) % 4) * 4 + (y - dy + 4) % 4
                entry = table[0, 1 + code]
                item = entry // 16
                wanted = jnp.where(item // 4 == head, (entry >> q) & 1, 0)
                block = giver * 4 + item % 4
            at = count

            @pl.when(wanted != 0)
            def _():
                units[at] = 16 * head + 2 * code + (block == 63).astype(jnp.int32)

            count = count + wanted
        touched[t] = (jnp.minimum(seen, first) > seen_before).astype(jnp.int32)
        return count, seen

    starts[8] = lax.fori_loop(0, 8, list_units, (0, 0))[0]

    @pl.when(starts[8] > 0)
    def _():
        start(0, 0)

    def columns(task, h):
        return pl.ds(pl.multiple_of((task // 4) * WIDE + h * HEAD, HEAD), HEAD)

    def load(task):
        q = task % 4
        for head in range(2):

            @pl.when(task // 4 == head)
            def _():
                for h in range(GROUP):
                    for y in range(4):
                        at = h * ROWS + y * CHUNK
                        part = left[q, y] if head == 0 else right[y, q]
                        stacked[at : at + CHUNK, :] = part[:, h * HEAD : (h + 1) * HEAD]

        @pl.when(touched[task] == 0)
        def _():
            peak[...] = jnp.full(peak.shape, NEG, jnp.float32)
            total[...] = jnp.zeros(total.shape, jnp.float32)

        if first:

            @pl.when(touched[task] != 0)
            def _():
                total[:, HEAD:] = jnp.ones((GROUP * ROWS, HEAD), jnp.float32)
                for h in range(GROUP):
                    rows = slice(h * ROWS, (h + 1) * ROWS)
                    level = before[task, :, WIDE + 4 * h : WIDE + 4 * h + 1]
                    peak[rows, :] = jnp.broadcast_to(level, (ROWS, HEAD))
                    total[rows, :HEAD] = before[task, :, h * HEAD : (h + 1) * HEAD]

    def attend(task, slot, masked):
        steps = [(k, r) for k in range(0, BLOCK, SPAN) for r in range(0, GROUP * ROWS, TILE)]

        def score(k, r):
            keys = key_buffer[slot, k : k + SPAN, :]
            return lax.dot_general(
                stacked[r : r + TILE, :], keys, NT, preferred_element_type=jnp.float32
            )

        s = score(*steps[0])
        for i, (k, r) in enumerate(steps):
            after = score(*steps[i + 1]) if i + 1 < len(steps) else None
            if masked and k + SPAN == BLOCK:
                row = lax.broadcasted_iota(jnp.int32, (TILE, 1024), 0) % ROWS
                token = (task % 4) * 256 + (row // CHUNK) * 64 + core * CHUNK + row % CHUNK
                col = lax.broadcasted_iota(jnp.int32, (TILE, 1024), 1)
                tail = jnp.where(col <= token, s[:, SPAN - 1024 :], NEG)
                s = jnp.concatenate([s[:, : SPAN - 1024], tail], axis=1)
            rows = slice(r, r + TILE)
            old = peak[rows, :]
            new = jnp.maximum(old, jnp.max(s, axis=1, keepdims=True) * SCALE)
            factor = jnp.exp2(old - new)
            weights = jnp.exp2(s * SCALE - new[:, :1]).astype(jnp.bfloat16)
            peak[rows, :] = new
            values = jnp.concatenate(
                [value_buffer[slot, k : k + SPAN, :], jnp.ones((SPAN, HEAD), jnp.bfloat16)], axis=1
            )
            total[rows, :] = total[rows, :] * jnp.concatenate([factor, factor], axis=1) + jnp.dot(
                weights, values, preferred_element_type=jnp.float32
            )
            s = after

    def visit(unit, task):
        slot = unit % 2
        wait(unit, slot)

        @pl.when(unit + 1 < starts[8])
        def _():
            start(unit + 1, 1 - slot)

        masked = units[unit] % 2

        @pl.when(masked != 0)
        def _():
            attend(task, slot, True)

        @pl.when(masked == 0)
        def _():
            attend(task, slot, False)

        return task

    def prepare():
        for h in range(GROUP):
            stacked[h * ROWS : (h + 1) * ROWS, :] = queries[:, h * HEAD : (h + 1) * HEAD]
        if handed:
            for h in range(GROUP):
                rows = slice(h * ROWS, (h + 1) * ROWS)
                level = before[0, :, WIDE + 4 * h : WIDE + 4 * h + 1]
                peak[rows, :] = jnp.broadcast_to(level, (ROWS, HEAD))
                total[rows, :HEAD] = before[0, :, h * HEAD : (h + 1) * HEAD]
                total[rows, HEAD:] = jnp.broadcast_to(
                    jnp.where(level > 0.5 * NEG, 1.0, 0.0), (ROWS, HEAD)
                )
        else:
            peak[...] = jnp.full(peak.shape, NEG, jnp.float32)
            total[...] = jnp.zeros(total.shape, jnp.float32)

    def write(task, h, value):
        if final:
            out[task % 4, :, columns(task, h)] = value.astype(jnp.bfloat16)
        else:
            out[task, :, h * HEAD : (h + 1) * HEAD] = value

    def write_levels(task, levels):
        if not final:
            out[task, :, WIDE:] = levels
            return
        q = task % 4
        packed = pack_stats(levels, lane)
        kept = out[q, :, 2 * WIDE :].astype(jnp.float32)
        kept = jnp.where(jnp.logical_and(task >= 4, lane < 32), kept, packed.astype(jnp.float32))
        out[q, :, 2 * WIDE :] = kept.astype(jnp.bfloat16)

    def one_task(task, carry):
        some = starts[task] < starts[task + 1]

        @pl.when(some)
        def _():
            load(task)
            lax.fori_loop(starts[task], starts[task + 1], visit, task)
            levels = jnp.full((ROWS, 128), NEG, jnp.float32)
            for h in range(GROUP):
                rows = slice(h * ROWS, (h + 1) * ROWS)
                mass = total[rows, HEAD:]
                write(task, h, total[rows, :HEAD] / mass)
                levels = jnp.where((lane % 32) // 4 == h, peak[rows, :] + jnp.log2(mass), levels)
            write_levels(task, levels)

        if first:

            @pl.when(jnp.logical_and(jnp.logical_not(some), touched[task] != 0))
            def _():
                for h in range(GROUP):
                    write(task, h, before[task, :, h * HEAD : (h + 1) * HEAD])
                write_levels(task, before[task, :, WIDE:])

        if final:

            @pl.when(jnp.logical_and(jnp.logical_not(some), touched[task] == 0))
            def _():
                for h in range(GROUP):
                    write(task, h, jnp.zeros((ROWS, HEAD), jnp.float32))
                write_levels(task, jnp.full((ROWS, 128), NEG, jnp.float32))

        return carry

    lax.fori_loop(0, 8, one_task, 0)


def pack_stats(level, lane):
    high = level.astype(jnp.bfloat16)
    rest = level - high.astype(jnp.float32)
    middle = rest.astype(jnp.bfloat16)
    low = (rest - middle.astype(jnp.float32)).astype(jnp.bfloat16)
    part = lane % 4
    terms = jnp.where(
        part == 0,
        high.astype(jnp.float32),
        jnp.where(part == 1, middle.astype(jnp.float32), low.astype(jnp.float32)),
    )
    return terms.astype(jnp.bfloat16)


def attention(table, queries, sources, first, limit, before=()):
    smem = pl.BlockSpec(memory_space=pltpu.SMEM)
    vmem = pl.BlockSpec(memory_space=pltpu.VMEM)
    hbm = pl.BlockSpec(memory_space=pl.ANY)
    if limit is None:
        shape = jax.ShapeDtypeStruct((4, ROWS, BOTH), jnp.bfloat16)
    else:
        shape = jax.ShapeDtypeStruct((8, ROWS, PACK), jnp.float32)
    return pl.pallas_call(
        functools.partial(attention_kernel, first=first, limit=limit),
        in_specs=[smem, vmem, vmem] + [hbm] * len(sources) + [vmem] * len(before),
        out_specs=vmem,
        out_shape=shape,
        scratch_shapes=[
            pltpu.VMEM((GROUP * ROWS, HEAD), jnp.bfloat16),
            pltpu.VMEM((GROUP * ROWS, HEAD), jnp.float32),
            pltpu.VMEM((GROUP * ROWS, 2 * HEAD), jnp.float32),
            pltpu.VMEM((2, BLOCK, HEAD), jnp.bfloat16),
            pltpu.VMEM((2, BLOCK, HEAD), jnp.bfloat16),
            pltpu.SMEM((65,), jnp.int32),
            pltpu.SMEM((9,), jnp.int32),
            pltpu.SMEM((8,), jnp.int32),
            pltpu.SemaphoreType.DMA((4, 2)),
        ],
        compiler_params=pltpu.CompilerParams(vmem_limit_bytes=ROOM),
        cost_estimate=pl.CostEstimate(flops=2 * 10**10, bytes_accessed=2**25, transcendentals=0),
        name="handed" if limit is None else "own",
    )(table, *queries, *sources, *before)


def finish_kernel(parts, out):
    level = parts[:, :, 2 * WIDE :].astype(jnp.float32)
    level = level + pltpu.roll(level, 127, 2) + pltpu.roll(level, 126, 2)
    share = jnp.exp2(level - jnp.max(level, axis=0, keepdims=True))
    share = share / jnp.sum(share, axis=0, keepdims=True)
    for h in range(2 * GROUP):
        columns = slice(h * HEAD, (h + 1) * HEAD)
        joined = jnp.zeros((CHUNK, HEAD), jnp.float32)
        for i in range(16):
            part = parts[i, :, columns].astype(jnp.float32)
            joined = joined + share[i, :, 4 * h : 4 * h + 1] * part
        out[:, columns] = joined.astype(jnp.bfloat16)


def finish(partial):
    parts = lax.all_to_all(
        partial.reshape(16, CHUNK, BOTH), ("x", "y"), split_axis=0, concat_axis=0, tiled=True
    )
    return pl.pallas_call(
        finish_kernel,
        out_shape=jax.ShapeDtypeStruct((CHUNK, 2 * WIDE), jnp.bfloat16),
        compiler_params=pltpu.CompilerParams(vmem_limit_bytes=VMEM),
        name="finish",
    )(parts)


def gather(queries, head, axes):
    columns = queries.reshape(8, 4, 2, WIDE)[:, :, head].transpose(1, 0, 2)
    sent = jnp.broadcast_to(columns[None], (4, 4, 8, WIDE)).reshape(16, 8, WIDE)
    got = lax.all_to_all(sent, (axes[0], "head"), split_axis=0, concat_axis=0, tiled=True)
    sent = jnp.broadcast_to(got.reshape(1, ROWS, WIDE), (4, ROWS, WIDE))
    got = lax.all_to_all(sent, axes[1], split_axis=0, concat_axis=0, tiled=True)
    return got.reshape(4, 4, CHUNK, WIDE)


def shards(queries, keys, values, gates):
    gathered = [gather(queries, 0, "yx"), gather(queries, 1, "xy")]
    table = plan(gates)
    sources = [in_hbm(a) for a in (keys, values, other_core(keys), other_core(values))]

    slots = []
    for d, half in enumerate(ship(table, sources)):
        got = hand_on(half, d)
        slots += [got, other_core(got)]

    partial = attention(table, gathered, sources, 0, EARLY)
    partial = attention(table, gathered, sources, EARLY, LATER, [partial])
    return finish(attention(table, gathered, sources + slots, LATER, None, [partial]))


def solution(mesh):
    parts = jax.sharding.Mesh(mesh.devices.reshape(4, 4, 2, 4), ("x", "y", "core", "head"))
    seq = ("x", "y", "core")
    placed = (P((*seq, "head"), None), P(seq, "head"), P(seq, "head"), P())
    return jax.shard_map(
        shards, mesh=parts, in_specs=placed, out_specs=P(seq, "head"), check_vma=False
    )
```

```python
import functools

import jax
import jax.numpy as jnp
from jax import lax
from jax.experimental import pallas as pl
from jax.experimental.pallas import tpu as pltpu
from jax.sharding import PartitionSpec as P

HEAD = 128
BLOCK = 4096
GROUP = 8
WIDE = GROUP * HEAD
PACK = WIDE + 128
BOTH = 2 * WIDE + 128
CHUNK = 32
ROWS = 4 * CHUNK
SCALE = 128**-0.5 * 1.4426950408889634
NEG = -1e30
NT = (((1,), (1,)), ((), ()))
VMEM = 127 * 2**19
ROOM = 36 * 2**20
EARLY, LATER = 3, 5
HALF = BLOCK // 2
SPAN = 2048
TILE = 512
ARRIVAL = 4
DIRECTIONS = ((1, 0), (-1, 0), (0, 1), (0, -1))


def other_core(array):
    return lax.ppermute(array, "core", [(0, 1), (1, 0)])


def in_hbm(array):
    return pltpu.with_memory_space_constraint(array, pltpu.HBM)


def hand_on(array, direction):
    dx, dy = DIRECTIONS[direction]
    axis, step = ("x", dx) if dx else ("y", dy)
    return lax.ppermute(array, axis, [(i, (i + step) % 4) for i in range(4)])


def plan_kernel(gates, table):
    lane = lax.broadcasted_iota(jnp.int32, (8, 128), 1)
    item = lax.broadcasted_iota(jnp.int32, (8, 128), 0)
    variant = lane // 16
    chip = lane % 16
    x, y = chip // 4, chip % 4
    block = chip * 4 + item % 4
    here_x, here_y, core = (lax.axis_index(name) for name in ("x", "y", "core"))
    first = lax.axis_index("head") * 2
    kept = []
    for q in range(4):
        hit = jnp.zeros((8, 128), jnp.int32)
        for k in range(12):
            chosen = jnp.where(item < 4, gates[q, first, k], gates[q, first + 1, k])
            hit = jnp.where(chosen == block, 1, hit)
        kept.append(hit)

    def ahead(value, direction):
        forward = jnp.where(x < 3, pltpu.roll(value, 124, 1), pltpu.roll(value, 12, 1))
        back = jnp.where(x > 0, pltpu.roll(value, 4, 1), pltpu.roll(value, 116, 1))
        up = jnp.where(y < 3, pltpu.roll(value, 127, 1), pltpu.roll(value, 3, 1))
        down = jnp.where(y > 0, pltpu.roll(value, 1, 1), pltpu.roll(value, 125, 1))
        along_x = jnp.where(direction == 0, forward, back)
        return jnp.where(direction < 2, along_x, jnp.where(direction == 2, up, down))

    def over_items(value, how):
        for step in (4, 2, 1):
            value = how(value, pltpu.roll(value, step, 0))
        return value

    own = over_items(kept[0] + kept[1] + kept[2] + kept[3], jnp.add)
    handed = jnp.zeros((8, 128), jnp.int32)
    given = [jnp.zeros((8, 128), jnp.int32)] * 4
    got = [jnp.zeros((8, 128), jnp.int32)] * 4
    for orders in zip((0, 1, 2, 3), (2, 3, 0, 1), (0, 2, 1, 3), (3, 1, 2, 0)):
        direction = jnp.zeros((8, 128), jnp.int32)
        for i, d in enumerate(orders):
            direction = jnp.where(variant // 2 == i, d, direction)
        ready = jnp.maximum(own, ARRIVAL) + handed
        done = jnp.where(handed > 0, ready, own)
        want = jnp.maximum(done - ahead(ready, direction) + variant % 2, 0) >> 1
        left = kept[0] + kept[1] + kept[2] + kept[3]
        moved = jnp.minimum(left, want)
        score = moved * 256 - left * 16 + item
        chosen = jnp.logical_and(score == over_items(score, jnp.maximum), moved > 0)
        moved = jnp.where(chosen, moved, 0)
        entry = jnp.where(chosen, item * 16, 0)
        taken = jnp.zeros((8, 128), jnp.int32)
        for q in range(4):
            goes = jnp.where(taken < moved, kept[q], 0)
            taken = taken + goes
            kept[q] = kept[q] - goes
            entry = entry + goes * (1 << q)
        moved = over_items(moved, jnp.add)
        entry = over_items(entry, jnp.add)
        gets = ahead(entry, direction ^ 1)
        for d in range(4):
            given[d] = jnp.where(direction == d, entry, given[d])
            got[d] = jnp.where(direction == d, gets, got[d])
        own = own - moved
        handed = handed + ahead(moved, direction ^ 1)
    worst = jnp.where(handed > 0, jnp.maximum(own, ARRIVAL) + handed, own)
    for step in (8, 4, 2, 1):
        around = jnp.where(chip + step < 16, pltpu.roll(worst, 128 - step, 1), pltpu.roll(worst, 16 - step, 1))
        worst = jnp.maximum(worst, around)
    best = jnp.min((worst * 8 + variant).astype(jnp.float32)).astype(jnp.int32) % 8
    here = best * 16 + here_x * 4 + here_y
    keeps = jnp.zeros((8, 128), jnp.int32)
    for q in range(4):
        keeps = keeps + (kept[q] << (8 * q + item))
    row = jnp.zeros((8, 128), jnp.int32)
    for i, value in enumerate([over_items(keeps, jnp.add)] + given + got):
        row = jnp.where(lane == i, pltpu.roll(value, (i + 128 - here) % 128, 1), row)
    for i, value in enumerate((here_x, here_y, core)):
        row = jnp.where(lane == 9 + i, value, row)
    table[...] = row


def plan(gates):
    return pl.pallas_call(
        plan_kernel,
        in_specs=[pl.BlockSpec(memory_space=pltpu.SMEM)],
        out_shape=jax.ShapeDtypeStruct((8, 128), jnp.int32),
        compiler_params=pltpu.CompilerParams(vmem_limit_bytes=VMEM),
        name="plan",
    )(gates)


def ship_kernel(table, keys, values, near_keys, near_values, *refs):
    outs, sems = refs[:4], refs[4]
    core = table[0, 11]
    for phase in range(2):
        for d in range(4):
            item = table[0, 1 + d] // 16
            block = item % 4
            rows = pl.ds(pl.multiple_of((block % 2) * BLOCK + core * HALF, HALF), HALF)
            cols = pl.ds(pl.multiple_of((item // 4) * HEAD, HEAD), HEAD)
            own = block // 2 == core
            for near, pair in ((False, (keys, values)), (True, (near_keys, near_values))):

                @pl.when(own != near)
                def _():
                    for part in range(2):
                        copy = pltpu.make_async_copy(
                            pair[part].at[rows, cols], outs[d].at[part], sems.at[d, part]
                        )
                        if phase == 0:
                            copy.start()
                        else:
                            copy.wait()


def ship(table, sources):
    hbm = pl.BlockSpec(memory_space=pl.ANY)
    return pl.pallas_call(
        ship_kernel,
        in_specs=[pl.BlockSpec(memory_space=pltpu.SMEM)] + [hbm] * 4,
        out_specs=[pl.BlockSpec(memory_space=pltpu.VMEM)] * 4,
        out_shape=[jax.ShapeDtypeStruct((2, HALF, HEAD), jnp.bfloat16)] * 4,
        scratch_shapes=[pltpu.SemaphoreType.DMA((4, 2))],
        cost_estimate=pl.CostEstimate(flops=0, bytes_accessed=2**10, transcendentals=0),
        compiler_params=pltpu.CompilerParams(vmem_limit_bytes=VMEM // 2),
        name="ship",
    )(table, *sources)


def attention_kernel(table, queries, *refs, first, limit):
    final = limit is None
    sources, refs = refs[: 12 if final else 4], refs[12 if final else 4 :]
    if first:
        before, refs = refs[0], refs[1:]
    out, stacked, peak, total, key_buffer, value_buffer, units, starts, touched, sems = refs
    x, y, core = table[0, 9], table[0, 10], table[0, 11]
    lane = lax.broadcasted_iota(jnp.int32, (ROWS, 128), 1)

    def copies(unit, slot):
        code = (units[unit] // 2) % 8
        head = units[unit] // 16
        result = []
        rows = pl.ds(pl.multiple_of((code % 2) * BLOCK, BLOCK), BLOCK)
        cols = pl.ds(pl.multiple_of(head * HEAD, HEAD), HEAD)
        for near in range(2):
            keys, values = sources[2 * near], sources[2 * near + 1]
            group = [
                pltpu.make_async_copy(keys.at[rows, cols], key_buffer.at[slot], sems.at[0, slot]),
                pltpu.make_async_copy(values.at[rows, cols], value_buffer.at[slot], sems.at[1, slot]),
            ]
            result.append((code // 2 == near, group))
        for d in range(4 if final else 0):
            group = []
            for part, buffer in ((0, key_buffer), (1, value_buffer)):
                for half, source in ((core, sources[4 + 2 * d]), (1 - core, sources[5 + 2 * d])):
                    rows = pl.ds(pl.multiple_of(half * HALF, HALF), HALF)
                    sem = sems.at[len(group), slot]
                    group.append(pltpu.make_async_copy(source.at[part], buffer.at[slot, rows], sem))
            result.append((code == 4 + d, group))
        return result

    def start(unit, slot):
        for inside, group in copies(unit, slot):

            @pl.when(inside)
            def _():
                for copy in group:
                    copy.start()

    def wait(unit, slot):
        for inside, group in copies(unit, slot):

            @pl.when(inside)
            def _():
                for copy in group:
                    copy.wait()

    def list_units(t, carry):
        count, seen = carry
        starts[t] = count
        head, q = t // 4, t % 4
        seen_before = seen
        for code in range(8 if final else 4):
            if code < 4:
                own = (core if code < 2 else 1 - core) * 2 + code % 2
                wanted = (table[0, 0] >> (8 * q + 4 * head + own)) & 1
                block = (x * 4 + y) * 4 + own
                ours = seen >= first
                if not final:
                    ours = jnp.logical_and(ours, seen < limit)
                seen = seen + wanted
                wanted = jnp.where(ours, wanted, 0)
            else:
                dx, dy = DIRECTIONS[code - 4]
                giver = ((x - dx + 4) % 4) * 4 + (y - dy + 4) % 4
                entry = table[0, 1 + code]
                item = entry // 16
                wanted = jnp.where(item // 4 == head, (entry >> q) & 1, 0)
                block = giver * 4 + item % 4
            at = count

            @pl.when(wanted != 0)
            def _():
                units[at] = 16 * head + 2 * code + (block == 63).astype(jnp.int32)

            count = count + wanted
        touched[t] = (jnp.minimum(seen, first) > seen_before).astype(jnp.int32)
        return count, seen

    starts[8] = lax.fori_loop(0, 8, list_units, (0, 0))[0]

    @pl.when(starts[8] > 0)
    def _():
        start(0, 0)

    def columns(task, h):
        return pl.ds(pl.multiple_of((task // 4) * WIDE + h * HEAD, HEAD), HEAD)

    def load(task):
        tokens = pl.ds(pl.multiple_of((task % 4) * ROWS, ROWS), ROWS)
        for h in range(GROUP):
            stacked[h * ROWS : (h + 1) * ROWS, :] = queries[tokens, columns(task, h)]

        @pl.when(touched[task] == 0)
        def _():
            peak[...] = jnp.full(peak.shape, NEG, jnp.float32)
            total[...] = jnp.zeros(total.shape, jnp.float32)

        if first:

            @pl.when(touched[task] != 0)
            def _():
                total[:, HEAD:] = jnp.ones((GROUP * ROWS, HEAD), jnp.float32)
                for h in range(GROUP):
                    rows = slice(h * ROWS, (h + 1) * ROWS)
                    level = before[task, :, WIDE + 4 * h : WIDE + 4 * h + 1]
                    peak[rows, :] = jnp.broadcast_to(level, (ROWS, HEAD))
                    total[rows, :HEAD] = before[task, :, h * HEAD : (h + 1) * HEAD]

    def attend(task, slot, masked):
        steps = [(k, r) for k in range(0, BLOCK, SPAN) for r in range(0, GROUP * ROWS, TILE)]

        def score(k, r):
            keys = key_buffer[slot, k : k + SPAN, :]
            return lax.dot_general(
                stacked[r : r + TILE, :], keys, NT, preferred_element_type=jnp.float32
            )

        s = score(*steps[0])
        for i, (k, r) in enumerate(steps):
            after = score(*steps[i + 1]) if i + 1 < len(steps) else None
            if masked and k + SPAN == BLOCK:
                row = lax.broadcasted_iota(jnp.int32, (TILE, 1024), 0) % ROWS
                token = (task % 4) * 256 + (row // CHUNK) * 64 + core * CHUNK + row % CHUNK
                col = lax.broadcasted_iota(jnp.int32, (TILE, 1024), 1)
                tail = jnp.where(col <= token, s[:, SPAN - 1024 :], NEG)
                s = jnp.concatenate([s[:, : SPAN - 1024], tail], axis=1)
            rows = slice(r, r + TILE)
            old = peak[rows, :]
            new = jnp.maximum(old, jnp.max(s, axis=1, keepdims=True) * SCALE)
            factor = jnp.exp2(old - new)
            weights = jnp.exp2(s * SCALE - new[:, :1]).astype(jnp.bfloat16)
            peak[rows, :] = new
            values = jnp.concatenate(
                [value_buffer[slot, k : k + SPAN, :], jnp.ones((SPAN, HEAD), jnp.bfloat16)], axis=1
            )
            total[rows, :] = total[rows, :] * jnp.concatenate([factor, factor], axis=1) + jnp.dot(
                weights, values, preferred_element_type=jnp.float32
            )
            s = after

    def visit(unit, task):
        slot = unit % 2
        wait(unit, slot)

        @pl.when(unit + 1 < starts[8])
        def _():
            start(unit + 1, 1 - slot)

        masked = units[unit] % 2

        @pl.when(masked != 0)
        def _():
            attend(task, slot, True)

        @pl.when(masked == 0)
        def _():
            attend(task, slot, False)

        return task

    def prepare():
        for h in range(GROUP):
            stacked[h * ROWS : (h + 1) * ROWS, :] = queries[:, h * HEAD : (h + 1) * HEAD]
        if handed:
            for h in range(GROUP):
                rows = slice(h * ROWS, (h + 1) * ROWS)
                level = before[0, :, WIDE + 4 * h : WIDE + 4 * h + 1]
                peak[rows, :] = jnp.broadcast_to(level, (ROWS, HEAD))
                total[rows, :HEAD] = before[0, :, h * HEAD : (h + 1) * HEAD]
                total[rows, HEAD:] = jnp.broadcast_to(
                    jnp.where(level > 0.5 * NEG, 1.0, 0.0), (ROWS, HEAD)
                )
        else:
            peak[...] = jnp.full(peak.shape, NEG, jnp.float32)
            total[...] = jnp.zeros(total.shape, jnp.float32)

    def write(task, h, value):
        if final:
            out[task % 4, :, columns(task, h)] = value.astype(jnp.bfloat16)
        else:
            out[task, :, h * HEAD : (h + 1) * HEAD] = value

    def write_levels(task, levels):
        if not final:
            out[task, :, WIDE:] = levels
            return
        q = task % 4
        packed = pack_stats(levels, lane)
        kept = out[q, :, 2 * WIDE :].astype(jnp.float32)
        kept = jnp.where(jnp.logical_and(task >= 4, lane < 32), kept, packed.astype(jnp.float32))
        out[q, :, 2 * WIDE :] = kept.astype(jnp.bfloat16)

    def one_task(task, carry):
        some = starts[task] < starts[task + 1]

        @pl.when(some)
        def _():
            load(task)
            lax.fori_loop(starts[task], starts[task + 1], visit, task)
            levels = jnp.full((ROWS, 128), NEG, jnp.float32)
            for h in range(GROUP):
                rows = slice(h * ROWS, (h + 1) * ROWS)
                mass = total[rows, HEAD:]
                write(task, h, total[rows, :HEAD] / mass)
                levels = jnp.where((lane % 32) // 4 == h, peak[rows, :] + jnp.log2(mass), levels)
            write_levels(task, levels)

        if first:

            @pl.when(jnp.logical_and(jnp.logical_not(some), touched[task] != 0))
            def _():
                for h in range(GROUP):
                    write(task, h, before[task, :, h * HEAD : (h + 1) * HEAD])
                write_levels(task, before[task, :, WIDE:])

        if final:

            @pl.when(jnp.logical_and(jnp.logical_not(some), touched[task] == 0))
            def _():
                for h in range(GROUP):
                    write(task, h, jnp.zeros((ROWS, HEAD), jnp.float32))
                write_levels(task, jnp.full((ROWS, 128), NEG, jnp.float32))

        return carry

    lax.fori_loop(0, 8, one_task, 0)


def pack_stats(level, lane):
    high = level.astype(jnp.bfloat16)
    rest = level - high.astype(jnp.float32)
    middle = rest.astype(jnp.bfloat16)
    low = (rest - middle.astype(jnp.float32)).astype(jnp.bfloat16)
    part = lane % 4
    terms = jnp.where(
        part == 0,
        high.astype(jnp.float32),
        jnp.where(part == 1, middle.astype(jnp.float32), low.astype(jnp.float32)),
    )
    return terms.astype(jnp.bfloat16)


def attention(table, queries, sources, first, limit, before=()):
    smem = pl.BlockSpec(memory_space=pltpu.SMEM)
    vmem = pl.BlockSpec(memory_space=pltpu.VMEM)
    hbm = pl.BlockSpec(memory_space=pl.ANY)
    if limit is None:
        shape = jax.ShapeDtypeStruct((4, ROWS, BOTH), jnp.bfloat16)
    else:
        shape = jax.ShapeDtypeStruct((8, ROWS, PACK), jnp.float32)
    return pl.pallas_call(
        functools.partial(attention_kernel, first=first, limit=limit),
        in_specs=[smem, vmem] + [hbm] * len(sources) + [vmem] * len(before),
        out_specs=vmem,
        out_shape=shape,
        scratch_shapes=[
            pltpu.VMEM((GROUP * ROWS, HEAD), jnp.bfloat16),
            pltpu.VMEM((GROUP * ROWS, HEAD), jnp.float32),
            pltpu.VMEM((GROUP * ROWS, 2 * HEAD), jnp.float32),
            pltpu.VMEM((2, BLOCK, HEAD), jnp.bfloat16),
            pltpu.VMEM((2, BLOCK, HEAD), jnp.bfloat16),
            pltpu.SMEM((65,), jnp.int32),
            pltpu.SMEM((9,), jnp.int32),
            pltpu.SMEM((8,), jnp.int32),
            pltpu.SemaphoreType.DMA((4, 2)),
        ],
        compiler_params=pltpu.CompilerParams(vmem_limit_bytes=ROOM),
        cost_estimate=pl.CostEstimate(flops=2 * 10**10, bytes_accessed=2**25, transcendentals=0),
        name="handed" if limit is None else "own",
    )(table, queries, *sources, *before)


def finish_kernel(parts, out):
    level = parts[:, :, 2 * WIDE :].astype(jnp.float32)
    level = level + pltpu.roll(level, 127, 2) + pltpu.roll(level, 126, 2)
    share = jnp.exp2(level - jnp.max(level, axis=0, keepdims=True))
    share = share / jnp.sum(share, axis=0, keepdims=True)
    for h in range(2 * GROUP):
        columns = slice(h * HEAD, (h + 1) * HEAD)
        joined = jnp.zeros((CHUNK, HEAD), jnp.float32)
        for i in range(16):
            part = parts[i, :, columns].astype(jnp.float32)
            joined = joined + share[i, :, 4 * h : 4 * h + 1] * part
        out[:, columns] = joined.astype(jnp.bfloat16)


def finish(partial):
    parts = lax.all_to_all(
        partial.reshape(16, CHUNK, BOTH), ("x", "y"), split_axis=0, concat_axis=0, tiled=True
    )
    return pl.pallas_call(
        finish_kernel,
        out_shape=jax.ShapeDtypeStruct((CHUNK, 2 * WIDE), jnp.bfloat16),
        compiler_params=pltpu.CompilerParams(vmem_limit_bytes=VMEM),
        name="finish",
    )(parts)


def gather(queries):
    columns = queries.reshape(8, 4, 2 * WIDE).transpose(1, 0, 2)
    sent = jnp.broadcast_to(columns[None], (16, 4, 8, 2 * WIDE)).reshape(64, 8, 2 * WIDE)
    got = lax.all_to_all(sent, ("x", "y", "head"), split_axis=0, concat_axis=0, tiled=True)
    return got.reshape(4 * ROWS, 2 * WIDE)


def shards(queries, keys, values, gates):
    gathered = gather(queries)
    table = plan(gates)
    sources = [in_hbm(a) for a in (keys, values, other_core(keys), other_core(values))]

    slots = []
    for d, half in enumerate(ship(table, sources)):
        got = hand_on(half, d)
        slots += [got, other_core(got)]

    partial = attention(table, gathered, sources, 0, EARLY)
    partial = attention(table, gathered, sources, EARLY, LATER, [partial])
    return finish(attention(table, gathered, sources + slots, LATER, None, [partial]))


def solution(mesh):
    parts = jax.sharding.Mesh(mesh.devices.reshape(4, 4, 2, 4), ("x", "y", "core", "head"))
    seq = ("x", "y", "core")
    placed = (P((*seq, "head"), None), P(seq, "head"), P(seq, "head"), P())
    return jax.shard_map(
        shards, mesh=parts, in_specs=placed, out_specs=P(seq, "head"), check_vma=False
    )
```

```python
import functools

import jax
import jax.numpy as jnp
from jax import lax
from jax.experimental import pallas as pl
from jax.experimental.pallas import tpu as pltpu
from jax.sharding import PartitionSpec as P

HEAD = 128
BLOCK = 4096
GROUP = 8
WIDE = GROUP * HEAD
PACK = WIDE + 128
BOTH = 2 * WIDE + 128
CHUNK = 32
ROWS = 4 * CHUNK
SCALE = 128**-0.5 * 1.4426950408889634
NEG = -1e30
NT = (((1,), (1,)), ((), ()))
VMEM = 127 * 2**19
ROOM = 36 * 2**20
EARLY, ALL = 3, 64
HALF = BLOCK // 2
SPAN = 2048
TILE = 512
ARRIVAL = 4
DIRECTIONS = ((1, 0), (-1, 0), (0, 1), (0, -1))


def other_core(array):
    return lax.ppermute(array, "core", [(0, 1), (1, 0)])


def in_hbm(array):
    return pltpu.with_memory_space_constraint(array, pltpu.HBM)


def hand_on(array, direction):
    dx, dy = DIRECTIONS[direction]
    axis, step = ("x", dx) if dx else ("y", dy)
    return lax.ppermute(array, axis, [(i, (i + step) % 4) for i in range(4)])


def plan_kernel(gates, table):
    lane = lax.broadcasted_iota(jnp.int32, (8, 128), 1)
    item = lax.broadcasted_iota(jnp.int32, (8, 128), 0)
    variant = lane // 16
    chip = lane % 16
    x, y = chip // 4, chip % 4
    block = chip * 4 + item % 4
    here_x, here_y, core = (lax.axis_index(name) for name in ("x", "y", "core"))
    first = lax.axis_index("head") * 2
    kept = []
    for q in range(4):
        hit = jnp.zeros((8, 128), jnp.int32)
        for k in range(12):
            chosen = jnp.where(item < 4, gates[q, first, k], gates[q, first + 1, k])
            hit = jnp.where(chosen == block, 1, hit)
        kept.append(hit)

    def ahead(value, direction):
        forward = jnp.where(x < 3, pltpu.roll(value, 124, 1), pltpu.roll(value, 12, 1))
        back = jnp.where(x > 0, pltpu.roll(value, 4, 1), pltpu.roll(value, 116, 1))
        up = jnp.where(y < 3, pltpu.roll(value, 127, 1), pltpu.roll(value, 3, 1))
        down = jnp.where(y > 0, pltpu.roll(value, 1, 1), pltpu.roll(value, 125, 1))
        along_x = jnp.where(direction == 0, forward, back)
        return jnp.where(direction < 2, along_x, jnp.where(direction == 2, up, down))

    def over_items(value, how):
        for step in (4, 2, 1):
            value = how(value, pltpu.roll(value, step, 0))
        return value

    own = over_items(kept[0] + kept[1] + kept[2] + kept[3], jnp.add)
    handed = jnp.zeros((8, 128), jnp.int32)
    given = [jnp.zeros((8, 128), jnp.int32)] * 4
    got = [jnp.zeros((8, 128), jnp.int32)] * 4
    for orders in zip((0, 1, 2, 3), (2, 3, 0, 1), (0, 2, 1, 3), (3, 1, 2, 0)):
        direction = jnp.zeros((8, 128), jnp.int32)
        for i, d in enumerate(orders):
            direction = jnp.where(variant // 2 == i, d, direction)
        ready = jnp.maximum(own, ARRIVAL) + handed
        done = jnp.where(handed > 0, ready, own)
        want = jnp.maximum(done - ahead(ready, direction) + variant % 2, 0) >> 1
        left = kept[0] + kept[1] + kept[2] + kept[3]
        moved = jnp.minimum(left, want)
        score = moved * 256 - left * 16 + item
        chosen = jnp.logical_and(score == over_items(score, jnp.maximum), moved > 0)
        moved = jnp.where(chosen, moved, 0)
        entry = jnp.where(chosen, item * 16, 0)
        taken = jnp.zeros((8, 128), jnp.int32)
        for q in range(4):
            goes = jnp.where(taken < moved, kept[q], 0)
            taken = taken + goes
            kept[q] = kept[q] - goes
            entry = entry + goes * (1 << q)
        moved = over_items(moved, jnp.add)
        entry = over_items(entry, jnp.add)
        gets = ahead(entry, direction ^ 1)
        for d in range(4):
            given[d] = jnp.where(direction == d, entry, given[d])
            got[d] = jnp.where(direction == d, gets, got[d])
        own = own - moved
        handed = handed + ahead(moved, direction ^ 1)
    worst = jnp.where(handed > 0, jnp.maximum(own, ARRIVAL) + handed, own)
    for step in (8, 4, 2, 1):
        around = jnp.where(chip + step < 16, pltpu.roll(worst, 128 - step, 1), pltpu.roll(worst, 16 - step, 1))
        worst = jnp.maximum(worst, around)
    best = jnp.min((worst * 8 + variant).astype(jnp.float32)).astype(jnp.int32) % 8
    here = best * 16 + here_x * 4 + here_y
    keeps = jnp.zeros((8, 128), jnp.int32)
    for q in range(4):
        keeps = keeps + (kept[q] << (8 * q + item))
    row = jnp.zeros((8, 128), jnp.int32)
    for i, value in enumerate([over_items(keeps, jnp.add)] + given + got):
        row = jnp.where(lane == i, pltpu.roll(value, (i + 128 - here) % 128, 1), row)
    for i, value in enumerate((here_x, here_y, core)):
        row = jnp.where(lane == 9 + i, value, row)
    table[...] = row


def plan(gates):
    return pl.pallas_call(
        plan_kernel,
        in_specs=[pl.BlockSpec(memory_space=pltpu.SMEM)],
        out_shape=jax.ShapeDtypeStruct((8, 128), jnp.int32),
        compiler_params=pltpu.CompilerParams(vmem_limit_bytes=VMEM),
        name="plan",
    )(gates)


def ship_kernel(table, keys, values, near_keys, near_values, *refs):
    outs, sems = refs[:4], refs[4]
    core = table[0, 11]
    for phase in range(2):
        for d in range(4):
            item = table[0, 1 + d] // 16
            block = item % 4
            rows = pl.ds(pl.multiple_of((block % 2) * BLOCK + core * HALF, HALF), HALF)
            cols = pl.ds(pl.multiple_of((item // 4) * HEAD, HEAD), HEAD)
            own = block // 2 == core
            for near, pair in ((False, (keys, values)), (True, (near_keys, near_values))):

                @pl.when(own != near)
                def _():
                    for part in range(2):
                        copy = pltpu.make_async_copy(
                            pair[part].at[rows, cols], outs[d].at[part], sems.at[d, part]
                        )
                        if phase == 0:
                            copy.start()
                        else:
                            copy.wait()


def ship(table, sources):
    hbm = pl.BlockSpec(memory_space=pl.ANY)
    return pl.pallas_call(
        ship_kernel,
        in_specs=[pl.BlockSpec(memory_space=pltpu.SMEM)] + [hbm] * 4,
        out_specs=[pl.BlockSpec(memory_space=pltpu.VMEM)] * 4,
        out_shape=[jax.ShapeDtypeStruct((2, HALF, HEAD), jnp.bfloat16)] * 4,
        scratch_shapes=[pltpu.SemaphoreType.DMA((4, 2))],
        cost_estimate=pl.CostEstimate(flops=0, bytes_accessed=2**10, transcendentals=0),
        compiler_params=pltpu.CompilerParams(vmem_limit_bytes=VMEM // 2),
        name="ship",
    )(table, *sources)


def attention_kernel(table, queries, *refs, first, limit):
    final = limit is None
    sources, refs = refs[: 8 if final else 4], refs[8 if final else 4 :]
    if first:
        before, refs = refs[0], refs[1:]
    out, stacked, peak, total, key_buffer, value_buffer, units, starts, touched, sems = refs
    x, y, core = table[0, 9], table[0, 10], table[0, 11]
    lane = lax.broadcasted_iota(jnp.int32, (ROWS, 128), 1)

    def copies(unit, slot):
        code = (units[unit] // 2) % 8
        head = units[unit] // 16
        result = []
        rows = pl.ds(pl.multiple_of((code % 2) * BLOCK, BLOCK), BLOCK)
        cols = pl.ds(pl.multiple_of(head * HEAD, HEAD), HEAD)
        for near in range(0 if final else 2):
            keys, values = sources[2 * near], sources[2 * near + 1]
            group = [
                pltpu.make_async_copy(keys.at[rows, cols], key_buffer.at[slot], sems.at[0, slot]),
                pltpu.make_async_copy(values.at[rows, cols], value_buffer.at[slot], sems.at[1, slot]),
            ]
            result.append((code // 2 == near, group))
        for d in range(4 if final else 0):
            group = []
            for part, buffer in ((0, key_buffer), (1, value_buffer)):
                for half, source in ((core, sources[2 * d]), (1 - core, sources[2 * d + 1])):
                    rows = pl.ds(pl.multiple_of(half * HALF, HALF), HALF)
                    sem = sems.at[len(group), slot]
                    group.append(pltpu.make_async_copy(source.at[part], buffer.at[slot, rows], sem))
            result.append((code == 4 + d, group))
        return result

    def start(unit, slot):
        for inside, group in copies(unit, slot):

            @pl.when(inside)
            def _():
                for copy in group:
                    copy.start()

    def wait(unit, slot):
        for inside, group in copies(unit, slot):

            @pl.when(inside)
            def _():
                for copy in group:
                    copy.wait()

    def list_units(t, carry):
        count, seen = carry
        starts[t] = count
        head, q = t // 4, t % 4
        seen_before = seen
        for code in range(4, 8) if final else range(4):
            if not final:
                own = (core if code < 2 else 1 - core) * 2 + code % 2
                wanted = (table[0, 0] >> (8 * q + 4 * head + own)) & 1
                block = (x * 4 + y) * 4 + own
                ours = jnp.logical_and(seen >= first, seen < limit)
                seen = seen + wanted
                wanted = jnp.where(ours, wanted, 0)
            else:
                dx, dy = DIRECTIONS[code - 4]
                giver = ((x - dx + 4) % 4) * 4 + (y - dy + 4) % 4
                entry = table[0, 1 + code]
                item = entry // 16
                wanted = jnp.where(item // 4 == head, (entry >> q) & 1, 0)
                block = giver * 4 + item % 4
            at = count

            @pl.when(wanted != 0)
            def _():
                units[at] = 16 * head + 2 * code + (block == 63).astype(jnp.int32)

            count = count + wanted
        if final:
            touched[t] = (table[0, 0] >> (8 * q + 4 * head)) & 15
        else:
            touched[t] = (jnp.minimum(seen, first) > seen_before).astype(jnp.int32)
        return count, seen

    starts[8] = lax.fori_loop(0, 8, list_units, (0, 0))[0]

    @pl.when(starts[8] > 0)
    def _():
        start(0, 0)

    def columns(task, h):
        return pl.ds(pl.multiple_of((task // 4) * WIDE + h * HEAD, HEAD), HEAD)

    def load(task):
        tokens = pl.ds(pl.multiple_of((task % 4) * ROWS, ROWS), ROWS)
        for h in range(GROUP):
            stacked[h * ROWS : (h + 1) * ROWS, :] = queries[tokens, columns(task, h)]

        @pl.when(touched[task] == 0)
        def _():
            peak[...] = jnp.full(peak.shape, NEG, jnp.float32)
            total[...] = jnp.zeros(total.shape, jnp.float32)

        if first:

            @pl.when(touched[task] != 0)
            def _():
                total[:, HEAD:] = jnp.ones((GROUP * ROWS, HEAD), jnp.float32)
                for h in range(GROUP):
                    rows = slice(h * ROWS, (h + 1) * ROWS)
                    level = before[task, :, WIDE + 4 * h : WIDE + 4 * h + 1]
                    peak[rows, :] = jnp.broadcast_to(level, (ROWS, HEAD))
                    total[rows, :HEAD] = before[task, :, h * HEAD : (h + 1) * HEAD]

    def attend(task, slot, masked):
        steps = [(k, r) for k in range(0, BLOCK, SPAN) for r in range(0, GROUP * ROWS, TILE)]

        def score(k, r):
            keys = key_buffer[slot, k : k + SPAN, :]
            return lax.dot_general(
                stacked[r : r + TILE, :], keys, NT, preferred_element_type=jnp.float32
            )

        s = score(*steps[0])
        for i, (k, r) in enumerate(steps):
            after = score(*steps[i + 1]) if i + 1 < len(steps) else None
            if masked and k + SPAN == BLOCK:
                row = lax.broadcasted_iota(jnp.int32, (TILE, 1024), 0) % ROWS
                token = (task % 4) * 256 + (row // CHUNK) * 64 + core * CHUNK + row % CHUNK
                col = lax.broadcasted_iota(jnp.int32, (TILE, 1024), 1)
                tail = jnp.where(col <= token, s[:, SPAN - 1024 :], NEG)
                s = jnp.concatenate([s[:, : SPAN - 1024], tail], axis=1)
            rows = slice(r, r + TILE)
            old = peak[rows, :]
            new = jnp.maximum(old, jnp.max(s, axis=1, keepdims=True) * SCALE)
            factor = jnp.exp2(old - new)
            weights = jnp.exp2(s * SCALE - new[:, :1]).astype(jnp.bfloat16)
            peak[rows, :] = new
            values = jnp.concatenate(
                [value_buffer[slot, k : k + SPAN, :], jnp.ones((SPAN, HEAD), jnp.bfloat16)], axis=1
            )
            total[rows, :] = total[rows, :] * jnp.concatenate([factor, factor], axis=1) + jnp.dot(
                weights, values, preferred_element_type=jnp.float32
            )
            s = after

    def visit(unit, task):
        slot = unit % 2
        wait(unit, slot)

        @pl.when(unit + 1 < starts[8])
        def _():
            start(unit + 1, 1 - slot)

        masked = units[unit] % 2

        @pl.when(masked != 0)
        def _():
            attend(task, slot, True)

        @pl.when(masked == 0)
        def _():
            attend(task, slot, False)

        return task

    def prepare():
        for h in range(GROUP):
            stacked[h * ROWS : (h + 1) * ROWS, :] = queries[:, h * HEAD : (h + 1) * HEAD]
        if handed:
            for h in range(GROUP):
                rows = slice(h * ROWS, (h + 1) * ROWS)
                level = before[0, :, WIDE + 4 * h : WIDE + 4 * h + 1]
                peak[rows, :] = jnp.broadcast_to(level, (ROWS, HEAD))
                total[rows, :HEAD] = before[0, :, h * HEAD : (h + 1) * HEAD]
                total[rows, HEAD:] = jnp.broadcast_to(
                    jnp.where(level > 0.5 * NEG, 1.0, 0.0), (ROWS, HEAD)
                )
        else:
            peak[...] = jnp.full(peak.shape, NEG, jnp.float32)
            total[...] = jnp.zeros(total.shape, jnp.float32)

    def write(task, h, value):
        if final:
            out[task % 4, :, columns(task, h)] = value.astype(jnp.bfloat16)
        else:
            out[task, :, h * HEAD : (h + 1) * HEAD] = value

    def write_levels(task, levels):
        if not final:
            out[task, :, WIDE:] = levels
            return
        q = task % 4
        packed = pack_stats(levels, lane)
        kept = out[q, :, 2 * WIDE :].astype(jnp.float32)
        kept = jnp.where(jnp.logical_and(task >= 4, lane < 32), kept, packed.astype(jnp.float32))
        out[q, :, 2 * WIDE :] = kept.astype(jnp.bfloat16)

    def one_task(task, carry):
        some = starts[task] < starts[task + 1]

        @pl.when(some)
        def _():
            load(task)
            lax.fori_loop(starts[task], starts[task + 1], visit, task)
            levels = jnp.full((ROWS, 128), NEG, jnp.float32)
            for h in range(GROUP):
                rows = slice(h * ROWS, (h + 1) * ROWS)
                mass = total[rows, HEAD:]
                write(task, h, total[rows, :HEAD] / mass)
                levels = jnp.where((lane % 32) // 4 == h, peak[rows, :] + jnp.log2(mass), levels)
            write_levels(task, levels)

        if first:

            @pl.when(jnp.logical_and(jnp.logical_not(some), touched[task] != 0))
            def _():
                for h in range(GROUP):
                    write(task, h, before[task, :, h * HEAD : (h + 1) * HEAD])
                write_levels(task, before[task, :, WIDE:])

        if final:

            @pl.when(jnp.logical_and(jnp.logical_not(some), touched[task] == 0))
            def _():
                for h in range(GROUP):
                    write(task, h, jnp.zeros((ROWS, HEAD), jnp.float32))
                write_levels(task, jnp.full((ROWS, 128), NEG, jnp.float32))

        return carry

    lax.fori_loop(0, 8, one_task, 0)


def pack_stats(level, lane):
    high = level.astype(jnp.bfloat16)
    rest = level - high.astype(jnp.float32)
    middle = rest.astype(jnp.bfloat16)
    low = (rest - middle.astype(jnp.float32)).astype(jnp.bfloat16)
    part = lane % 4
    terms = jnp.where(
        part == 0,
        high.astype(jnp.float32),
        jnp.where(part == 1, middle.astype(jnp.float32), low.astype(jnp.float32)),
    )
    return terms.astype(jnp.bfloat16)


def attention(table, queries, sources, first, limit, before=()):
    smem = pl.BlockSpec(memory_space=pltpu.SMEM)
    vmem = pl.BlockSpec(memory_space=pltpu.VMEM)
    hbm = pl.BlockSpec(memory_space=pl.ANY)
    if limit is None:
        shape = jax.ShapeDtypeStruct((4, ROWS, BOTH), jnp.bfloat16)
    else:
        shape = jax.ShapeDtypeStruct((8, ROWS, PACK), jnp.float32)
    return pl.pallas_call(
        functools.partial(attention_kernel, first=first, limit=limit),
        in_specs=[smem, vmem] + [hbm] * len(sources) + [vmem] * len(before),
        out_specs=vmem,
        out_shape=shape,
        scratch_shapes=[
            pltpu.VMEM((GROUP * ROWS, HEAD), jnp.bfloat16),
            pltpu.VMEM((GROUP * ROWS, HEAD), jnp.float32),
            pltpu.VMEM((GROUP * ROWS, 2 * HEAD), jnp.float32),
            pltpu.VMEM((2, BLOCK, HEAD), jnp.bfloat16),
            pltpu.VMEM((2, BLOCK, HEAD), jnp.bfloat16),
            pltpu.SMEM((65,), jnp.int32),
            pltpu.SMEM((9,), jnp.int32),
            pltpu.SMEM((8,), jnp.int32),
            pltpu.SemaphoreType.DMA((4, 2)),
        ],
        compiler_params=pltpu.CompilerParams(vmem_limit_bytes=ROOM),
        cost_estimate=pl.CostEstimate(flops=2 * 10**10, bytes_accessed=2**25, transcendentals=0),
        name="handed" if limit is None else "own",
    )(table, queries, *sources, *before)


def finish_kernel(parts, out):
    level = parts[:, :, 2 * WIDE :].astype(jnp.float32)
    level = level + pltpu.roll(level, 127, 2) + pltpu.roll(level, 126, 2)
    share = jnp.exp2(level - jnp.max(level, axis=0, keepdims=True))
    share = share / jnp.sum(share, axis=0, keepdims=True)
    for h in range(2 * GROUP):
        columns = slice(h * HEAD, (h + 1) * HEAD)
        joined = jnp.zeros((CHUNK, HEAD), jnp.float32)
        for i in range(16):
            part = parts[i, :, columns].astype(jnp.float32)
            joined = joined + share[i, :, 4 * h : 4 * h + 1] * part
        out[:, columns] = joined.astype(jnp.bfloat16)


def finish(partial):
    parts = lax.all_to_all(
        partial.reshape(16, CHUNK, BOTH), ("x", "y"), split_axis=0, concat_axis=0, tiled=True
    )
    return pl.pallas_call(
        finish_kernel,
        out_shape=jax.ShapeDtypeStruct((CHUNK, 2 * WIDE), jnp.bfloat16),
        compiler_params=pltpu.CompilerParams(vmem_limit_bytes=VMEM),
        name="finish",
    )(parts)


def gather(queries):
    columns = queries.reshape(8, 4, 2 * WIDE).transpose(1, 0, 2)
    sent = jnp.broadcast_to(columns[None], (16, 4, 8, 2 * WIDE)).reshape(64, 8, 2 * WIDE)
    got = lax.all_to_all(sent, ("x", "y", "head"), split_axis=0, concat_axis=0, tiled=True)
    return got.reshape(4 * ROWS, 2 * WIDE)


def shards(queries, keys, values, gates):
    gathered = gather(queries)
    table = plan(gates)
    sources = [in_hbm(a) for a in (keys, values, other_core(keys), other_core(values))]

    slots = []
    for d, half in enumerate(ship(table, sources)):
        got = hand_on(half, d)
        slots += [got, other_core(got)]

    partial = attention(table, gathered, sources, 0, EARLY)
    partial = attention(table, gathered, sources, EARLY, ALL, [partial])
    return finish(attention(table, gathered, slots, ALL, None, [partial]))


def solution(mesh):
    parts = jax.sharding.Mesh(mesh.devices.reshape(4, 4, 2, 4), ("x", "y", "core", "head"))
    seq = ("x", "y", "core")
    placed = (P((*seq, "head"), None), P(seq, "head"), P(seq, "head"), P())
    return jax.shard_map(
        shards, mesh=parts, in_specs=placed, out_specs=P(seq, "head"), check_vma=False
    )
```

```python
import functools

import jax
import jax.numpy as jnp
from jax import lax
from jax.experimental import pallas as pl
from jax.experimental.pallas import tpu as pltpu
from jax.sharding import PartitionSpec as P

HEAD = 128
BLOCK = 4096
GROUP = 8
WIDE = GROUP * HEAD
PACK = WIDE + 128
BOTH = 2 * WIDE + 128
CHUNK = 32
ROWS = 4 * CHUNK
SCALE = 128**-0.5 * 1.4426950408889634
NEG = -1e30
NT = (((1,), (1,)), ((), ()))
VMEM = 127 * 2**19
ROOM = 36 * 2**20
EARLY, ALL = 4, 64
HALF = BLOCK // 2
SPAN = 2048
TILE = 512
ARRIVAL = 4
DIRECTIONS = ((1, 0), (-1, 0), (0, 1), (0, -1))


def other_core(array):
    return lax.ppermute(array, "core", [(0, 1), (1, 0)])


def in_hbm(array):
    return pltpu.with_memory_space_constraint(array, pltpu.HBM)


def hand_on(array, direction):
    dx, dy = DIRECTIONS[direction]
    axis, step = ("x", dx) if dx else ("y", dy)
    return lax.ppermute(array, axis, [(i, (i + step) % 4) for i in range(4)])


def plan_kernel(gates, table):
    lane = lax.broadcasted_iota(jnp.int32, (8, 128), 1)
    item = lax.broadcasted_iota(jnp.int32, (8, 128), 0)
    variant = lane // 16
    chip = lane % 16
    x, y = chip // 4, chip % 4
    block = chip * 4 + item % 4
    here_x, here_y, core = (lax.axis_index(name) for name in ("x", "y", "core"))
    first = lax.axis_index("head") * 2
    kept = []
    for q in range(4):
        hit = jnp.zeros((8, 128), jnp.int32)
        for k in range(12):
            chosen = jnp.where(item < 4, gates[q, first, k], gates[q, first + 1, k])
            hit = jnp.where(chosen == block, 1, hit)
        kept.append(hit)

    def ahead(value, direction):
        forward = jnp.where(x < 3, pltpu.roll(value, 124, 1), pltpu.roll(value, 12, 1))
        back = jnp.where(x > 0, pltpu.roll(value, 4, 1), pltpu.roll(value, 116, 1))
        up = jnp.where(y < 3, pltpu.roll(value, 127, 1), pltpu.roll(value, 3, 1))
        down = jnp.where(y > 0, pltpu.roll(value, 1, 1), pltpu.roll(value, 125, 1))
        along_x = jnp.where(direction == 0, forward, back)
        return jnp.where(direction < 2, along_x, jnp.where(direction == 2, up, down))

    def over_items(value, how):
        for step in (4, 2, 1):
            value = how(value, pltpu.roll(value, step, 0))
        return value

    own = over_items(kept[0] + kept[1] + kept[2] + kept[3], jnp.add)
    handed = jnp.zeros((8, 128), jnp.int32)
    given = [jnp.zeros((8, 128), jnp.int32)] * 4
    got = [jnp.zeros((8, 128), jnp.int32)] * 4
    for orders in zip((0, 1, 2, 3), (2, 3, 0, 1), (0, 2, 1, 3), (3, 1, 2, 0)):
        direction = jnp.zeros((8, 128), jnp.int32)
        for i, d in enumerate(orders):
            direction = jnp.where(variant // 2 == i, d, direction)
        ready = jnp.maximum(own, ARRIVAL) + handed
        done = jnp.where(handed > 0, ready, own)
        want = jnp.maximum(done - ahead(ready, direction) + variant % 2, 0) >> 1
        left = kept[0] + kept[1] + kept[2] + kept[3]
        moved = jnp.minimum(left, want)
        score = moved * 256 - left * 16 + item
        chosen = jnp.logical_and(score == over_items(score, jnp.maximum), moved > 0)
        moved = jnp.where(chosen, moved, 0)
        entry = jnp.where(chosen, item * 16, 0)
        taken = jnp.zeros((8, 128), jnp.int32)
        for q in range(4):
            goes = jnp.where(taken < moved, kept[q], 0)
            taken = taken + goes
            kept[q] = kept[q] - goes
            entry = entry + goes * (1 << q)
        moved = over_items(moved, jnp.add)
        entry = over_items(entry, jnp.add)
        gets = ahead(entry, direction ^ 1)
        for d in range(4):
            given[d] = jnp.where(direction == d, entry, given[d])
            got[d] = jnp.where(direction == d, gets, got[d])
        own = own - moved
        handed = handed + ahead(moved, direction ^ 1)
    worst = jnp.where(handed > 0, jnp.maximum(own, ARRIVAL) + handed, own)
    for step in (8, 4, 2, 1):
        around = jnp.where(chip + step < 16, pltpu.roll(worst, 128 - step, 1), pltpu.roll(worst, 16 - step, 1))
        worst = jnp.maximum(worst, around)
    best = jnp.min((worst * 8 + variant).astype(jnp.float32)).astype(jnp.int32) % 8
    here = best * 16 + here_x * 4 + here_y
    keeps = jnp.zeros((8, 128), jnp.int32)
    for q in range(4):
        keeps = keeps + (kept[q] << (8 * q + item))
    row = jnp.zeros((8, 128), jnp.int32)
    for i, value in enumerate([over_items(keeps, jnp.add)] + given + got):
        row = jnp.where(lane == i, pltpu.roll(value, (i + 128 - here) % 128, 1), row)
    for i, value in enumerate((here_x, here_y, core)):
        row = jnp.where(lane == 9 + i, value, row)
    table[...] = row


def plan(gates):
    return pl.pallas_call(
        plan_kernel,
        in_specs=[pl.BlockSpec(memory_space=pltpu.SMEM)],
        out_shape=jax.ShapeDtypeStruct((8, 128), jnp.int32),
        compiler_params=pltpu.CompilerParams(vmem_limit_bytes=VMEM),
        name="plan",
    )(gates)


def ship_kernel(table, keys, values, near_keys, near_values, *refs):
    outs, sems = refs[:4], refs[4]
    core = table[0, 11]
    for phase in range(2):
        for d in range(4):
            item = table[0, 1 + d] // 16
            block = item % 4
            rows = pl.ds(pl.multiple_of((block % 2) * BLOCK + core * HALF, HALF), HALF)
            cols = pl.ds(pl.multiple_of((item // 4) * HEAD, HEAD), HEAD)
            own = block // 2 == core
            for near, pair in ((False, (keys, values)), (True, (near_keys, near_values))):

                @pl.when(own != near)
                def _():
                    for part in range(2):
                        copy = pltpu.make_async_copy(
                            pair[part].at[rows, cols], outs[d].at[part], sems.at[d, part]
                        )
                        if phase == 0:
                            copy.start()
                        else:
                            copy.wait()


def ship(table, sources):
    hbm = pl.BlockSpec(memory_space=pl.ANY)
    return pl.pallas_call(
        ship_kernel,
        in_specs=[pl.BlockSpec(memory_space=pltpu.SMEM)] + [hbm] * 4,
        out_specs=[pl.BlockSpec(memory_space=pltpu.VMEM)] * 4,
        out_shape=[jax.ShapeDtypeStruct((2, HALF, HEAD), jnp.bfloat16)] * 4,
        scratch_shapes=[pltpu.SemaphoreType.DMA((4, 2))],
        cost_estimate=pl.CostEstimate(flops=0, bytes_accessed=2**10, transcendentals=0),
        compiler_params=pltpu.CompilerParams(vmem_limit_bytes=VMEM // 2),
        name="ship",
    )(table, *sources)


def attention_kernel(table, queries, *refs, first, limit):
    final = limit is None
    sources, refs = refs[: 8 if final else 4], refs[8 if final else 4 :]
    if first:
        before, refs = refs[0], refs[1:]
    out, stacked, peak, total, key_buffer, value_buffer, units, starts, touched, sems = refs
    x, y, core = table[0, 9], table[0, 10], table[0, 11]
    lane = lax.broadcasted_iota(jnp.int32, (ROWS, 128), 1)

    def copies(unit, slot):
        code = (units[unit] // 2) % 8
        head = units[unit] // 16
        result = []
        rows = pl.ds(pl.multiple_of((code % 2) * BLOCK, BLOCK), BLOCK)
        cols = pl.ds(pl.multiple_of(head * HEAD, HEAD), HEAD)
        for near in range(0 if final else 2):
            keys, values = sources[2 * near], sources[2 * near + 1]
            group = [
                pltpu.make_async_copy(keys.at[rows, cols], key_buffer.at[slot], sems.at[0, slot]),
                pltpu.make_async_copy(values.at[rows, cols], value_buffer.at[slot], sems.at[1, slot]),
            ]
            result.append((code // 2 == near, group))
        for d in range(4 if final else 0):
            group = []
            for part, buffer in ((0, key_buffer), (1, value_buffer)):
                for half, source in ((core, sources[2 * d]), (1 - core, sources[2 * d + 1])):
                    rows = pl.ds(pl.multiple_of(half * HALF, HALF), HALF)
                    sem = sems.at[len(group), slot]
                    group.append(pltpu.make_async_copy(source.at[part], buffer.at[slot, rows], sem))
            result.append((code == 4 + d, group))
        return result

    def start(unit, slot):
        for inside, group in copies(unit, slot):

            @pl.when(inside)
            def _():
                for copy in group:
                    copy.start()

    def wait(unit, slot):
        for inside, group in copies(unit, slot):

            @pl.when(inside)
            def _():
                for copy in group:
                    copy.wait()

    def list_units(t, carry):
        count, seen = carry
        starts[t] = count
        head, q = t // 4, t % 4
        seen_before = seen
        for code in range(4, 8) if final else range(4):
            if not final:
                own = (core if code < 2 else 1 - core) * 2 + code % 2
                wanted = (table[0, 0] >> (8 * q + 4 * head + own)) & 1
                block = (x * 4 + y) * 4 + own
                ours = jnp.logical_and(seen >= first, seen < limit)
                seen = seen + wanted
                wanted = jnp.where(ours, wanted, 0)
            else:
                dx, dy = DIRECTIONS[code - 4]
                giver = ((x - dx + 4) % 4) * 4 + (y - dy + 4) % 4
                entry = table[0, 1 + code]
                item = entry // 16
                wanted = jnp.where(item // 4 == head, (entry >> q) & 1, 0)
                block = giver * 4 + item % 4
            at = count

            @pl.when(wanted != 0)
            def _():
                units[at] = 16 * head + 2 * code + (block == 63).astype(jnp.int32)

            count = count + wanted
        if final:
            touched[t] = (table[0, 0] >> (8 * q + 4 * head)) & 15
        else:
            touched[t] = (jnp.minimum(seen, first) > seen_before).astype(jnp.int32)
        return count, seen

    starts[8] = lax.fori_loop(0, 8, list_units, (0, 0))[0]

    @pl.when(starts[8] > 0)
    def _():
        start(0, 0)

    def columns(task, h):
        return pl.ds(pl.multiple_of((task // 4) * WIDE + h * HEAD, HEAD), HEAD)

    def load(task):
        tokens = pl.ds(pl.multiple_of((task % 4) * ROWS, ROWS), ROWS)
        for h in range(GROUP):
            stacked[h * ROWS : (h + 1) * ROWS, :] = queries[tokens, columns(task, h)]

        @pl.when(touched[task] == 0)
        def _():
            peak[...] = jnp.full(peak.shape, NEG, jnp.float32)
            total[...] = jnp.zeros(total.shape, jnp.float32)

        if first:

            @pl.when(touched[task] != 0)
            def _():
                total[:, HEAD:] = jnp.ones((GROUP * ROWS, HEAD), jnp.float32)
                for h in range(GROUP):
                    rows = slice(h * ROWS, (h + 1) * ROWS)
                    level = before[task, :, WIDE + 4 * h : WIDE + 4 * h + 1]
                    peak[rows, :] = jnp.broadcast_to(level, (ROWS, HEAD))
                    total[rows, :HEAD] = before[task, :, h * HEAD : (h + 1) * HEAD]

    def attend(task, slot, masked):
        steps = [(k, r) for k in range(0, BLOCK, SPAN) for r in range(0, GROUP * ROWS, TILE)]

        def score(k, r):
            keys = key_buffer[slot, k : k + SPAN, :]
            return lax.dot_general(
                stacked[r : r + TILE, :], keys, NT, preferred_element_type=jnp.float32
            )

        s = score(*steps[0])
        for i, (k, r) in enumerate(steps):
            after = score(*steps[i + 1]) if i + 1 < len(steps) else None
            if masked and k + SPAN == BLOCK:
                row = lax.broadcasted_iota(jnp.int32, (TILE, 1024), 0) % ROWS
                token = (task % 4) * 256 + (row // CHUNK) * 64 + core * CHUNK + row % CHUNK
                col = lax.broadcasted_iota(jnp.int32, (TILE, 1024), 1)
                tail = jnp.where(col <= token, s[:, SPAN - 1024 :], NEG)
                s = jnp.concatenate([s[:, : SPAN - 1024], tail], axis=1)
            rows = slice(r, r + TILE)
            old = peak[rows, :]
            new = jnp.maximum(old, jnp.max(s, axis=1, keepdims=True) * SCALE)
            factor = jnp.exp2(old - new)
            weights = jnp.exp2(s * SCALE - new[:, :1]).astype(jnp.bfloat16)
            peak[rows, :] = new
            values = jnp.concatenate(
                [value_buffer[slot, k : k + SPAN, :], jnp.ones((SPAN, HEAD), jnp.bfloat16)], axis=1
            )
            total[rows, :] = total[rows, :] * jnp.concatenate([factor, factor], axis=1) + jnp.dot(
                weights, values, preferred_element_type=jnp.float32
            )
            s = after

    def visit(unit, task):
        slot = unit % 2
        wait(unit, slot)

        @pl.when(unit + 1 < starts[8])
        def _():
            start(unit + 1, 1 - slot)

        masked = units[unit] % 2

        @pl.when(masked != 0)
        def _():
            attend(task, slot, True)

        @pl.when(masked == 0)
        def _():
            attend(task, slot, False)

        return task

    def prepare():
        for h in range(GROUP):
            stacked[h * ROWS : (h + 1) * ROWS, :] = queries[:, h * HEAD : (h + 1) * HEAD]
        if handed:
            for h in range(GROUP):
                rows = slice(h * ROWS, (h + 1) * ROWS)
                level = before[0, :, WIDE + 4 * h : WIDE + 4 * h + 1]
                peak[rows, :] = jnp.broadcast_to(level, (ROWS, HEAD))
                total[rows, :HEAD] = before[0, :, h * HEAD : (h + 1) * HEAD]
                total[rows, HEAD:] = jnp.broadcast_to(
                    jnp.where(level > 0.5 * NEG, 1.0, 0.0), (ROWS, HEAD)
                )
        else:
            peak[...] = jnp.full(peak.shape, NEG, jnp.float32)
            total[...] = jnp.zeros(total.shape, jnp.float32)

    def write(task, h, value):
        if final:
            out[task % 4, :, columns(task, h)] = value.astype(jnp.bfloat16)
        else:
            out[task, :, h * HEAD : (h + 1) * HEAD] = value

    def write_levels(task, levels):
        if not final:
            out[task, :, WIDE:] = levels
            return
        q = task % 4
        packed = pack_stats(levels, lane)
        kept = out[q, :, 2 * WIDE :].astype(jnp.float32)
        kept = jnp.where(jnp.logical_and(task >= 4, lane < 32), kept, packed.astype(jnp.float32))
        out[q, :, 2 * WIDE :] = kept.astype(jnp.bfloat16)

    def one_task(task, carry):
        some = starts[task] < starts[task + 1]

        @pl.when(some)
        def _():
            load(task)
            lax.fori_loop(starts[task], starts[task + 1], visit, task)
            levels = jnp.full((ROWS, 128), NEG, jnp.float32)
            for h in range(GROUP):
                rows = slice(h * ROWS, (h + 1) * ROWS)
                mass = total[rows, HEAD:]
                write(task, h, total[rows, :HEAD] / mass)
                levels = jnp.where((lane % 32) // 4 == h, peak[rows, :] + jnp.log2(mass), levels)
            write_levels(task, levels)

        if first:

            @pl.when(jnp.logical_and(jnp.logical_not(some), touched[task] != 0))
            def _():
                for h in range(GROUP):
                    write(task, h, before[task, :, h * HEAD : (h + 1) * HEAD])
                write_levels(task, before[task, :, WIDE:])

        if final:

            @pl.when(jnp.logical_and(jnp.logical_not(some), touched[task] == 0))
            def _():
                for h in range(GROUP):
                    write(task, h, jnp.zeros((ROWS, HEAD), jnp.float32))
                write_levels(task, jnp.full((ROWS, 128), NEG, jnp.float32))

        return carry

    lax.fori_loop(0, 8, one_task, 0)


def pack_stats(level, lane):
    high = level.astype(jnp.bfloat16)
    rest = level - high.astype(jnp.float32)
    middle = rest.astype(jnp.bfloat16)
    low = (rest - middle.astype(jnp.float32)).astype(jnp.bfloat16)
    part = lane % 4
    terms = jnp.where(
        part == 0,
        high.astype(jnp.float32),
        jnp.where(part == 1, middle.astype(jnp.float32), low.astype(jnp.float32)),
    )
    return terms.astype(jnp.bfloat16)


def attention(table, queries, sources, first, limit, before=()):
    smem = pl.BlockSpec(memory_space=pltpu.SMEM)
    vmem = pl.BlockSpec(memory_space=pltpu.VMEM)
    hbm = pl.BlockSpec(memory_space=pl.ANY)
    if limit is None:
        shape = jax.ShapeDtypeStruct((4, ROWS, BOTH), jnp.bfloat16)
    else:
        shape = jax.ShapeDtypeStruct((8, ROWS, PACK), jnp.float32)
    return pl.pallas_call(
        functools.partial(attention_kernel, first=first, limit=limit),
        in_specs=[smem, vmem] + [hbm] * len(sources) + [vmem] * len(before),
        out_specs=vmem,
        out_shape=shape,
        scratch_shapes=[
            pltpu.VMEM((GROUP * ROWS, HEAD), jnp.bfloat16),
            pltpu.VMEM((GROUP * ROWS, HEAD), jnp.float32),
            pltpu.VMEM((GROUP * ROWS, 2 * HEAD), jnp.float32),
            pltpu.VMEM((2, BLOCK, HEAD), jnp.bfloat16),
            pltpu.VMEM((2, BLOCK, HEAD), jnp.bfloat16),
            pltpu.SMEM((65,), jnp.int32),
            pltpu.SMEM((9,), jnp.int32),
            pltpu.SMEM((8,), jnp.int32),
            pltpu.SemaphoreType.DMA((4, 2)),
        ],
        compiler_params=pltpu.CompilerParams(vmem_limit_bytes=ROOM),
        cost_estimate=pl.CostEstimate(flops=2 * 10**10, bytes_accessed=2**25, transcendentals=0),
        name="handed" if limit is None else "own",
    )(table, queries, *sources, *before)


def finish_kernel(parts, out):
    level = parts[:, :, 2 * WIDE :].astype(jnp.float32)
    level = level + pltpu.roll(level, 127, 2) + pltpu.roll(level, 126, 2)
    share = jnp.exp2(level - jnp.max(level, axis=0, keepdims=True))
    share = share / jnp.sum(share, axis=0, keepdims=True)
    for h in range(2 * GROUP):
        columns = slice(h * HEAD, (h + 1) * HEAD)
        joined = jnp.zeros((CHUNK, HEAD), jnp.float32)
        for i in range(16):
            part = parts[i, :, columns].astype(jnp.float32)
            joined = joined + share[i, :, 4 * h : 4 * h + 1] * part
        out[:, columns] = joined.astype(jnp.bfloat16)


def finish(partial):
    parts = lax.all_to_all(
        partial.reshape(16, CHUNK, BOTH), ("x", "y"), split_axis=0, concat_axis=0, tiled=True
    )
    return pl.pallas_call(
        finish_kernel,
        out_shape=jax.ShapeDtypeStruct((CHUNK, 2 * WIDE), jnp.bfloat16),
        compiler_params=pltpu.CompilerParams(vmem_limit_bytes=VMEM),
        name="finish",
    )(parts)


def gather(queries):
    columns = queries.reshape(8, 4, 2 * WIDE).transpose(1, 0, 2)
    sent = jnp.broadcast_to(columns[None], (16, 4, 8, 2 * WIDE)).reshape(64, 8, 2 * WIDE)
    got = lax.all_to_all(sent, ("x", "y", "head"), split_axis=0, concat_axis=0, tiled=True)
    return got.reshape(4 * ROWS, 2 * WIDE)


def shards(queries, keys, values, gates):
    gathered = gather(queries)
    table = plan(gates)
    sources = [in_hbm(a) for a in (keys, values, other_core(keys), other_core(values))]

    slots = []
    for d, half in enumerate(ship(table, sources)):
        got = hand_on(half, d)
        slots += [got, other_core(got)]

    partial = attention(table, gathered, sources, 0, EARLY)
    partial = attention(table, gathered, sources, EARLY, ALL, [partial])
    return finish(attention(table, gathered, slots, ALL, None, [partial]))


def solution(mesh):
    parts = jax.sharding.Mesh(mesh.devices.reshape(4, 4, 2, 4), ("x", "y", "core", "head"))
    seq = ("x", "y", "core")
    placed = (P((*seq, "head"), None), P(seq, "head"), P(seq, "head"), P())
    return jax.shard_map(
        shards, mesh=parts, in_specs=placed, out_specs=P(seq, "head"), check_vma=False
    )
```

```python
import functools

import jax
import jax.numpy as jnp
from jax import lax
from jax.experimental import pallas as pl
from jax.experimental.pallas import tpu as pltpu
from jax.sharding import PartitionSpec as P

HEAD = 128
BLOCK = 4096
GROUP = 8
WIDE = GROUP * HEAD
PACK = WIDE + 128
BOTH = 2 * WIDE + 128
CHUNK = 32
ROWS = 4 * CHUNK
SCALE = 128**-0.5 * 1.4426950408889634
NEG = -1e30
NT = (((1,), (1,)), ((), ()))
VMEM = 127 * 2**19
ROOM = 36 * 2**20
EARLY, ALL = 4, 64
HALF = BLOCK // 2
SPAN = 2048
TILE = 512
ARRIVAL = 4
DIRECTIONS = ((1, 0), (-1, 0), (0, 1), (0, -1))


def other_core(array):
    return lax.ppermute(array, "core", [(0, 1), (1, 0)])


def in_hbm(array):
    return pltpu.with_memory_space_constraint(array, pltpu.HBM)


def hand_on(array, direction):
    dx, dy = DIRECTIONS[direction]
    axis, step = ("x", dx) if dx else ("y", dy)
    return lax.ppermute(array, axis, [(i, (i + step) % 4) for i in range(4)])


def plan_kernel(gates, table):
    lane = lax.broadcasted_iota(jnp.int32, (8, 128), 1)
    item = lax.broadcasted_iota(jnp.int32, (8, 128), 0)
    variant = lane // 16
    chip = lane % 16
    x, y = chip // 4, chip % 4
    block = chip * 4 + item % 4
    here_x, here_y, core = (lax.axis_index(name) for name in ("x", "y", "core"))
    first = lax.axis_index("head") * 2
    kept = []
    for q in range(4):
        hit = jnp.zeros((8, 128), jnp.int32)
        for k in range(12):
            chosen = jnp.where(item < 4, gates[q, first, k], gates[q, first + 1, k])
            hit = jnp.where(chosen == block, 1, hit)
        kept.append(hit)

    def ahead(value, direction):
        forward = jnp.where(x < 3, pltpu.roll(value, 124, 1), pltpu.roll(value, 12, 1))
        back = jnp.where(x > 0, pltpu.roll(value, 4, 1), pltpu.roll(value, 116, 1))
        up = jnp.where(y < 3, pltpu.roll(value, 127, 1), pltpu.roll(value, 3, 1))
        down = jnp.where(y > 0, pltpu.roll(value, 1, 1), pltpu.roll(value, 125, 1))
        along_x = jnp.where(direction == 0, forward, back)
        return jnp.where(direction < 2, along_x, jnp.where(direction == 2, up, down))

    def over_items(value, how):
        for step in (4, 2, 1):
            value = how(value, pltpu.roll(value, step, 0))
        return value

    own = over_items(kept[0] + kept[1] + kept[2] + kept[3], jnp.add)
    handed = jnp.zeros((8, 128), jnp.int32)
    given = [jnp.zeros((8, 128), jnp.int32)] * 4
    got = [jnp.zeros((8, 128), jnp.int32)] * 4
    for orders in zip((0, 1, 2, 3), (2, 3, 0, 1), (0, 2, 1, 3), (3, 1, 2, 0)):
        direction = jnp.zeros((8, 128), jnp.int32)
        for i, d in enumerate(orders):
            direction = jnp.where(variant // 2 == i, d, direction)
        ready = jnp.maximum(own, ARRIVAL) + handed
        done = jnp.where(handed > 0, ready, own)
        want = jnp.maximum(done - ahead(ready, direction) + variant % 2, 0) >> 1
        left = kept[0] + kept[1] + kept[2] + kept[3]
        moved = jnp.minimum(left, want)
        score = moved * 256 - left * 16 + item
        chosen = jnp.logical_and(score == over_items(score, jnp.maximum), moved > 0)
        moved = jnp.where(chosen, moved, 0)
        entry = jnp.where(chosen, item * 16, 0)
        taken = jnp.zeros((8, 128), jnp.int32)
        for q in range(4):
            goes = jnp.where(taken < moved, kept[q], 0)
            taken = taken + goes
            kept[q] = kept[q] - goes
            entry = entry + goes * (1 << q)
        moved = over_items(moved, jnp.add)
        entry = over_items(entry, jnp.add)
        gets = ahead(entry, direction ^ 1)
        for d in range(4):
            given[d] = jnp.where(direction == d, entry, given[d])
            got[d] = jnp.where(direction == d, gets, got[d])
        own = own - moved
        handed = handed + ahead(moved, direction ^ 1)
    worst = jnp.where(handed > 0, jnp.maximum(own, ARRIVAL) + handed, own)
    for step in (8, 4, 2, 1):
        around = jnp.where(chip + step < 16, pltpu.roll(worst, 128 - step, 1), pltpu.roll(worst, 16 - step, 1))
        worst = jnp.maximum(worst, around)
    best = jnp.min((worst * 8 + variant).astype(jnp.float32)).astype(jnp.int32) % 8
    here = best * 16 + here_x * 4 + here_y
    keeps = jnp.zeros((8, 128), jnp.int32)
    for q in range(4):
        keeps = keeps + (kept[q] << (8 * q + item))
    row = jnp.zeros((8, 128), jnp.int32)
    values = enumerate([over_items(keeps, jnp.add)] + given + got)
    for i, value in [*values, (12, own)]:
        row = jnp.where(lane == i, pltpu.roll(value, (i + 128 - here) % 128, 1), row)
    for i, value in enumerate((here_x, here_y, core)):
        row = jnp.where(lane == 9 + i, value, row)
    table[...] = row


def plan(gates):
    return pl.pallas_call(
        plan_kernel,
        in_specs=[pl.BlockSpec(memory_space=pltpu.SMEM)],
        out_shape=jax.ShapeDtypeStruct((8, 128), jnp.int32),
        compiler_params=pltpu.CompilerParams(vmem_limit_bytes=VMEM),
        name="plan",
    )(gates)


def ship_kernel(table, keys, values, near_keys, near_values, *refs):
    outs, sems = refs[:4], refs[4]
    core = table[0, 11]
    for phase in range(2):
        for d in range(4):
            item = table[0, 1 + d] // 16
            block = item % 4
            rows = pl.ds(pl.multiple_of((block % 2) * BLOCK + core * HALF, HALF), HALF)
            cols = pl.ds(pl.multiple_of((item // 4) * HEAD, HEAD), HEAD)
            own = block // 2 == core
            for near, pair in ((False, (keys, values)), (True, (near_keys, near_values))):

                @pl.when(own != near)
                def _():
                    for part in range(2):
                        copy = pltpu.make_async_copy(
                            pair[part].at[rows, cols], outs[d].at[part], sems.at[d, part]
                        )
                        if phase == 0:
                            copy.start()
                        else:
                            copy.wait()


def ship(table, sources):
    hbm = pl.BlockSpec(memory_space=pl.ANY)
    return pl.pallas_call(
        ship_kernel,
        in_specs=[pl.BlockSpec(memory_space=pltpu.SMEM)] + [hbm] * 4,
        out_specs=[pl.BlockSpec(memory_space=pltpu.VMEM)] * 4,
        out_shape=[jax.ShapeDtypeStruct((2, HALF, HEAD), jnp.bfloat16)] * 4,
        scratch_shapes=[pltpu.SemaphoreType.DMA((4, 2))],
        cost_estimate=pl.CostEstimate(flops=0, bytes_accessed=2**10, transcendentals=0),
        compiler_params=pltpu.CompilerParams(vmem_limit_bytes=VMEM // 2),
        name="ship",
    )(table, *sources)


def attention_kernel(table, queries, *refs, first, limit):
    final = limit is None
    sources, refs = refs[: 8 if final else 4], refs[8 if final else 4 :]
    if first:
        before, refs = refs[0], refs[1:]
    out, stacked, peak, total, key_buffer, value_buffer, units, starts, touched, sems = refs
    x, y, core = table[0, 9], table[0, 10], table[0, 11]
    spared = (table[0, 12] == EARLY).astype(jnp.int32)
    begin = first - spared if first else 0
    end = limit - spared if limit == EARLY else limit
    lane = lax.broadcasted_iota(jnp.int32, (ROWS, 128), 1)

    def copies(unit, slot):
        code = (units[unit] // 2) % 8
        head = units[unit] // 16
        result = []
        rows = pl.ds(pl.multiple_of((code % 2) * BLOCK, BLOCK), BLOCK)
        cols = pl.ds(pl.multiple_of(head * HEAD, HEAD), HEAD)
        for near in range(0 if final else 2):
            keys, values = sources[2 * near], sources[2 * near + 1]
            group = [
                pltpu.make_async_copy(keys.at[rows, cols], key_buffer.at[slot], sems.at[0, slot]),
                pltpu.make_async_copy(values.at[rows, cols], value_buffer.at[slot], sems.at[1, slot]),
            ]
            result.append((code // 2 == near, group))
        for d in range(4 if final else 0):
            group = []
            for part, buffer in ((0, key_buffer), (1, value_buffer)):
                for half, source in ((core, sources[2 * d]), (1 - core, sources[2 * d + 1])):
                    rows = pl.ds(pl.multiple_of(half * HALF, HALF), HALF)
                    sem = sems.at[len(group), slot]
                    group.append(pltpu.make_async_copy(source.at[part], buffer.at[slot, rows], sem))
            result.append((code == 4 + d, group))
        return result

    def start(unit, slot):
        for inside, group in copies(unit, slot):

            @pl.when(inside)
            def _():
                for copy in group:
                    copy.start()

    def wait(unit, slot):
        for inside, group in copies(unit, slot):

            @pl.when(inside)
            def _():
                for copy in group:
                    copy.wait()

    def list_units(t, carry):
        count, seen = carry
        starts[t] = count
        head, q = t // 4, t % 4
        seen_before = seen
        for code in range(4, 8) if final else range(4):
            if not final:
                own = (core if code < 2 else 1 - core) * 2 + code % 2
                wanted = (table[0, 0] >> (8 * q + 4 * head + own)) & 1
                block = (x * 4 + y) * 4 + own
                ours = jnp.logical_and(seen >= begin, seen < end)
                seen = seen + wanted
                wanted = jnp.where(ours, wanted, 0)
            else:
                dx, dy = DIRECTIONS[code - 4]
                giver = ((x - dx + 4) % 4) * 4 + (y - dy + 4) % 4
                entry = table[0, 1 + code]
                item = entry // 16
                wanted = jnp.where(item // 4 == head, (entry >> q) & 1, 0)
                block = giver * 4 + item % 4
            at = count

            @pl.when(wanted != 0)
            def _():
                units[at] = 16 * head + 2 * code + (block == 63).astype(jnp.int32)

            count = count + wanted
        if final:
            touched[t] = (table[0, 0] >> (8 * q + 4 * head)) & 15
        else:
            touched[t] = (jnp.minimum(seen, begin) > seen_before).astype(jnp.int32)
        return count, seen

    starts[8] = lax.fori_loop(0, 8, list_units, (0, 0))[0]

    @pl.when(starts[8] > 0)
    def _():
        start(0, 0)

    def columns(task, h):
        return pl.ds(pl.multiple_of((task // 4) * WIDE + h * HEAD, HEAD), HEAD)

    def load(task):
        tokens = pl.ds(pl.multiple_of((task % 4) * ROWS, ROWS), ROWS)
        for h in range(GROUP):
            stacked[h * ROWS : (h + 1) * ROWS, :] = queries[tokens, columns(task, h)]

        @pl.when(touched[task] == 0)
        def _():
            peak[...] = jnp.full(peak.shape, NEG, jnp.float32)
            total[...] = jnp.zeros(total.shape, jnp.float32)

        if first:

            @pl.when(touched[task] != 0)
            def _():
                total[:, HEAD:] = jnp.ones((GROUP * ROWS, HEAD), jnp.float32)
                for h in range(GROUP):
                    rows = slice(h * ROWS, (h + 1) * ROWS)
                    level = before[task, :, WIDE + 4 * h : WIDE + 4 * h + 1]
                    peak[rows, :] = jnp.broadcast_to(level, (ROWS, HEAD))
                    total[rows, :HEAD] = before[task, :, h * HEAD : (h + 1) * HEAD]

    def attend(task, slot, masked):
        steps = [(k, r) for k in range(0, BLOCK, SPAN) for r in range(0, GROUP * ROWS, TILE)]

        def score(k, r):
            keys = key_buffer[slot, k : k + SPAN, :]
            return lax.dot_general(
                stacked[r : r + TILE, :], keys, NT, preferred_element_type=jnp.float32
            )

        s = score(*steps[0])
        for i, (k, r) in enumerate(steps):
            after = score(*steps[i + 1]) if i + 1 < len(steps) else None
            if masked and k + SPAN == BLOCK:
                row = lax.broadcasted_iota(jnp.int32, (TILE, 1024), 0) % ROWS
                token = (task % 4) * 256 + (row // CHUNK) * 64 + core * CHUNK + row % CHUNK
                col = lax.broadcasted_iota(jnp.int32, (TILE, 1024), 1)
                tail = jnp.where(col <= token, s[:, SPAN - 1024 :], NEG)
                s = jnp.concatenate([s[:, : SPAN - 1024], tail], axis=1)
            rows = slice(r, r + TILE)
            old = peak[rows, :]
            new = jnp.maximum(old, jnp.max(s, axis=1, keepdims=True) * SCALE)
            factor = jnp.exp2(old - new)
            weights = jnp.exp2(s * SCALE - new[:, :1]).astype(jnp.bfloat16)
            peak[rows, :] = new
            values = jnp.concatenate(
                [value_buffer[slot, k : k + SPAN, :], jnp.ones((SPAN, HEAD), jnp.bfloat16)], axis=1
            )
            total[rows, :] = total[rows, :] * jnp.concatenate([factor, factor], axis=1) + jnp.dot(
                weights, values, preferred_element_type=jnp.float32
            )
            s = after

    def visit(unit, task):
        slot = unit % 2
        wait(unit, slot)

        @pl.when(unit + 1 < starts[8])
        def _():
            start(unit + 1, 1 - slot)

        masked = units[unit] % 2

        @pl.when(masked != 0)
        def _():
            attend(task, slot, True)

        @pl.when(masked == 0)
        def _():
            attend(task, slot, False)

        return task

    def prepare():
        for h in range(GROUP):
            stacked[h * ROWS : (h + 1) * ROWS, :] = queries[:, h * HEAD : (h + 1) * HEAD]
        if handed:
            for h in range(GROUP):
                rows = slice(h * ROWS, (h + 1) * ROWS)
                level = before[0, :, WIDE + 4 * h : WIDE + 4 * h + 1]
                peak[rows, :] = jnp.broadcast_to(level, (ROWS, HEAD))
                total[rows, :HEAD] = before[0, :, h * HEAD : (h + 1) * HEAD]
                total[rows, HEAD:] = jnp.broadcast_to(
                    jnp.where(level > 0.5 * NEG, 1.0, 0.0), (ROWS, HEAD)
                )
        else:
            peak[...] = jnp.full(peak.shape, NEG, jnp.float32)
            total[...] = jnp.zeros(total.shape, jnp.float32)

    def write(task, h, value):
        if final:
            out[task % 4, :, columns(task, h)] = value.astype(jnp.bfloat16)
        else:
            out[task, :, h * HEAD : (h + 1) * HEAD] = value

    def write_levels(task, levels):
        if not final:
            out[task, :, WIDE:] = levels
            return
        q = task % 4
        packed = pack_stats(levels, lane)
        kept = out[q, :, 2 * WIDE :].astype(jnp.float32)
        kept = jnp.where(jnp.logical_and(task >= 4, lane < 32), kept, packed.astype(jnp.float32))
        out[q, :, 2 * WIDE :] = kept.astype(jnp.bfloat16)

    def one_task(task, carry):
        some = starts[task] < starts[task + 1]

        @pl.when(some)
        def _():
            load(task)
            lax.fori_loop(starts[task], starts[task + 1], visit, task)
            levels = jnp.full((ROWS, 128), NEG, jnp.float32)
            for h in range(GROUP):
                rows = slice(h * ROWS, (h + 1) * ROWS)
                mass = total[rows, HEAD:]
                write(task, h, total[rows, :HEAD] / mass)
                levels = jnp.where((lane % 32) // 4 == h, peak[rows, :] + jnp.log2(mass), levels)
            write_levels(task, levels)

        if first:

            @pl.when(jnp.logical_and(jnp.logical_not(some), touched[task] != 0))
            def _():
                for h in range(GROUP):
                    write(task, h, before[task, :, h * HEAD : (h + 1) * HEAD])
                write_levels(task, before[task, :, WIDE:])

        if final:

            @pl.when(jnp.logical_and(jnp.logical_not(some), touched[task] == 0))
            def _():
                for h in range(GROUP):
                    write(task, h, jnp.zeros((ROWS, HEAD), jnp.float32))
                write_levels(task, jnp.full((ROWS, 128), NEG, jnp.float32))

        return carry

    lax.fori_loop(0, 8, one_task, 0)


def pack_stats(level, lane):
    high = level.astype(jnp.bfloat16)
    rest = level - high.astype(jnp.float32)
    middle = rest.astype(jnp.bfloat16)
    low = (rest - middle.astype(jnp.float32)).astype(jnp.bfloat16)
    part = lane % 4
    terms = jnp.where(
        part == 0,
        high.astype(jnp.float32),
        jnp.where(part == 1, middle.astype(jnp.float32), low.astype(jnp.float32)),
    )
    return terms.astype(jnp.bfloat16)


def attention(table, queries, sources, first, limit, before=()):
    smem = pl.BlockSpec(memory_space=pltpu.SMEM)
    vmem = pl.BlockSpec(memory_space=pltpu.VMEM)
    hbm = pl.BlockSpec(memory_space=pl.ANY)
    if limit is None:
        shape = jax.ShapeDtypeStruct((4, ROWS, BOTH), jnp.bfloat16)
    else:
        shape = jax.ShapeDtypeStruct((8, ROWS, PACK), jnp.float32)
    return pl.pallas_call(
        functools.partial(attention_kernel, first=first, limit=limit),
        in_specs=[smem, vmem] + [hbm] * len(sources) + [vmem] * len(before),
        out_specs=vmem,
        out_shape=shape,
        scratch_shapes=[
            pltpu.VMEM((GROUP * ROWS, HEAD), jnp.bfloat16),
            pltpu.VMEM((GROUP * ROWS, HEAD), jnp.float32),
            pltpu.VMEM((GROUP * ROWS, 2 * HEAD), jnp.float32),
            pltpu.VMEM((2, BLOCK, HEAD), jnp.bfloat16),
            pltpu.VMEM((2, BLOCK, HEAD), jnp.bfloat16),
            pltpu.SMEM((65,), jnp.int32),
            pltpu.SMEM((9,), jnp.int32),
            pltpu.SMEM((8,), jnp.int32),
            pltpu.SemaphoreType.DMA((4, 2)),
        ],
        compiler_params=pltpu.CompilerParams(vmem_limit_bytes=ROOM),
        cost_estimate=pl.CostEstimate(flops=2 * 10**10, bytes_accessed=2**25, transcendentals=0),
        name="handed" if limit is None else "own",
    )(table, queries, *sources, *before)


def finish_kernel(parts, out):
    level = parts[:, :, 2 * WIDE :].astype(jnp.float32)
    level = level + pltpu.roll(level, 127, 2) + pltpu.roll(level, 126, 2)
    share = jnp.exp2(level - jnp.max(level, axis=0, keepdims=True))
    share = share / jnp.sum(share, axis=0, keepdims=True)
    for h in range(2 * GROUP):
        columns = slice(h * HEAD, (h + 1) * HEAD)
        joined = jnp.zeros((CHUNK, HEAD), jnp.float32)
        for i in range(16):
            part = parts[i, :, columns].astype(jnp.float32)
            joined = joined + share[i, :, 4 * h : 4 * h + 1] * part
        out[:, columns] = joined.astype(jnp.bfloat16)


def finish(partial):
    parts = lax.all_to_all(
        partial.reshape(16, CHUNK, BOTH), ("x", "y"), split_axis=0, concat_axis=0, tiled=True
    )
    return pl.pallas_call(
        finish_kernel,
        out_shape=jax.ShapeDtypeStruct((CHUNK, 2 * WIDE), jnp.bfloat16),
        compiler_params=pltpu.CompilerParams(vmem_limit_bytes=VMEM),
        name="finish",
    )(parts)


def gather(queries):
    columns = queries.reshape(8, 4, 2 * WIDE).transpose(1, 0, 2)
    sent = jnp.broadcast_to(columns[None], (16, 4, 8, 2 * WIDE)).reshape(64, 8, 2 * WIDE)
    got = lax.all_to_all(sent, ("x", "y", "head"), split_axis=0, concat_axis=0, tiled=True)
    return got.reshape(4 * ROWS, 2 * WIDE)


def shards(queries, keys, values, gates):
    gathered = gather(queries)
    table = plan(gates)
    sources = [in_hbm(a) for a in (keys, values, other_core(keys), other_core(values))]

    slots = []
    for d, half in enumerate(ship(table, sources)):
        got = hand_on(half, d)
        slots += [got, other_core(got)]

    partial = attention(table, gathered, sources, 0, EARLY)
    partial = attention(table, gathered, sources, EARLY, ALL, [partial])
    return finish(attention(table, gathered, slots, ALL, None, [partial]))


def solution(mesh):
    parts = jax.sharding.Mesh(mesh.devices.reshape(4, 4, 2, 4), ("x", "y", "core", "head"))
    seq = ("x", "y", "core")
    placed = (P((*seq, "head"), None), P(seq, "head"), P(seq, "head"), P())
    return jax.shard_map(
        shards, mesh=parts, in_specs=placed, out_specs=P(seq, "head"), check_vma=False
    )
```
